32 devices in a mesh: expert: 8 (over y, x, core), tensor: 4 (over z).
Axes of the slice: x: 2, y: 2, z: 4, core: 2. Of those that a mesh axis runs over, the one named last changes fastest.
Arguments:
- hidden_in: bfloat16 [8192, 2048], P(('expert', 'tensor')), may hold values from -6 to 6
- attn_gain: bfloat16 [2048], replicated, may hold values from 0.099609375 to 1.8984375
- query_gain: bfloat16 [128], replicated, may hold values from 0.099609375 to 1.8984375
- key_gain: bfloat16 [128], replicated, may hold values from 0.099609375 to 1.8984375
- w_qkv: bfloat16 [2048, 5120], P(None, 'tensor'), may hold values from -0.125 to 0.125
- w_out: bfloat16 [4096, 2048], P('tensor'), may hold values from -2 to 2
- moe_gain: bfloat16 [2048], replicated, may hold values from 0.099609375 to 1.8984375
- w_router: bfloat16 [2048, 32], replicated, may hold values from -0.0625 to 0.0625
- w_gate: bfloat16 [32, 2048, 768], P('expert', None, 'tensor'), may hold values from -0.125 to 0.125
- w_up: bfloat16 [32, 2048, 768], P('expert', None, 'tensor'), may hold values from -0.125 to 0.125
- w_down: bfloat16 [32, 768, 2048], P('expert', 'tensor'), may hold values from -0.875 to 0.875
- routes: int32 [8192, 8], P('expert'), may hold values from 0 to 31, as said below
- pair_rank: int32 [8, 8192], P('expert'), may hold values from 0 to 8191, as said below
- out_grad: bfloat16 [8192, 2048], P(('expert', 'tensor')), may hold values from -6 to 6
Outputs:
- layer_out: bfloat16 [8192, 2048], P(('expert', 'tensor'))
- grad_in: float32 [8192, 2048], P(('expert', 'tensor'))
- grad_attn_gain: float32 [2048], replicated
- grad_query_gain: float32 [128], replicated
- grad_key_gain: float32 [128], replicated
- grad_qkv: float32 [2048, 5120], P('expert', 'tensor')
- grad_out: float32 [4096, 2048], P('tensor', 'expert')
- grad_moe_gain: float32 [2048], replicated
- grad_router: float32 [2048, 32], replicated
- grad_gate: float32 [32, 2048, 768], P('expert', None, 'tensor')
- grad_up: float32 [32, 2048, 768], P('expert', None, 'tensor')
- grad_down: float32 [32, 768, 2048], P('expert', 'tensor')
The draws below stay inside these ranges and needn't reach their ends.
Inputs may be any that keep to these rules, and one draw needn't show every extreme that they name: `routes`: each row names 8 different experts, and every expert is named by some row. `pair_rank`: each row is a permutation; entry i * 8 + k is the priority of route k of the row's token i.
All inputs are finite; a program needn't handle non-finite values.
Results may differ from the reference program's by a relative error of at most 0.029.
Values may be sent and summed in bfloat16 or wider, within the bound.
No kernel may reach another device: no remote copies, remote signals or barrier semaphores. Data moves between devices by JAX's collectives and lax.ppermute only.
A program may use at most 512 MiB of HBM per device.

```python
import jax
import jax.numpy as jnp
from jax import lax

D = 2048
HQ = 32
HK = 4
HD = 128
FF = 768
TOPK = 8
SEQ = 1024
ATT_BLOCK = 256
EXPERTS = 32
GROUP_TOK = 1024
GROUPS = 8
TOKENS = 8192
CAP = 288
N_TENSOR = 4


def draw_routes(key, part):
    key_noise = jax.random.fold_in(key, 11)
    key_pop = jax.random.fold_in(key, 12)
    key_perm = jax.random.fold_in(key, 13)
    noise = jax.random.randint(key_noise, (TOKENS, EXPERTS), 0, 4096, dtype=jnp.int32)
    popular = jax.random.randint(key_pop, (EXPERTS,), 0, 2048, dtype=jnp.int32)
    shuffled = jax.random.permutation(key_perm, EXPERTS).astype(jnp.int32)
    rows = jnp.arange(TOKENS, dtype=jnp.int32)[:, None]
    columns = jnp.arange(EXPERTS, dtype=jnp.int32)[None, :]
    forced = ((rows < EXPERTS // TOPK) & (shuffled[None, :] // TOPK == rows)).astype(jnp.int32)
    score = (noise + popular[None, :] + forced * 100000) * EXPERTS + columns
    picked = lax.top_k(score, TOPK)[1]
    return picked.astype(jnp.int32)


def draw_pair_rank(key, part):
    base = jax.random.fold_in(key, 21)
    keys = jax.random.split(base, GROUPS)
    ranks = jax.vmap(lambda one_key: jax.random.permutation(one_key, GROUP_TOK * TOPK))(keys)
    return ranks.astype(jnp.int32)


def raised(entries, key, source, target, parts, factor):
    def block_of(position):
        return (jnp.arange(entries.shape[position]) // (entries.shape[position] // parts)).reshape((-1,) + (1,) * (entries.ndim - 1 - position))

    one_side = jax.random.permutation(key, parts)[block_of(target)]
    second = (block_of(target) + parts // 2) % parts
    return jnp.where((block_of(source) == one_side) | (block_of(source) == second), factor * entries, entries)


def level_of(rng, shape, shards, smallest, largest):
    level = 1.0
    for axis_at, blocks in shards:
        steps = jax.random.uniform(jax.random.fold_in(jax.random.fold_in(rng, 6), axis_at), (blocks,), jnp.float32, smallest / len(shards), largest / len(shards))
        level = level * jnp.repeat(jnp.exp(steps), shape[axis_at] // blocks).reshape((-1,) + (1,) * (len(shape) - 1 - axis_at))
    return level


def gaussian(key, dims, deviation, most, cuts=(), held_as=jnp.bfloat16):
    values = deviation * jax.random.normal(key, dims, jnp.float32)
    if cuts:
        values = values * level_of(key, dims, cuts, -0.22, 0.18)
    return jnp.clip(values, -most, most).astype(held_as)


def bell_draw_with(key, shape, deviation, limit, pieces, heavy, kind=jnp.bfloat16):
    values = deviation * jax.random.normal(key, shape, jnp.float32)
    if pieces:
        values = values * level_of(key, shape, pieces, -0.22, 0.18)
    return jnp.clip(raised(values, jax.random.fold_in(key, 3), *heavy), -limit, limit).astype(kind)


def setup_inputs(seed: int = 0) -> dict:
    arg_keys = jax.random.split(jax.random.key(seed), 15)
    return {
        "hidden_in": bell_draw_with(arg_keys[0], (TOKENS, D), 1.0, 6.0, ((0, 32),), (0, 1, 32, 2.75)),
        "attn_gain": jnp.clip(1.0 + 0.18 * jax.random.normal(arg_keys[1], (D,), jnp.float32), 0.099609375, 1.8984375).astype(jnp.bfloat16),
        "query_gain": jnp.clip(1.0 + 0.18 * jax.random.normal(arg_keys[2], (HD,), jnp.float32), 0.099609375, 1.8984375).astype(jnp.bfloat16),
        "key_gain": jnp.clip(1.0 + 0.18 * jax.random.normal(arg_keys[3], (HD,), jnp.float32), 0.099609375, 1.8984375).astype(jnp.bfloat16),
        "w_qkv": gaussian(arg_keys[4], (D, (HQ + 2 * HK) * HD), D ** -0.5, 0.125, ((1, 4),)),
        "w_out": gaussian(arg_keys[5], (HQ * HD, D), (max(HQ * HD // 512, 1)) ** -0.5, 2.0, ((0, 4),)),
        "moe_gain": jnp.clip(1.0 + 0.18 * jax.random.normal(arg_keys[6], (D,), jnp.float32), 0.099609375, 1.8984375).astype(jnp.bfloat16),
        "w_router": gaussian(arg_keys[7], (D, EXPERTS), (4 * D) ** -0.5, 0.0625),
        "w_gate": gaussian(arg_keys[8], (EXPERTS, D, FF), D ** -0.5, 0.125, ((0, 8), (2, 4))),
        "w_up": gaussian(arg_keys[9], (EXPERTS, D, FF), D ** -0.5, 0.125, ((0, 8), (2, 4))),
        "w_down": gaussian(arg_keys[10], (EXPERTS, FF, D), (FF // 16) ** -0.5, 0.875, ((0, 8), (1, 4))),
        "routes": draw_routes(jax.random.fold_in(arg_keys[14], 71), 0),
        "pair_rank": draw_pair_rank(jax.random.fold_in(arg_keys[14], 71), 0),
        "out_grad": gaussian(arg_keys[13], (TOKENS, D), 1.0, 6.0, ((0, 32),)),
    }


norm_eps = 1e-06
rope_base = 1000000.0
highest = lax.Precision.HIGHEST

@jax.custom_vjp
def low(v):
    return lax.optimization_barrier(v.astype(jnp.bfloat16)).astype(jnp.float32)

@jax.custom_vjp
def low_back(v):
    return v

def low_keep(v):
    return (low(v), None)

def low_pass(kept, grad):
    return (grad,)

def back_keep(v):
    return (v, None)

def back_low(kept, grad):
    return (low(grad),)
low.defvjp(low_keep, low_pass)
low_back.defvjp(back_keep, back_low)

def row_norm(values, gain):
    return values * lax.rsqrt(lax.optimization_barrier(jnp.mean(values * values, axis=-1, keepdims=True)) + norm_eps) * gain

def rotate(values, positions):
    middle_at = values.shape[-1] // 2
    fraction = jnp.arange(middle_at).astype(jnp.float32) * (2.0 / values.shape[-1])
    freqs = jnp.power(rope_base, -fraction)
    angles = positions[:, None] * freqs[None, :]
    cosine = jnp.concatenate([jnp.cos(angles), jnp.cos(angles)], axis=-1)[:, None, :]
    sine = jnp.concatenate([jnp.sin(angles), jnp.sin(angles)], axis=-1)[:, None, :]
    turned = jnp.concatenate([-values[..., middle_at:], values[..., :middle_at]], axis=-1)
    return values * cosine + turned * sine

def pair_slots(route_rows, rank_row, n_experts, capacity):
    pairs = route_rows.shape[0] * route_rows.shape[1]
    experts_flat = route_rows.reshape(pairs).astype(jnp.int32)
    order = jnp.zeros((pairs,), jnp.int32).at[rank_row.astype(jnp.int32)].set(jnp.arange(pairs, dtype=jnp.int32))
    ranked = experts_flat[order]
    onehot = (ranked[:, None] == jnp.arange(n_experts, dtype=jnp.int32)[None, :]).astype(jnp.int32)
    filled = lax.optimization_barrier(jnp.sum(jnp.cumsum(onehot, axis=0) * onehot, axis=1)) - 1
    slots = jnp.zeros((pairs,), jnp.int32).at[order].set(filled.astype(jnp.int32))
    return (experts_flat, slots, slots < capacity)

def attend_sequence(normed, w_qkv, query_gain, key_gain, w_out):
    length = normed.shape[0]
    local_q = HQ // N_TENSOR
    local_kv = HK // N_TENSOR
    projected = low_back(jnp.dot(normed, w_qkv, precision=highest))
    projected = projected.reshape(length, N_TENSOR, local_q + 2 * local_kv, HD)
    raw_query = projected[:, :, :local_q].reshape(length, HQ, HD)
    raw_key = projected[:, :, local_q:local_q + local_kv].reshape(length, HK, HD)
    values = low(projected[:, :, local_q + local_kv:].reshape(length, HK, HD))
    positions = jnp.arange(length).astype(jnp.float32)
    queries = low(rotate(row_norm(raw_query, query_gain), positions))
    keys_rot = low(rotate(row_norm(raw_key, key_gain), positions))
    grouped = queries.reshape(length, HK, HQ // HK, HD)
    scores = jnp.einsum('qkrd,skd->krqs', grouped, keys_rot, precision=highest) * HD ** (-0.5)
    scores = low_back(scores)
    blocks = jnp.arange(length) // ATT_BLOCK
    allowed = blocks[None, :] <= blocks[:, None]
    scores = jnp.where(allowed[None, None, :, :], scores, -jnp.inf)
    probs = low(jax.nn.softmax(scores, axis=-1))
    mixed = jnp.einsum('krqs,skd->qkrd', probs, values, precision=highest).reshape(length, HQ * HD)
    mixed = low_back(low(mixed))
    return jnp.dot(mixed, w_out, precision=highest)

def moe_group(moe_rows, gate_rows, route_rows, rank_row, w_gate, w_up, w_down):
    experts_flat, slots, keep = pair_slots(route_rows, rank_row, EXPERTS, CAP)
    pairs = GROUP_TOK * TOPK
    total = EXPERTS * CAP
    target = jnp.where(keep, experts_flat * CAP + slots, total)
    owners = jnp.arange(pairs, dtype=jnp.int32) // TOPK
    source = jnp.full((total,), GROUP_TOK, jnp.int32).at[target].set(owners, mode='drop')
    padded = jnp.concatenate([moe_rows, jnp.zeros((1, D), jnp.float32)], axis=0)
    dispatched = padded[source].reshape(EXPERTS, CAP, D)
    quarter = FF // N_TENSOR
    combined = jnp.zeros((EXPERTS, CAP, D), jnp.float32)
    for member in range(N_TENSOR):
        part_in = low_back(dispatched)
        gate_val = low_back(jnp.einsum('ecd,edf->ecf', part_in, w_gate[:, :, member * quarter:(member + 1) * quarter], precision=highest))
        up_val = low_back(jnp.einsum('ecd,edf->ecf', part_in, w_up[:, :, member * quarter:(member + 1) * quarter], precision=highest))
        hidden = low(jax.nn.silu(gate_val) * up_val)
        out_part = jnp.einsum('ecf,efd->ecd', hidden, w_down[:, member * quarter:(member + 1) * quarter, :], precision=highest)
        combined = combined + low_back(low(out_part))
    table = jnp.concatenate([combined.reshape(total, D), jnp.zeros((1, D), jnp.float32)], axis=0)
    picked = table[target].reshape(GROUP_TOK, TOPK, D)
    return lax.optimization_barrier(jnp.sum(picked * gate_rows[:, :, None], axis=1))

def reference(hidden_in, attn_gain, query_gain, key_gain, w_qkv, w_out, moe_gain, w_router, w_gate, w_up, w_down, routes, pair_rank, out_grad):

    def forward(inputs, gain_attn, gain_query, gain_key, weight_qkv, weight_out, gain_moe, weight_router, weight_gate, weight_up, weight_down):
        normed = low(row_norm(inputs, gain_attn))

        def one_sequence(seq_rows):
            return attend_sequence(seq_rows, weight_qkv, gain_query, gain_key, weight_out)
        attn = lax.map(jax.checkpoint(one_sequence), normed.reshape(TOKENS // SEQ, SEQ, D)).reshape(TOKENS, D)
        middle = inputs + low_back(attn)
        moe_in = low(row_norm(middle, gain_moe))
        logits = low_back(jnp.dot(moe_in, weight_router, precision=highest))
        chosen = jnp.take_along_axis(logits, routes.astype(jnp.int32), axis=1)
        gates = low(jax.nn.softmax(chosen, axis=-1))

        def one_group(packed):
            return moe_group(packed[0], packed[1], packed[2], packed[3], weight_gate, weight_up, weight_down)
        mixed = lax.map(jax.checkpoint(one_group), (moe_in.reshape(GROUPS, GROUP_TOK, D), gates.reshape(GROUPS, GROUP_TOK, TOPK), routes.reshape(GROUPS, GROUP_TOK, TOPK), pair_rank)).reshape(TOKENS, D)
        return middle + mixed
    floats = [array_in.astype(jnp.float32) for array_in in (hidden_in, attn_gain, query_gain, key_gain, w_qkv, w_out, moe_gain, w_router, w_gate, w_up, w_down)]
    result, pullback = jax.vjp(forward, *floats)
    grads = pullback(out_grad.astype(jnp.float32))
    return (result.astype(jnp.bfloat16), grads[0], grads[1], grads[2], grads[3], grads[4], grads[5], grads[6], grads[7], grads[8], grads[9], grads[10])
```

```python
import functools

import jax
import jax.numpy as jnp
from jax import lax
from jax.experimental import pallas as pl
from jax.experimental.pallas import tpu as pltpu
from jax.sharding import PartitionSpec as P

HD = 128
ATT_BLOCK = 256
norm_eps = 1e-06
rope_base = 1000000.0
bf16 = jnp.bfloat16
f32 = jnp.float32
MIB = 1 << 20


def dot(a, b, contract=((1,), (0,))):
    return lax.dot_general(a, b, (contract, ((), ())), preferred_element_type=f32)


NT = ((1,), (1,))
TN = ((0,), (0,))


def rope_tables(length):
    half = HD // 2
    freqs = jnp.power(rope_base, -(jnp.arange(half).astype(f32) * (2.0 / HD)))
    angles = jnp.arange(length).astype(f32)[:, None] * freqs[None, :]
    cosine, sine = jnp.cos(angles), jnp.sin(angles)
    return jnp.concatenate([cosine, cosine], axis=1), jnp.concatenate([-sine, sine], axis=1)


def project_kernel(local_q, local_kv, x_ref, w_ref, qg_ref, kg_ref, cos_ref, sin_ref, raw_ref, q_ref, k_ref, v_ref):
    raw = dot(x_ref[...], w_ref[...])
    cosine, sine = cos_ref[...], sin_ref[...]
    raw_ref[...] = raw[:, : (local_q + local_kv) * HD]
    for h in range(local_q + local_kv):
        head = raw[:, h * HD : (h + 1) * HD]
        gain = qg_ref[...] if h < local_q else kg_ref[...]
        normed = head * lax.rsqrt(jnp.mean(head * head, axis=1, keepdims=True) + norm_eps) * gain
        turned = (normed * cosine + pltpu.roll(normed, HD // 2, 1) * sine).astype(bf16)
        if h < local_q:
            q_ref[:, h * HD : (h + 1) * HD] = turned
        else:
            k_ref[:, (h - local_q) * HD : (h - local_q + 1) * HD] = turned
    v_ref[...] = raw[:, (local_q + local_kv) * HD :].astype(bf16)


def project(x, w, q_gain, k_gain, cosine, sine, local_q, local_kv):
    rows, width = x.shape
    tile = 256
    cols = w.shape[1]
    full = lambda shape: pl.BlockSpec(shape, lambda i: (0,) * len(shape))
    row = lambda n: pl.BlockSpec((tile, n), lambda i: (i, 0))
    heads = local_q + local_kv
    return pl.pallas_call(
        functools.partial(project_kernel, local_q, local_kv),
        grid=(rows // tile,),
        in_specs=[row(width), full((width, cols)), full((1, HD)), full((1, HD)), row(HD), row(HD)],
        out_specs=[row(heads * HD), row(local_q * HD), row(local_kv * HD), row(local_kv * HD)],
        out_shape=[
            jax.ShapeDtypeStruct((rows, heads * HD), f32),
            jax.ShapeDtypeStruct((rows, local_q * HD), bf16),
            jax.ShapeDtypeStruct((rows, local_kv * HD), bf16),
            jax.ShapeDtypeStruct((rows, local_kv * HD), bf16),
        ],
        compiler_params=pltpu.CompilerParams(vmem_limit_bytes=40 * MIB),
        cost_estimate=pl.CostEstimate(flops=2 * rows * width * cols, bytes_accessed=rows * width * 2 + width * cols * 2 + rows * cols * 6, transcendentals=0),
        name="project",
    )(x, w, q_gain, k_gain, cosine, sine)


def attend_kernel(scale, q_ref, k_ref, vt_ref, o_ref):
    for b in range(q_ref.shape[0] // ATT_BLOCK):
        n = (b + 1) * ATT_BLOCK
        at = slice(b * ATT_BLOCK, n)
        weight = jnp.exp(dot(k_ref[:n, :], q_ref[at, :], NT) * scale)
        total = jnp.sum(weight, axis=0, keepdims=True)
        mixed = dot(vt_ref[:, :n], weight.astype(bf16)) * (1.0 / total)
        o_ref[at, :] = mixed.T.astype(bf16)


def attend(q, k, v_t, local_q, local_kv):
    rows = q.shape[0]
    repeat = local_q // local_kv
    return pl.pallas_call(
        functools.partial(attend_kernel, HD**-0.5),
        grid=(local_q,),
        in_specs=[
            pl.BlockSpec((rows, HD), lambda h: (0, h)),
            pl.BlockSpec((rows, HD), lambda h: (0, h // repeat)),
            pl.BlockSpec((HD, rows), lambda h: (h // repeat, 0)),
        ],
        out_specs=pl.BlockSpec((rows, HD), lambda h: (0, h)),
        out_shape=jax.ShapeDtypeStruct((rows, local_q * HD), bf16),
        compiler_params=pltpu.CompilerParams(vmem_limit_bytes=32 * MIB),
        cost_estimate=pl.CostEstimate(flops=local_q * rows * rows * HD * 3, bytes_accessed=rows * local_q * HD * 4, transcendentals=local_q * rows * rows),
        name="attend",
    )(q, k, v_t)


def unturn(grad, raw, gain, cosine, sine):
    grad = grad * cosine - pltpu.roll(grad, HD // 2, 1) * sine
    inv = lax.rsqrt(jnp.mean(raw * raw, axis=1, keepdims=True) + norm_eps)
    part = gain * grad
    back = inv * part - raw * (inv * inv * inv) * jnp.mean(raw * part, axis=1, keepdims=True)
    return back, jnp.sum(grad * raw * inv, axis=0, keepdims=True)


def attend_back_kernel(
    scale, repeat, q_ref, do_ref, raw_ref, k_ref, kt_ref, v_ref, rawk_ref, qg_ref, kg_ref, cos_ref, sin_ref,
    dq_ref, dk_ref, dv_ref, dqg_ref, dkg_ref, dqs, dks, dvs,
):
    h = pl.program_id(0)

    @pl.when(h == 0)
    def _():
        dqg_ref[...] = jnp.zeros_like(dqg_ref)
        dkg_ref[...] = jnp.zeros_like(dkg_ref)

    @pl.when(lax.rem(h, repeat) == 0)
    def _():
        dks[...] = jnp.zeros_like(dks)
        dvs[...] = jnp.zeros_like(dvs)

    for b in range(q_ref.shape[0] // ATT_BLOCK):
        n = (b + 1) * ATT_BLOCK
        at = slice(b * ATT_BLOCK, n)
        query, given = q_ref[at, :], do_ref[at, :]
        weight = jnp.exp(dot(k_ref[:n, :], query, NT) * scale)
        prob = weight * (1.0 / jnp.sum(weight, axis=0, keepdims=True))
        prob_grad = dot(v_ref[:n, :], given, NT)
        inner = jnp.sum(prob * prob_grad, axis=0, keepdims=True)
        score_grad = (prob * (prob_grad - inner)).astype(bf16)
        dks[:n, :] += dot(score_grad, query)
        dvs[:n, :] += dot(prob.astype(bf16), given)
        dqs[at, :] = dot(kt_ref[:, :n], score_grad).T * scale
    back, gain_part = unturn(dqs[...], raw_ref[...], qg_ref[...], cos_ref[...], sin_ref[...])
    dq_ref[...] = back.astype(bf16)
    dqg_ref[...] += gain_part

    @pl.when(lax.rem(h, repeat) == repeat - 1)
    def _():
        back_k, gain_k = unturn(dks[...] * scale, rawk_ref[...], kg_ref[...], cos_ref[...], sin_ref[...])
        dk_ref[...] = back_k.astype(bf16)
        dv_ref[...] = dvs[...].astype(bf16)
        dkg_ref[...] += gain_k


def attend_back(q, given, raw, k, k_t, v, q_gain, k_gain, cosine, sine, local_q, local_kv):
    rows = q.shape[0]
    repeat = local_q // local_kv
    head = pl.BlockSpec((rows, HD), lambda h: (0, h))
    shared = pl.BlockSpec((rows, HD), lambda h: (0, h // repeat))
    whole = pl.BlockSpec((rows, HD), lambda h: (0, 0))
    gain = pl.BlockSpec((1, HD), lambda h: (0, 0))
    return pl.pallas_call(
        functools.partial(attend_back_kernel, HD**-0.5, repeat),
        grid=(local_q,),
        in_specs=[
            head, head, head, shared, pl.BlockSpec((HD, rows), lambda h: (h // repeat, 0)), shared,
            pl.BlockSpec((rows, HD), lambda h: (0, local_q + h // repeat)), gain, gain, whole, whole,
        ],
        out_specs=[head, shared, shared, gain, gain],
        out_shape=[
            jax.ShapeDtypeStruct((rows, local_q * HD), bf16),
            jax.ShapeDtypeStruct((rows, local_kv * HD), bf16),
            jax.ShapeDtypeStruct((rows, local_kv * HD), bf16),
            jax.ShapeDtypeStruct((1, HD), f32),
            jax.ShapeDtypeStruct((1, HD), f32),
        ],
        scratch_shapes=[pltpu.VMEM((rows, HD), f32)] * 3,
        compiler_params=pltpu.CompilerParams(vmem_limit_bytes=40 * MIB),
        cost_estimate=pl.CostEstimate(flops=local_q * rows * rows * HD * 7, bytes_accessed=rows * local_q * HD * 10, transcendentals=local_q * rows * rows),
        name="attend_back",
    )(q, given, raw, k, k_t, v, raw, q_gain, k_gain, cosine, sine)


def experts_kernel(
    table, x_ref, g_ref, gate_ref, spread_ref, wg_ref, wu_ref, wd_ref, hw_ref, gb_ref, ub_ref, score_ref, back_ref
):
    x = x_ref[...]
    gate_pre = dot(x, wg_ref[...])
    sigma = 1.0 / (1.0 + jnp.exp(-gate_pre))
    active = gate_pre * sigma
    up_pre = dot(x, wu_ref[...])
    pre = dot(g_ref[...], wd_ref[...], NT)
    hidden = active * up_pre
    score_ref[...] = dot(spread_ref[...], (hidden * pre).astype(bf16), NT)
    weight = dot(gate_ref[...], spread_ref[...])
    hw_ref[...] = (hidden * weight).astype(bf16)
    hidden_grad = pre * weight
    up_back = (hidden_grad * active).astype(bf16)
    gate_back = (hidden_grad * up_pre * sigma * (1.0 + gate_pre * (1.0 - sigma))).astype(bf16)
    gb_ref[...] = gate_back
    ub_ref[...] = up_back
    back_ref[...] = (dot(gate_back, wg_ref[...], NT) + dot(up_back, wu_ref[...], NT)).astype(bf16)


def experts(order, x, g, gates, spread, gate_w, up_w, down_w, tile):
    rows, width = x.shape
    hidden = gate_w.shape[1]
    lanes = spread.shape[0]
    at = lambda n: pl.BlockSpec((tile, n), lambda j, order: (order[j], 0))
    full = lambda shape: pl.BlockSpec(shape, lambda j, order: (0, 0), pipeline_mode=pl.Buffered(1))
    return pl.pallas_call(
        experts_kernel,
        grid_spec=pltpu.PrefetchScalarGridSpec(
            num_scalar_prefetch=1,
            grid=(rows // tile,),
            in_specs=[
                at(width), at(width), at(lanes), full((lanes, hidden)),
                full((width, hidden)), full((width, hidden)), full((hidden, width)),
            ],
            out_specs=[
                at(hidden), at(hidden), at(hidden),
                pl.BlockSpec((lanes, tile), lambda j, order: (0, order[j])),
                pl.BlockSpec((tile, width), lambda j, order: (j, 0)),
            ],
        ),
        out_shape=[
            jax.ShapeDtypeStruct((rows, hidden), bf16),
            jax.ShapeDtypeStruct((rows, hidden), bf16),
            jax.ShapeDtypeStruct((rows, hidden), bf16),
            jax.ShapeDtypeStruct((lanes, rows), f32),
            jax.ShapeDtypeStruct((rows, width), bf16),
        ],
        compiler_params=pltpu.CompilerParams(vmem_limit_bytes=58 * MIB),
        cost_estimate=pl.CostEstimate(flops=10 * rows * width * hidden, bytes_accessed=rows * width * 6 + rows * hidden * 6, transcendentals=rows * hidden),
        name="experts",
    )(order, x, g, gates, spread, gate_w, up_w, down_w)


TOPK = 8


def row_norm(values, gain):
    return values * lax.rsqrt(jnp.mean(values * values, axis=-1, keepdims=True) + norm_eps) * gain


def after(value, *others):
    return lax.optimization_barrier((value, *others))[0]


def hop(block, bit, axis):
    size = lax.axis_size(axis)
    return lax.ppermute(block, axis, [(i, i ^ bit) for i in range(size)])


def bits_of(size):
    return [1 << k for k in range(size.bit_length() - 1)]


def add_up(value):
    for axis in ("expert", "tensor"):
        for bit in bits_of(lax.axis_size(axis)):
            value = value + hop(value, bit, axis)
    return value


def to_members(parts):
    size, me = lax.axis_size("tensor"), lax.axis_index("tensor")
    found = [lax.dynamic_index_in_dim(parts, me, 0, keepdims=False)]
    for step in range(1, size):
        block = lax.dynamic_index_in_dim(parts, lax.rem(me + step, size), 0, keepdims=False)
        found.append(lax.ppermute(block, "tensor", [(i, (i + step) % size) for i in range(size)]))
    return found


def step_order(bits):
    order = [0]
    for bit in reversed(bits):
        order = [r | bit for r in order] + order
    return order


def scatter_sum(blocks, bits):
    for bit in bits:
        half = blocks.shape[0] // 2
        moved = hop(blocks[:half], bit, "expert")
        blocks = (blocks[half:].astype(f32) + moved.astype(f32)).astype(bf16)
    return blocks


def local(
    hidden_in,
    attn_gain,
    query_gain,
    key_gain,
    w_qkv,
    w_out,
    moe_gain,
    w_router,
    w_gate,
    w_up,
    w_down,
    routes,
    pair_rank,
    out_grad,
):
    tok_dev, width = hidden_in.shape
    n_tensor = lax.axis_size("tensor")
    n_expert = lax.axis_size("expert")
    member = lax.axis_index("tensor")
    place = lax.axis_index("expert")
    group = tok_dev * n_tensor
    local_experts = w_gate.shape[0]
    quarter = w_gate.shape[2]
    n_experts = local_experts * n_expert
    hidden_loc = local_experts * quarter
    capacity = 9 * group * TOPK // (8 * n_experts)
    local_q = w_out.shape[0] // HD
    local_kv = (w_qkv.shape[1] // HD - local_q) // 2
    both = ("expert", "tensor")
    bits = bits_of(n_expert)
    chunks = 2 * max(n_expert // 8, 1)
    piece = tok_dev // chunks
    rows = n_tensor * piece
    total = n_expert * rows
    lanes = 8 * (-(-local_experts // 8))

    hidden_f = hidden_in.astype(f32)
    attn_normed, attn_pull = jax.vjp(row_norm, hidden_f, attn_gain.astype(f32))
    gathered = lax.all_gather(attn_normed.astype(bf16), "tensor", axis=0, tiled=True)
    given = after(out_grad, gathered)

    def spread_out(values, c):
        return lax.all_gather(values[c * piece : (c + 1) * piece], both, axis=0, tiled=True)

    cosine, sine = rope_tables(group)
    q_gain, k_gain = query_gain.astype(f32)[None, :], key_gain.astype(f32)[None, :]
    raw, queries, keys, values = project(gathered, w_qkv, q_gain, k_gain, cosine, sine, local_q, local_kv)
    mixed_all = attend(queries, keys, values.T, local_q, local_kv)
    attn = lax.psum_scatter(
        dot(mixed_all, w_out).astype(bf16), "tensor", scatter_dimension=0, tiled=True
    )
    middle = hidden_f + attn.astype(f32)
    moe_normed, moe_pull = jax.vjp(row_norm, middle, moe_gain.astype(f32))
    moe_in = moe_normed.astype(bf16)

    expert_ids = jnp.arange(n_experts, dtype=jnp.int32)
    hits = routes.T[None, :, :] == expert_ids[:, None, None]
    ranks = jnp.where(hits, pair_rank[0].reshape(group, TOPK).T[None, :, :] + 1, 0).sum(axis=1)
    ranks = jnp.where(ranks == 0, group * TOPK + 1, ranks)
    own_ranks = lax.dynamic_slice_in_dim(ranks, member * tok_dev, tok_dev, 1)
    before = (ranks[:, :, None] < own_ranks[:, None, :]).astype(f32).sum(axis=1)
    routed = own_ranks <= group * TOPK
    keep = routed & (before < capacity)

    logits = dot(w_router, moe_in, ((0,), (1,)))
    gates = jax.nn.softmax(jnp.where(routed, logits, -jnp.inf), axis=0)
    sent_gates = jnp.where(keep, gates, 0.0).astype(bf16).astype(f32)
    gates_in = lax.all_to_all(
        sent_gates.reshape(n_expert, local_experts, tok_dev), "expert", 0, 0, tiled=True
    )
    gates_in = jnp.stack(to_members(jnp.broadcast_to(gates_in[None], (n_tensor, *gates_in.shape))))
    gates_in = jnp.take(gates_in, lax.rem(member - jnp.arange(n_tensor) + n_tensor, n_tensor), axis=0)
    gates_in = gates_in.reshape(n_tensor, n_expert, local_experts, chunks, piece)
    gates_in = gates_in.transpose(3, 1, 0, 4, 2).reshape(chunks, total, local_experts)
    gates_in = jnp.pad(gates_in, ((0, 0), (0, 0), (0, lanes - local_experts))).astype(bf16)

    gate_w = w_gate.transpose(1, 0, 2).reshape(width, hidden_loc)
    up_w = w_up.transpose(1, 0, 2).reshape(width, hidden_loc)
    down_w = w_down.reshape(hidden_loc, width)
    spread = (jnp.arange(hidden_loc)[None, :] // quarter == jnp.arange(lanes)[:, None]).astype(bf16)

    def run_experts(c, x_c, g_c):
        way = [bits[0]] + (bits[1:] if c % 2 else bits[:0:-1])
        order = place ^ jnp.array(step_order(way), jnp.int32)
        hidden_wt, gate_back, up_back, score, back = experts(
            order, x_c, g_c, gates_in[c], spread, gate_w, up_w, down_w, rows
        )
        return way, order, hidden_wt, gate_back, up_back, score, back

    def out_of(hidden_wt, way, order):
        blocks = hidden_wt.reshape(n_expert, rows, hidden_loc)
        blocks = jnp.take(blocks, order, axis=0).reshape(total, hidden_loc)
        return scatter_sum(dot(blocks, down_w).astype(bf16), way)

    def weight_grads(x_c, g_c, hidden_wt, gate_back, up_back):
        return dot(hidden_wt, g_c, TN), dot(x_c, gate_back, TN), dot(x_c, up_back, TN)

    def own_rows(part):
        return lax.psum_scatter(part, "tensor", scatter_dimension=0, tiled=True)

    if chunks == 2:
        grad_all = [spread_out(given, c) for c in range(chunks)]
        moe_all = [spread_out(moe_in, c) for c in range(chunks)]
        done = [run_experts(c, moe_all[c], grad_all[c]) for c in range(chunks)]
        back_own = [own_rows(scatter_sum(d[6], d[0])) for d in done]
        scores = [d[5] for d in done]
        out_own = [own_rows(out_of(after(d[2], done[1][6]), d[0], d[1])) for d in done]
        grads = [
            weight_grads(moe_all[c], grad_all[c], *done[c][2:5]) for c in range(chunks)
        ]
        grads = [sum(parts) for parts in zip(*grads)]
    else:
        def one_chunk(sums, c):
            x_c = lax.all_gather(lax.dynamic_slice_in_dim(moe_in, c * piece, piece, 0), both, axis=0, tiled=True)
            g_c = lax.all_gather(lax.dynamic_slice_in_dim(given, c * piece, piece, 0), both, axis=0, tiled=True)
            way = bits
            order = place ^ jnp.array(step_order(way), jnp.int32)
            hidden_wt, gate_back, up_back, score, back = experts(
                order, x_c, g_c, lax.dynamic_index_in_dim(gates_in, c, 0, keepdims=False), spread, gate_w, up_w, down_w, rows
            )
            parts = weight_grads(x_c, g_c, hidden_wt, gate_back, up_back)
            sums = tuple(a + b for a, b in zip(sums, parts))
            return sums, (own_rows(scatter_sum(back, way)), score, own_rows(out_of(hidden_wt, way, order)))

        zeros = (
            jnp.zeros((hidden_loc, width), f32),
            jnp.zeros((width, hidden_loc), f32),
            jnp.zeros((width, hidden_loc), f32),
        )
        grads, (back_own, scores, out_own) = lax.scan(one_chunk, zeros, jnp.arange(chunks))
    grad_down = grads[0].reshape(local_experts, quarter, width)
    grad_gate, grad_up = (
        part.reshape(width, local_experts, quarter).transpose(1, 0, 2) for part in grads[1:]
    )
    moe_back = jnp.concatenate(list(back_own), axis=0).astype(f32)
    moe_out = jnp.concatenate(list(out_own), axis=0).astype(f32)

    scores = jnp.stack([s[:local_experts] for s in scores]).reshape(
        chunks, local_experts, n_expert, n_tensor, piece
    )
    scores = scores.transpose(2, 3, 1, 0, 4).reshape(n_expert, n_tensor, local_experts, tok_dev)
    scores = lax.all_to_all(scores, "expert", 0, 0, tiled=True)
    scores = sum(to_members(scores.transpose(1, 0, 2, 3)))
    scores = jnp.where(keep, scores.reshape(n_experts, tok_dev), 0.0)

    layer_out = (middle + moe_out).astype(bf16)
    inner_gate = jnp.sum(gates * scores, axis=0, keepdims=True)
    logit_grad = (gates * (scores - inner_gate)).astype(bf16)
    router_grad = dot(logit_grad, moe_in)
    moe_in_grad = moe_back + dot(logit_grad, w_router, ((0,), (1,)))
    middle_part, moe_gain_grad = moe_pull(moe_in_grad)
    middle_grad = out_grad.astype(f32) + middle_part

    middle_all = lax.all_gather(middle_grad.astype(bf16), "tensor", axis=0, tiled=True)
    mixed_grad = dot(middle_all, w_out, NT).astype(bf16)
    dq, dk, dv, query_gain_grad, key_gain_grad = attend_back(
        queries, mixed_grad, raw, keys, keys.T, values, q_gain, k_gain, cosine, sine, local_q, local_kv
    )
    out_weight_grad = dot(mixed_all, middle_all, TN).astype(bf16)
    grad_out = lax.psum_scatter(out_weight_grad, "expert", scatter_dimension=1, tiled=True).astype(f32)
    qkv_grad = jnp.concatenate([dq, dk, dv], axis=1)
    normed_part = dot(qkv_grad, w_qkv, NT)
    normed_grad = lax.psum_scatter(
        normed_part.astype(bf16), "tensor", scatter_dimension=0, tiled=True
    ).astype(f32)
    attn_gain_grad = jnp.sum(normed_part * gathered.astype(f32), axis=0) / attn_gain.astype(f32)
    qkv_weight_grad = dot(gathered, qkv_grad, TN).astype(bf16)
    order = place ^ jnp.array(step_order(bits), jnp.int32)
    blocks = jnp.take(qkv_weight_grad.reshape(n_expert, -1, w_qkv.shape[1]), order, axis=0)
    grad_qkv = scatter_sum(blocks.reshape(qkv_weight_grad.shape), bits).astype(f32)
    hidden_part, _ = attn_pull(normed_grad)
    input_grad = middle_grad + hidden_part
    small = jnp.concatenate(
        [attn_gain_grad[None, :], jnp.pad(query_gain_grad, ((0, 0), (0, width - HD))), jnp.pad(key_gain_grad, ((0, 0), (0, width - HD)))],
        axis=0,
    )
    small = add_up(small)
    router_sum = add_up(jnp.concatenate([router_grad, moe_gain_grad[None, :]], axis=0))
    return (
        layer_out,
        input_grad,
        small[0],
        small[1, :HD],
        small[2, :HD],
        grad_qkv,
        grad_out,
        router_sum[n_experts],
        router_sum[:n_experts].T,
        grad_gate,
        grad_up,
        grad_down,
    )


def solution(mesh):
    in_specs = (
        P(("expert", "tensor"), None),
        P(),
        P(),
        P(),
        P(None, "tensor"),
        P("tensor", None),
        P(),
        P(),
        P("expert", None, "tensor"),
        P("expert", None, "tensor"),
        P("expert", "tensor", None),
        P("expert", None),
        P("expert", None),
        P(("expert", "tensor"), None),
    )
    out_specs = (
        P(("expert", "tensor"), None),
        P(("expert", "tensor"), None),
        P(),
        P(),
        P(),
        P("expert", "tensor"),
        P("tensor", "expert"),
        P(),
        P(),
        P("expert", None, "tensor"),
        P("expert", None, "tensor"),
        P("expert", "tensor", None),
    )
    return jax.shard_map(local, mesh=mesh, in_specs=in_specs, out_specs=out_specs, check_vma=False)
```

```python
import functools
import itertools
import jax
import jax.numpy as jnp
from jax import lax
from jax.experimental import pallas as pl
from jax.experimental.pallas import tpu as pltpu
from jax.sharding import PartitionSpec as P

HD = 128
ATT_BLOCK = 256
norm_eps = 1e-06
rope_base = 1000000.0
bf16 = jnp.bfloat16
f32 = jnp.float32
MIB = 1 << 20


def dot(a, b, contract=((1,), (0,))):
    return lax.dot_general(a, b, (contract, ((), ())), preferred_element_type=f32)


NT = ((1,), (1,))
TN = ((0,), (0,))


def rope_tables(length):
    half = HD // 2
    freqs = jnp.power(rope_base, -(jnp.arange(half).astype(f32) * (2.0 / HD)))
    angles = jnp.arange(length).astype(f32)[:, None] * freqs[None, :]
    cosine, sine = jnp.cos(angles), jnp.sin(angles)
    return jnp.concatenate([cosine, cosine], axis=1), jnp.concatenate([-sine, sine], axis=1)


def project_kernel(local_q, local_kv, x_ref, w_ref, qg_ref, kg_ref, cos_ref, sin_ref, raw_ref, q_ref, k_ref, v_ref):
    raw = dot(x_ref[...], w_ref[...])
    cosine, sine = cos_ref[...], sin_ref[...]
    raw_ref[...] = raw[:, : (local_q + local_kv) * HD]
    for h in range(local_q + local_kv):
        head = raw[:, h * HD : (h + 1) * HD]
        gain = qg_ref[...] if h < local_q else kg_ref[...]
        normed = head * lax.rsqrt(jnp.mean(head * head, axis=1, keepdims=True) + norm_eps) * gain
        turned = (normed * cosine + pltpu.roll(normed, HD // 2, 1) * sine).astype(bf16)
        if h < local_q:
            q_ref[:, h * HD : (h + 1) * HD] = turned
        else:
            k_ref[:, (h - local_q) * HD : (h - local_q + 1) * HD] = turned
    v_ref[...] = raw[:, (local_q + local_kv) * HD :].astype(bf16)


def project(x, w, q_gain, k_gain, cosine, sine, local_q, local_kv):
    rows, width = x.shape
    tile = 256
    cols = w.shape[1]
    full = lambda shape: pl.BlockSpec(shape, lambda i: (0,) * len(shape))
    row = lambda n: pl.BlockSpec((tile, n), lambda i: (i, 0))
    heads = local_q + local_kv
    return pl.pallas_call(
        functools.partial(project_kernel, local_q, local_kv),
        grid=(rows // tile,),
        in_specs=[row(width), full((width, cols)), full((1, HD)), full((1, HD)), row(HD), row(HD)],
        out_specs=[row(heads * HD), row(local_q * HD), row(local_kv * HD), row(local_kv * HD)],
        out_shape=[
            jax.ShapeDtypeStruct((rows, heads * HD), f32),
            jax.ShapeDtypeStruct((rows, local_q * HD), bf16),
            jax.ShapeDtypeStruct((rows, local_kv * HD), bf16),
            jax.ShapeDtypeStruct((rows, local_kv * HD), bf16),
        ],
        compiler_params=pltpu.CompilerParams(vmem_limit_bytes=40 * MIB),
        cost_estimate=pl.CostEstimate(flops=2 * rows * width * cols, bytes_accessed=rows * width * 2 + width * cols * 2 + rows * cols * 6, transcendentals=0),
        name="project",
    )(x, w, q_gain, k_gain, cosine, sine)


def attend_kernel(scale, q_ref, k_ref, vt_ref, o_ref):
    for b in range(q_ref.shape[0] // ATT_BLOCK):
        n = (b + 1) * ATT_BLOCK
        at = slice(b * ATT_BLOCK, n)
        weight = jnp.exp(dot(k_ref[:n, :], q_ref[at, :], NT) * scale)
        total = jnp.sum(weight, axis=0, keepdims=True)
        mixed = dot(vt_ref[:, :n], weight.astype(bf16)) * (1.0 / total)
        o_ref[at, :] = mixed.T.astype(bf16)


def attend(q, k, v_t, local_q, local_kv):
    rows = q.shape[0]
    repeat = local_q // local_kv
    return pl.pallas_call(
        functools.partial(attend_kernel, HD**-0.5),
        grid=(local_q,),
        in_specs=[
            pl.BlockSpec((rows, HD), lambda h: (0, h)),
            pl.BlockSpec((rows, HD), lambda h: (0, h // repeat)),
            pl.BlockSpec((HD, rows), lambda h: (h // repeat, 0)),
        ],
        out_specs=pl.BlockSpec((rows, HD), lambda h: (0, h)),
        out_shape=jax.ShapeDtypeStruct((rows, local_q * HD), bf16),
        compiler_params=pltpu.CompilerParams(vmem_limit_bytes=32 * MIB),
        cost_estimate=pl.CostEstimate(flops=local_q * rows * rows * HD * 3, bytes_accessed=rows * local_q * HD * 4, transcendentals=local_q * rows * rows),
        name="attend",
    )(q, k, v_t)


def unturn(grad, raw, gain, cosine, sine):
    grad = grad * cosine - pltpu.roll(grad, HD // 2, 1) * sine
    inv = lax.rsqrt(jnp.mean(raw * raw, axis=1, keepdims=True) + norm_eps)
    part = gain * grad
    back = inv * part - raw * (inv * inv * inv) * jnp.mean(raw * part, axis=1, keepdims=True)
    return back, jnp.sum(grad * raw * inv, axis=0, keepdims=True)


def attend_back_kernel(
    scale, repeat, q_ref, do_ref, raw_ref, k_ref, kt_ref, v_ref, rawk_ref, qg_ref, kg_ref, cos_ref, sin_ref,
    dq_ref, dk_ref, dv_ref, dqg_ref, dkg_ref, dqs, dks, dvs,
):
    h = pl.program_id(0)

    @pl.when(h == 0)
    def _():
        dqg_ref[...] = jnp.zeros_like(dqg_ref)
        dkg_ref[...] = jnp.zeros_like(dkg_ref)

    @pl.when(lax.rem(h, repeat) == 0)
    def _():
        dks[...] = jnp.zeros_like(dks)
        dvs[...] = jnp.zeros_like(dvs)

    for b in range(q_ref.shape[0] // ATT_BLOCK):
        n = (b + 1) * ATT_BLOCK
        at = slice(b * ATT_BLOCK, n)
        query, given = q_ref[at, :], do_ref[at, :]
        weight = jnp.exp(dot(k_ref[:n, :], query, NT) * scale)
        prob = weight * (1.0 / jnp.sum(weight, axis=0, keepdims=True))
        prob_grad = dot(v_ref[:n, :], given, NT)
        inner = jnp.sum(prob * prob_grad, axis=0, keepdims=True)
        score_grad = (prob * (prob_grad - inner)).astype(bf16)
        dks[:n, :] += dot(score_grad, query)
        dvs[:n, :] += dot(prob.astype(bf16), given)
        dqs[at, :] = dot(kt_ref[:, :n], score_grad).T * scale
    back, gain_part = unturn(dqs[...], raw_ref[...], qg_ref[...], cos_ref[...], sin_ref[...])
    dq_ref[...] = back.astype(bf16)
    dqg_ref[...] += gain_part

    @pl.when(lax.rem(h, repeat) == repeat - 1)
    def _():
        back_k, gain_k = unturn(dks[...] * scale, rawk_ref[...], kg_ref[...], cos_ref[...], sin_ref[...])
        dk_ref[...] = back_k.astype(bf16)
        dv_ref[...] = dvs[...].astype(bf16)
        dkg_ref[...] += gain_k


def attend_back(q, given, raw, k, k_t, v, q_gain, k_gain, cosine, sine, local_q, local_kv):
    rows = q.shape[0]
    repeat = local_q // local_kv
    head = pl.BlockSpec((rows, HD), lambda h: (0, h))
    shared = pl.BlockSpec((rows, HD), lambda h: (0, h // repeat))
    whole = pl.BlockSpec((rows, HD), lambda h: (0, 0))
    gain = pl.BlockSpec((1, HD), lambda h: (0, 0))
    return pl.pallas_call(
        functools.partial(attend_back_kernel, HD**-0.5, repeat),
        grid=(local_q,),
        in_specs=[
            head, head, head, shared, pl.BlockSpec((HD, rows), lambda h: (h // repeat, 0)), shared,
            pl.BlockSpec((rows, HD), lambda h: (0, local_q + h // repeat)), gain, gain, whole, whole,
        ],
        out_specs=[head, shared, shared, gain, gain],
        out_shape=[
            jax.ShapeDtypeStruct((rows, local_q * HD), bf16),
            jax.ShapeDtypeStruct((rows, local_kv * HD), bf16),
            jax.ShapeDtypeStruct((rows, local_kv * HD), bf16),
            jax.ShapeDtypeStruct((1, HD), f32),
            jax.ShapeDtypeStruct((1, HD), f32),
        ],
        scratch_shapes=[pltpu.VMEM((rows, HD), f32)] * 3,
        compiler_params=pltpu.CompilerParams(vmem_limit_bytes=40 * MIB),
        cost_estimate=pl.CostEstimate(flops=local_q * rows * rows * HD * 7, bytes_accessed=rows * local_q * HD * 10, transcendentals=local_q * rows * rows),
        name="attend_back",
    )(q, given, raw, k, k_t, v, raw, q_gain, k_gain, cosine, sine)


def experts_kernel(
    held, order, x_ref, pre_ref, gate_ref, spread_ref, wg_ref, wu_ref, *refs
):
    hw_ref, gb_ref, ub_ref, score_ref, back_ref = refs[held:]
    x = x_ref[...]
    gate_pre = dot(x, wg_ref[...])
    sigma = 1.0 / (1.0 + jnp.exp(-gate_pre))
    active = gate_pre * sigma
    up_pre = dot(x, wu_ref[...])
    pre = pre_ref[...].reshape(gate_pre.shape)
    hidden = active * up_pre
    score_ref[...] = dot(spread_ref[...], (hidden * pre).astype(bf16), NT)
    weight = dot(gate_ref[...], spread_ref[...])
    hw_ref[...] = (hidden * weight).astype(bf16).reshape(hw_ref.shape)
    hidden_grad = pre * weight
    up_back = (hidden_grad * active).astype(bf16)
    gate_back = (hidden_grad * up_pre * sigma * (1.0 + gate_pre * (1.0 - sigma))).astype(bf16)
    gb_ref[...] = gate_back
    ub_ref[...] = up_back
    back = (dot(gate_back, wg_ref[...], NT) + dot(up_back, wu_ref[...], NT)).astype(bf16)
    back_ref[...] = back


def row_block(array, c):
    _, members, _, piece, columns = array.shape
    return pl.BlockSpec((1, members, 1, piece, columns), lambda j, order: (order[j], 0, c, 0, 0))


def experts(order, c, x, pre, gates, spread, gate_w, up_w, held=()):
    rows, width = x.shape
    tile = rows // pre.shape[0]
    hidden = gate_w.shape[1]
    lanes = spread.shape[0]
    steps = order.shape[0]
    at = lambda n: pl.BlockSpec((tile, n), lambda j, order: (order[j], 0))
    full = lambda shape: pl.BlockSpec(shape, lambda j, order: (0, 0), pipeline_mode=pl.Buffered(1))
    return pl.pallas_call(
        functools.partial(experts_kernel, len(held)),
        grid_spec=pltpu.PrefetchScalarGridSpec(
            num_scalar_prefetch=1,
            grid=(steps,),
            in_specs=[
                at(width), row_block(pre, c), at(lanes), full((lanes, hidden)), full((width, hidden)), full((width, hidden)),
                *[pl.BlockSpec(memory_space=pl.ANY)] * len(held),
            ],
            out_specs=[
                row_block(pre, c), at(hidden), at(hidden), pl.BlockSpec((lanes, tile), lambda j, order: (0, order[j])),
                pl.BlockSpec((tile, width), lambda j, order: (j, 0)),
            ],
        ),
        out_shape=[
            jax.ShapeDtypeStruct(pre.shape, bf16),
            jax.ShapeDtypeStruct((rows, hidden), bf16),
            jax.ShapeDtypeStruct((rows, hidden), bf16),
            jax.ShapeDtypeStruct((lanes, rows), f32),
            jax.ShapeDtypeStruct((steps * tile, width), bf16),
        ],
        input_output_aliases={7 + i: output for i, (output, _) in enumerate(held)},
        compiler_params=pltpu.CompilerParams(vmem_limit_bytes=58 * MIB),
        cost_estimate=pl.CostEstimate(flops=8 * steps * tile * width * hidden, bytes_accessed=steps * tile * (width * 4 + hidden * 10), transcendentals=steps * tile * hidden),
        name="experts",
    )(order, x, pre, gates, spread, gate_w, up_w, *[array for _, array in held])


def outputs_kernel(half, order, h_ref, w_ref, far_ref, near_ref):
    hidden = h_ref[...].reshape(far_ref.shape[0], w_ref.shape[0])
    value = dot(hidden, w_ref[...]).astype(bf16)

    @pl.when(pl.program_id(0) < half)
    def _():
        far_ref[...] = value

    @pl.when(pl.program_id(0) >= half)
    def _():
        near_ref[...] = value


def outputs(order, c, hidden_wt, down_w):
    steps, members, _, piece, hidden = hidden_wt.shape
    tile = members * piece
    width = down_w.shape[1]
    half = steps // 2
    return pl.pallas_call(
        functools.partial(outputs_kernel, half),
        grid_spec=pltpu.PrefetchScalarGridSpec(
            num_scalar_prefetch=1,
            grid=(steps,),
            in_specs=[
                row_block(hidden_wt, c),
                pl.BlockSpec((hidden, width), lambda j, order: (0, 0), pipeline_mode=pl.Buffered(1)),
            ],
            out_specs=[
                pl.BlockSpec((tile, width), lambda j, order: (jnp.minimum(j, half - 1), 0)),
                pl.BlockSpec((tile, width), lambda j, order: (jnp.maximum(j - half, 0), 0)),
            ],
        ),
        out_shape=[jax.ShapeDtypeStruct((half * tile, width), bf16)] * 2,
        compiler_params=pltpu.CompilerParams(vmem_limit_bytes=32 * MIB),
        cost_estimate=pl.CostEstimate(flops=2 * steps * tile * width * hidden, bytes_accessed=steps * tile * (width + hidden) * 2, transcendentals=0),
        name="outputs",
    )(order, hidden_wt, down_w)


TOPK = 8


def row_norm(values, gain):
    return values * lax.rsqrt(jnp.mean(values * values, axis=-1, keepdims=True) + norm_eps) * gain


def after(value, *others):
    return lax.optimization_barrier((value, *others))[0]


def hop(block, bit, axis):
    size = lax.axis_size(axis)
    return lax.ppermute(block, axis, [(i, i ^ bit) for i in range(size)])


def bits_of(size):
    return [1 << k for k in range(size.bit_length() - 1)]


def add_up(value, axis):
    for bit in bits_of(lax.axis_size(axis)):
        value = value + hop(value, bit, axis)
    return value


def to_members(parts):
    size, me = lax.axis_size("tensor"), lax.axis_index("tensor")
    found = [lax.dynamic_index_in_dim(parts, me, 0, keepdims=False)]
    for step in range(1, size):
        block = lax.dynamic_index_in_dim(parts, lax.rem(me + step, size), 0, keepdims=False)
        found.append(lax.ppermute(block, "tensor", [(i, (i + step) % size) for i in range(size)]))
    return found


def step_order(bits):
    order = [0]
    for bit in reversed(bits):
        order = [r | bit for r in order] + order
    return order


class Exchange:
    def __init__(self, far, near, bits):
        self.moved = [hop(far, bits[0], "expert")]
        self.near, self.rest = near, bits[1:]
        self.left = [list(range(len(self.rest))) for _ in range(2)]
        self.sides = None

    def wait(self, behind):
        if self.sides is None:
            moved = after(self.moved, *behind) if behind else self.moved
            rows, width = self.near.shape[0] >> len(self.rest), self.near.shape[1]
            near, moved = self.near.reshape(-1, rows, width), moved[0].reshape(-1, rows, width)
            spots = itertools.product(range(2), repeat=len(self.rest))
            index = {spot: i for i, spot in enumerate(spots)}
            self.sides = []
            for part in (slice(0, rows // 2), slice(rows // 2, None)):
                self.sides.append({spot: [near[i, part], moved[i, part]] for spot, i in index.items()})
        else:
            for number, (side, got) in enumerate(zip(self.sides, self.got)):
                got = after(got, *behind) if behind else got
                self.sides[number] = {spot: [*parts, got[i]] for i, (spot, parts) in enumerate(side.items())}

    def send(self, *behind):
        self.wait(behind)
        sent, self.got = [], []
        add = lambda parts: sum(p.astype(f32) for p in parts).astype(bf16)
        for number, side in enumerate(self.sides):
            at = len(self.left[number]) - 1 if number else 0
            bit = self.rest[self.left[number].pop(at)]
            spots = sorted({spot[:at] + spot[at + 1 :] for spot in side})
            block = jnp.stack([add(side[spot[:at] + (0,) + spot[at:]]) for spot in spots])
            self.got.append(hop(block, bit, "expert"))
            sent.append(block)
            self.sides[number] = {spot: side[spot[:at] + (1,) + spot[at:]] for spot in spots}
        return sent

    def total(self, *behind):
        while any(self.left):
            self.send()
        self.wait(behind)
        parts = [sum(p.astype(f32) for p in side[()]).astype(bf16) for side in self.sides]
        return jnp.concatenate(parts, axis=0)


def neighbours():
    size = lax.axis_size("tensor")
    up = lambda v: lax.ppermute(v, "tensor", [(i, (i + 1) % size) for i in range(size)])
    down = lambda v: lax.ppermute(v, "tensor", [(i, (i - 1) % size) for i in range(size)])
    return up, down


def gather_line(block, behind=()):
    size, me = lax.axis_size("tensor"), lax.axis_index("tensor")
    if size != 4:
        return lax.all_gather(block, "tensor", axis=0, tiled=True)
    rows = block.shape[0]
    cut = rows // 2
    up, down = neighbours()
    low, high = up(block), down(block)
    if behind:
        low, high = after((low, high), *behind)
    far_low, far_high = up(low[:cut]), down(high[cut:])
    whole = jnp.zeros((rows * size, block.shape[1]), block.dtype)
    for part, member, shift in ((block, 0, 0), (low, 3, 0), (high, 1, 0), (far_low, 2, 0), (far_high, 2, cut)):
        at = lax.rem(me + member, size) * rows + shift
        whole = lax.dynamic_update_slice(whole, part, (at, 0))
    return whole


class Line:
    def __init__(self, part):
        self.size, self.me = lax.axis_size("tensor"), lax.axis_index("tensor")
        self.part, self.rows = part, part.shape[0] // self.size
        self.got = None

    def of(self, member, start, end):
        at = lax.rem(self.me + member, self.size) * self.rows
        return lax.dynamic_slice_in_dim(self.part, at + start, end - start, 0)

    def send(self, *behind):
        cut, rows = self.rows // 2, self.rows
        if self.size != 4:
            return []
        if behind:
            self.got = after(self.got, *behind)
        if self.got is None:
            low, high = self.of(2, cut, rows), self.of(2, 0, cut)
        else:
            from_low, from_high = (part.astype(f32) for part in self.got)
            low = jnp.concatenate([self.of(1, 0, cut), (self.of(1, cut, rows).astype(f32) + from_low).astype(bf16)])
            high = jnp.concatenate([(self.of(3, 0, cut).astype(f32) + from_high).astype(bf16), self.of(3, cut, rows)])
        up, down = neighbours()
        self.got = up(low), down(high)
        return [low, high]

    def total(self, *behind):
        if self.size != 4:
            return lax.psum_scatter(self.part, "tensor", scatter_dimension=0, tiled=True).astype(f32)
        low, high = after(self.got, *behind) if behind else self.got
        return self.of(0, 0, self.rows).astype(f32) + low.astype(f32) + high.astype(f32)


def local(
    hidden_in,
    attn_gain,
    query_gain,
    key_gain,
    w_qkv,
    w_out,
    moe_gain,
    w_router,
    w_gate,
    w_up,
    w_down,
    routes,
    pair_rank,
    out_grad,
):
    tok_dev, width = hidden_in.shape
    n_tensor = lax.axis_size("tensor")
    n_expert = lax.axis_size("expert")
    member = lax.axis_index("tensor")
    place = lax.axis_index("expert")
    group = tok_dev * n_tensor
    local_experts = w_gate.shape[0]
    quarter = w_gate.shape[2]
    n_experts = local_experts * n_expert
    hidden_loc = local_experts * quarter
    capacity = 9 * group * TOPK // (8 * n_experts)
    local_q = w_out.shape[0] // HD
    local_kv = (w_qkv.shape[1] // HD - local_q) // 2
    both = ("expert", "tensor")
    bits = bits_of(n_expert)
    chunks = 2 * max(n_expert // 8, 1)
    piece = tok_dev // chunks
    rows = n_tensor * piece
    total = n_expert * rows
    lanes = 8 * (-(-local_experts // 8))

    gate_w = w_gate.transpose(1, 0, 2).reshape(width, hidden_loc)
    up_w = w_up.transpose(1, 0, 2).reshape(width, hidden_loc)
    down_w = w_down.reshape(hidden_loc, width)
    spread = (jnp.arange(hidden_loc)[None, :] // quarter == jnp.arange(lanes)[:, None]).astype(bf16)

    hidden_f = hidden_in.astype(f32)
    attn_normed, attn_pull = jax.vjp(row_norm, hidden_f, attn_gain.astype(f32))
    gathered = gather_line(attn_normed.astype(bf16))
    given = after(out_grad, gathered)

    cosine, sine = rope_tables(group)
    q_gain, k_gain = query_gain.astype(f32)[None, :], key_gain.astype(f32)[None, :]
    by_chunk = (n_expert, n_tensor, 1, piece, hidden_loc)
    if chunks == 2:
        gathered = after(gathered, gate_w, up_w)
    raw, queries, keys, values = project(gathered, w_qkv, q_gain, k_gain, cosine, sine, local_q, local_kv)
    mixed_all = attend(queries, keys, values.T, local_q, local_kv)
    attn = mixed_all
    if chunks == 2:
        grad_line = [
            gather_line(given[:piece], (queries,)),
            gather_line(after(given[piece:], queries), (mixed_all,)),
        ]
        grad_all = [lax.all_gather(part, "expert", axis=0, tiled=True) for part in grad_line]
        pre = [dot(part, down_w, NT).reshape(by_chunk) for part in grad_all]
        attn = after(attn, *grad_line)
    attn = Line(dot(attn, w_out).astype(bf16))
    attn.send()
    attn.send()
    attn = attn.total()
    middle = hidden_f + attn
    moe_normed, moe_pull = jax.vjp(row_norm, middle, moe_gain.astype(f32))
    moe_in = moe_normed.astype(bf16)

    expert_ids = jnp.arange(n_experts, dtype=jnp.int32)
    hits = routes.T[None, :, :] == expert_ids[:, None, None]
    ranks = jnp.where(hits, pair_rank[0].reshape(group, TOPK).T[None, :, :] + 1, 0).sum(axis=1)
    ranks = jnp.where(ranks == 0, group * TOPK + 1, ranks)
    own_ranks = lax.dynamic_slice_in_dim(ranks, member * tok_dev, tok_dev, 1)
    before = (ranks[:, :, None] < own_ranks[:, None, :]).astype(f32).sum(axis=1)
    routed = own_ranks <= group * TOPK
    keep = routed & (before < capacity)

    logits = dot(w_router, moe_in, ((0,), (1,)))
    gates = jax.nn.softmax(jnp.where(routed, logits, -jnp.inf), axis=0)
    sent_gates = jnp.where(keep, gates, 0.0).astype(bf16).astype(f32)
    gates_in = lax.all_to_all(
        sent_gates.reshape(n_expert, local_experts, tok_dev), "expert", 0, 0, tiled=True
    )
    gates_in = jnp.stack(to_members(jnp.broadcast_to(gates_in[None], (n_tensor, *gates_in.shape))))
    gates_in = jnp.take(gates_in, lax.rem(member - jnp.arange(n_tensor) + n_tensor, n_tensor), axis=0)
    gates_in = gates_in.reshape(n_tensor, n_expert, local_experts, chunks, piece)
    gates_in = gates_in.transpose(3, 1, 0, 4, 2).reshape(chunks, total, local_experts)
    gates_in = jnp.pad(gates_in, ((0, 0), (0, 0), (0, lanes - local_experts))).astype(bf16)

    order = place ^ jnp.array(step_order(bits), jnp.int32)

    def own_rows(part):
        return lax.psum_scatter(part, "tensor", scatter_dimension=0, tiled=True)

    def to_tokens(scores):
        scores = jnp.stack([s[:local_experts] for s in scores])
        scores = scores.reshape(chunks, local_experts, n_expert, n_tensor, piece)
        scores = scores.transpose(2, 3, 1, 0, 4).reshape(n_expert, n_tensor, local_experts, tok_dev)
        scores = lax.all_to_all(scores, "expert", 0, 0, tiled=True)
        scores = sum(to_members(scores.transpose(1, 0, 2, 3)))
        return jnp.where(keep, scores.reshape(n_experts, tok_dev), 0.0)

    if chunks == 2:
        moe_line = [gather_line(moe_in[:piece], (pre[0],)), gather_line(moe_in[piece:])]
        moe_line[0] = after(moe_line[0], grad_all[1])
        moe_all = [lax.all_gather(part, "expert", axis=0, tiled=True) for part in moe_line]
        front, rear = order[: n_expert // 2], order[n_expert // 2 :]
        fixed = (spread, gate_w, up_w)
        x_0 = after(moe_all[0], pre[1])
        *kept_0, back_0 = experts(jnp.arange(n_expert, dtype=jnp.int32), 0, x_0, pre[0], gates_in[0], *fixed)
        back_0 = lax.psum_scatter(back_0, "expert", scatter_dimension=0, tiled=True)
        back_own = [own_rows(back_0)]
        outs = [outputs(order, 0, kept_0[0], down_w)]
        x_1 = after(moe_all[1], *outs[0])
        *kept_1, near = experts(rear, 0, x_1, pre[1], gates_in[1], *fixed)
        *kept_1, far = experts(front, 0, x_1, pre[1], gates_in[1], *fixed, list(enumerate(kept_1)))
        back_1 = Exchange(far, near, bits)
        outs.append(outputs(order, 0, kept_1[0], down_w))
        sent = back_1.send(*outs[1])
        scores = to_tokens(after([kept_0[3], kept_1[3]], *sent))
        x_0 = after(moe_all[0], *sent)
        gate_grad = dot(x_0, kept_0[1], TN)
        sent = back_1.send(gate_grad, scores, back_0)
        out_0, out_1 = (Exchange(*out, bits) for out in outs)
        sent = out_0.send(*sent)
        up_grad = dot(after(x_0, *sent), kept_0[2], TN)
        back_1 = back_1.total(up_grad, back_own[0])
        back_own.append(own_rows(back_1))
        x_1, g_0 = after((moe_all[1], grad_all[0]), back_1)
        gate_grad = gate_grad + dot(x_1, kept_1[1], TN)
        down_grad = dot(kept_0[0].reshape(-1, hidden_loc), g_0, TN)
        sent = out_0.send(gate_grad, down_grad)
        back_own = after(back_own, *sent)
    else:
        def one_chunk(sums, c):
            x_c = lax.all_gather(lax.dynamic_slice_in_dim(moe_in, c * piece, piece, 0), both, axis=0, tiled=True)
            g_c = lax.all_gather(lax.dynamic_slice_in_dim(given, c * piece, piece, 0), both, axis=0, tiled=True)
            gates_c = lax.dynamic_index_in_dim(gates_in, c, 0, keepdims=False)
            pre = dot(g_c, down_w, NT).reshape(n_expert, n_tensor, 1, piece, hidden_loc)
            given_c = (0, x_c, pre, gates_c, spread, gate_w, up_w)
            *kept, far = experts(order[: n_expert // 2], *given_c)
            *kept, near = experts(order[n_expert // 2 :], *given_c, list(enumerate(kept)))
            hw, gate_back, up_back, score = kept
            parts = (dot(hw.reshape(-1, hidden_loc), g_c, TN), dot(x_c, gate_back, TN), dot(x_c, up_back, TN))
            sums = tuple(a + b for a, b in zip(sums, parts))
            back = own_rows(Exchange(far, near, bits).total())
            out = own_rows(Exchange(*outputs(order, 0, hw, down_w), bits).total())
            return sums, (back, score, out)

        zeros = (
            jnp.zeros((hidden_loc, width), f32),
            jnp.zeros((width, hidden_loc), f32),
            jnp.zeros((width, hidden_loc), f32),
        )
        grads, (back_own, scores, out_own) = lax.scan(one_chunk, zeros, jnp.arange(chunks))
        scores = to_tokens(scores)
        moe_out = jnp.concatenate(list(out_own), axis=0)
    moe_back = jnp.concatenate(list(back_own), axis=0).astype(f32)

    inner_gate = jnp.sum(gates * scores, axis=0, keepdims=True)
    logit_grad = (gates * (scores - inner_gate)).astype(bf16)
    router_grad = dot(logit_grad, moe_in)
    moe_in_grad = moe_back + dot(logit_grad, w_router, ((0,), (1,)))
    middle_part, moe_gain_grad = moe_pull(moe_in_grad)
    middle_grad = out_grad.astype(f32) + middle_part

    middle_all = lax.all_gather(middle_grad.astype(bf16), "tensor", axis=0, tiled=True)
    if chunks == 2:
        sent = out_1.send(middle_grad)
        x_1, g_1 = after((moe_all[1], grad_all[1]), *sent)
        up_grad = up_grad + dot(x_1, kept_1[2], TN)
        out_0 = out_0.total(up_grad)
        down_grad = down_grad + dot(kept_1[0].reshape(-1, hidden_loc), after(g_1, out_0), TN)
        sent = out_1.send(down_grad)
        middle_all = after(middle_all, *sent)
    mixed_grad = dot(middle_all, w_out, NT).astype(bf16)
    out_weight_grad = dot(middle_all, mixed_all, TN).astype(bf16)
    mixed_grad, out_weight_grad = lax.optimization_barrier((mixed_grad, out_weight_grad))
    if chunks == 2:
        out_1 = out_1.total(out_weight_grad)
        mixed_grad = after(mixed_grad, out_1)
    grad_out = lax.psum_scatter(out_weight_grad, "expert", scatter_dimension=0, tiled=True)
    dq, dk, dv, query_gain_grad, key_gain_grad = attend_back(
        queries, mixed_grad, raw, keys, keys.T, values, q_gain, k_gain, cosine, sine, local_q, local_kv
    )
    qkv_grad = jnp.concatenate([dq, dk, dv], axis=1)
    if chunks == 2:
        out_own = [own_rows(part) for part in (out_0, out_1)]
        qkv_grad = after(qkv_grad, *out_own)
        moe_out = jnp.concatenate(out_own, axis=0)
    normed_part = dot(qkv_grad, w_qkv, NT)
    normed_low = normed_part.astype(bf16)
    normed_line = Line(normed_low)
    sent = normed_line.send()
    weight_grad = dot(after(gathered, *sent), qkv_grad, TN).astype(bf16)
    attn_gain_grad = jnp.sum(normed_part * gathered.astype(f32), axis=0) / attn_gain.astype(f32)
    gain_rows = [attn_gain_grad[None, :], moe_gain_grad[None, :]]
    gain_rows += [jnp.pad(part, ((0, 0), (0, width - HD))) for part in (query_gain_grad, key_gain_grad)]
    small = add_up(jnp.concatenate([router_grad, *gain_rows], axis=0), "expert")
    blocks = weight_grad.reshape(n_expert, -1, weight_grad.shape[1])
    blocks = [lax.dynamic_index_in_dim(blocks, order[r], 0, keepdims=False) for r in range(n_expert)]
    far, near = (
        jnp.concatenate(part, axis=0) for part in (blocks[: n_expert // 2], blocks[n_expert // 2 :])
    )
    grad_qkv = Exchange(far, near, bits)
    sent = normed_line.send(small, far, near)
    small = add_up(after(small, *sent), "tensor") if sent else add_up(small, "tensor")
    sent = sum([grad_qkv.send(*sent) for _ in bits[1:]], [])
    grad_qkv = grad_qkv.total().astype(f32)
    normed_grad = normed_line.total(*sent)
    layer_out = (middle + moe_out.astype(f32)).astype(bf16)
    if chunks == 2:
        grads = [down_grad, gate_grad, up_grad]
    grad_down = grads[0].reshape(local_experts, quarter, width)
    grad_gate, grad_up = (
        part.reshape(width, local_experts, quarter).transpose(1, 0, 2) for part in grads[1:]
    )
    hidden_part, _ = attn_pull(normed_grad)
    input_grad = middle_grad + hidden_part
    return (
        layer_out,
        input_grad,
        small[n_experts],
        small[n_experts + 2, :HD],
        small[n_experts + 3, :HD],
        grad_qkv,
        grad_out.astype(f32).T,
        small[n_experts + 1],
        small[:n_experts].T,
        grad_gate,
        grad_up,
        grad_down,
    )


def solution(mesh):
    in_specs = (
        P(("expert", "tensor"), None),
        P(),
        P(),
        P(),
        P(None, "tensor"),
        P("tensor", None),
        P(),
        P(),
        P("expert", None, "tensor"),
        P("expert", None, "tensor"),
        P("expert", "tensor", None),
        P("expert", None),
        P("expert", None),
        P(("expert", "tensor"), None),
    )
    out_specs = (
        P(("expert", "tensor"), None),
        P(("expert", "tensor"), None),
        P(),
        P(),
        P(),
        P("expert", "tensor"),
        P("tensor", "expert"),
        P(),
        P(),
        P("expert", None, "tensor"),
        P("expert", None, "tensor"),
        P("expert", "tensor", None),
    )
    return jax.shard_map(local, mesh=mesh, in_specs=in_specs, out_specs=out_specs, check_vma=False)
```

```python
import functools
import itertools
import jax
import jax.numpy as jnp
from jax import lax
from jax.experimental import pallas as pl
from jax.experimental.pallas import tpu as pltpu
from jax.sharding import PartitionSpec as P

HD = 128
ATT_BLOCK = 256
norm_eps = 1e-06
rope_base = 1000000.0
bf16 = jnp.bfloat16
f32 = jnp.float32
MIB = 1 << 20


def dot(a, b, contract=((1,), (0,))):
    return lax.dot_general(a, b, (contract, ((), ())), preferred_element_type=f32)


NT = ((1,), (1,))
TN = ((0,), (0,))


def rope_tables(length):
    half = HD // 2
    freqs = jnp.power(rope_base, -(jnp.arange(half).astype(f32) * (2.0 / HD)))
    angles = jnp.arange(length).astype(f32)[:, None] * freqs[None, :]
    cosine, sine = jnp.cos(angles), jnp.sin(angles)
    return jnp.concatenate([cosine, cosine], axis=1), jnp.concatenate([-sine, sine], axis=1)


def project_kernel(local_q, local_kv, x_ref, w_ref, qg_ref, kg_ref, cos_ref, sin_ref, raw_ref, q_ref, k_ref, v_ref):
    raw = dot(x_ref[...], w_ref[...])
    cosine, sine = cos_ref[...], sin_ref[...]
    raw_ref[...] = raw[:, : (local_q + local_kv) * HD]
    for h in range(local_q + local_kv):
        head = raw[:, h * HD : (h + 1) * HD]
        gain = qg_ref[...] if h < local_q else kg_ref[...]
        normed = head * lax.rsqrt(jnp.mean(head * head, axis=1, keepdims=True) + norm_eps) * gain
        turned = (normed * cosine + pltpu.roll(normed, HD // 2, 1) * sine).astype(bf16)
        if h < local_q:
            q_ref[:, h * HD : (h + 1) * HD] = turned
        else:
            k_ref[:, (h - local_q) * HD : (h - local_q + 1) * HD] = turned
    v_ref[...] = raw[:, (local_q + local_kv) * HD :].astype(bf16)


def project(x, w, q_gain, k_gain, cosine, sine, local_q, local_kv):
    rows, width = x.shape
    tile = 256
    cols = w.shape[1]
    full = lambda shape: pl.BlockSpec(shape, lambda i: (0,) * len(shape))
    row = lambda n: pl.BlockSpec((tile, n), lambda i: (i, 0))
    heads = local_q + local_kv
    return pl.pallas_call(
        functools.partial(project_kernel, local_q, local_kv),
        grid=(rows // tile,),
        in_specs=[row(width), full((width, cols)), full((1, HD)), full((1, HD)), row(HD), row(HD)],
        out_specs=[row(heads * HD), row(local_q * HD), row(local_kv * HD), row(local_kv * HD)],
        out_shape=[
            jax.ShapeDtypeStruct((rows, heads * HD), f32),
            jax.ShapeDtypeStruct((rows, local_q * HD), bf16),
            jax.ShapeDtypeStruct((rows, local_kv * HD), bf16),
            jax.ShapeDtypeStruct((rows, local_kv * HD), bf16),
        ],
        compiler_params=pltpu.CompilerParams(vmem_limit_bytes=40 * MIB),
        cost_estimate=pl.CostEstimate(flops=2 * rows * width * cols, bytes_accessed=rows * width * 2 + width * cols * 2 + rows * cols * 6, transcendentals=0),
        name="project",
    )(x, w, q_gain, k_gain, cosine, sine)


def attend_kernel(scale, q_ref, k_ref, vt_ref, o_ref):
    for b in range(q_ref.shape[0] // ATT_BLOCK):
        n = (b + 1) * ATT_BLOCK
        at = slice(b * ATT_BLOCK, n)
        weight = jnp.exp(dot(k_ref[:n, :], q_ref[at, :], NT) * scale)
        total = jnp.sum(weight, axis=0, keepdims=True)
        mixed = dot(vt_ref[:, :n], weight.astype(bf16)) * (1.0 / total)
        o_ref[at, :] = mixed.T.astype(bf16)


def attend(q, k, v_t, local_q, local_kv):
    rows = q.shape[0]
    repeat = local_q // local_kv
    return pl.pallas_call(
        functools.partial(attend_kernel, HD**-0.5),
        grid=(local_q,),
        in_specs=[
            pl.BlockSpec((rows, HD), lambda h: (0, h)),
            pl.BlockSpec((rows, HD), lambda h: (0, h // repeat)),
            pl.BlockSpec((HD, rows), lambda h: (h // repeat, 0)),
        ],
        out_specs=pl.BlockSpec((rows, HD), lambda h: (0, h)),
        out_shape=jax.ShapeDtypeStruct((rows, local_q * HD), bf16),
        compiler_params=pltpu.CompilerParams(vmem_limit_bytes=32 * MIB),
        cost_estimate=pl.CostEstimate(flops=local_q * rows * rows * HD * 3, bytes_accessed=rows * local_q * HD * 4, transcendentals=local_q * rows * rows),
        name="attend",
    )(q, k, v_t)


def unturn(grad, raw, gain, cosine, sine):
    grad = grad * cosine - pltpu.roll(grad, HD // 2, 1) * sine
    inv = lax.rsqrt(jnp.mean(raw * raw, axis=1, keepdims=True) + norm_eps)
    part = gain * grad
    back = inv * part - raw * (inv * inv * inv) * jnp.mean(raw * part, axis=1, keepdims=True)
    return back, jnp.sum(grad * raw * inv, axis=0, keepdims=True)


def attend_back_kernel(
    scale, repeat, q_ref, do_ref, raw_ref, k_ref, kt_ref, v_ref, rawk_ref, qg_ref, kg_ref, cos_ref, sin_ref,
    dq_ref, dk_ref, dv_ref, dqg_ref, dkg_ref, dqs, dks, dvs,
):
    h = pl.program_id(0)

    @pl.when(h == 0)
    def _():
        dqg_ref[...] = jnp.zeros_like(dqg_ref)
        dkg_ref[...] = jnp.zeros_like(dkg_ref)

    @pl.when(lax.rem(h, repeat) == 0)
    def _():
        dks[...] = jnp.zeros_like(dks)
        dvs[...] = jnp.zeros_like(dvs)

    for b in range(q_ref.shape[0] // ATT_BLOCK):
        n = (b + 1) * ATT_BLOCK
        at = slice(b * ATT_BLOCK, n)
        query, given = q_ref[at, :], do_ref[at, :]
        weight = jnp.exp(dot(k_ref[:n, :], query, NT) * scale)
        prob = weight * (1.0 / jnp.sum(weight, axis=0, keepdims=True))
        prob_grad = dot(v_ref[:n, :], given, NT)
        inner = jnp.sum(prob * prob_grad, axis=0, keepdims=True)
        score_grad = (prob * (prob_grad - inner)).astype(bf16)
        dks[:n, :] += dot(score_grad, query)
        dvs[:n, :] += dot(prob.astype(bf16), given)
        dqs[at, :] = dot(kt_ref[:, :n], score_grad).T * scale
    back, gain_part = unturn(dqs[...], raw_ref[...], qg_ref[...], cos_ref[...], sin_ref[...])
    dq_ref[...] = back.astype(bf16)
    dqg_ref[...] += gain_part

    @pl.when(lax.rem(h, repeat) == repeat - 1)
    def _():
        back_k, gain_k = unturn(dks[...] * scale, rawk_ref[...], kg_ref[...], cos_ref[...], sin_ref[...])
        dk_ref[...] = back_k.astype(bf16)
        dv_ref[...] = dvs[...].astype(bf16)
        dkg_ref[...] += gain_k


def attend_back(q, given, raw, k, k_t, v, q_gain, k_gain, cosine, sine, local_q, local_kv):
    rows = q.shape[0]
    repeat = local_q // local_kv
    head = pl.BlockSpec((rows, HD), lambda h: (0, h))
    shared = pl.BlockSpec((rows, HD), lambda h: (0, h // repeat))
    whole = pl.BlockSpec((rows, HD), lambda h: (0, 0))
    gain = pl.BlockSpec((1, HD), lambda h: (0, 0))
    return pl.pallas_call(
        functools.partial(attend_back_kernel, HD**-0.5, repeat),
        grid=(local_q,),
        in_specs=[
            head, head, head, shared, pl.BlockSpec((HD, rows), lambda h: (h // repeat, 0)), shared,
            pl.BlockSpec((rows, HD), lambda h: (0, local_q + h // repeat)), gain, gain, whole, whole,
        ],
        out_specs=[head, shared, shared, gain, gain],
        out_shape=[
            jax.ShapeDtypeStruct((rows, local_q * HD), bf16),
            jax.ShapeDtypeStruct((rows, local_kv * HD), bf16),
            jax.ShapeDtypeStruct((rows, local_kv * HD), bf16),
            jax.ShapeDtypeStruct((1, HD), f32),
            jax.ShapeDtypeStruct((1, HD), f32),
        ],
        scratch_shapes=[pltpu.VMEM((rows, HD), f32)] * 3,
        compiler_params=pltpu.CompilerParams(vmem_limit_bytes=40 * MIB),
        cost_estimate=pl.CostEstimate(flops=local_q * rows * rows * HD * 7, bytes_accessed=rows * local_q * HD * 10, transcendentals=local_q * rows * rows),
        name="attend_back",
    )(q, given, raw, k, k_t, v, raw, q_gain, k_gain, cosine, sine)


def experts_kernel(
    held, order, x_ref, pre_ref, gate_ref, spread_ref, wg_ref, wu_ref, *refs
):
    hw_ref, gb_ref, ub_ref, score_ref, *back_refs = refs[held:]
    x = x_ref[...]
    gate_pre = dot(x, wg_ref[...])
    sigma = 1.0 / (1.0 + jnp.exp(-gate_pre))
    active = gate_pre * sigma
    up_pre = dot(x, wu_ref[...])
    pre = pre_ref[...].reshape(gate_pre.shape)
    hidden = active * up_pre
    score_ref[...] = dot(spread_ref[...], (hidden * pre).astype(bf16), NT).reshape(score_ref.shape)
    weight = dot(gate_ref[...], spread_ref[...])
    hw_ref[...] = (hidden * weight).astype(bf16).reshape(hw_ref.shape)
    hidden_grad = pre * weight
    up_back = (hidden_grad * active).astype(bf16)
    gate_back = (hidden_grad * up_pre * sigma * (1.0 + gate_pre * (1.0 - sigma))).astype(bf16)
    gb_ref[...] = gate_back
    ub_ref[...] = up_back
    back = (dot(gate_back, wg_ref[...], NT) + dot(up_back, wu_ref[...], NT)).astype(bf16)
    if len(back_refs) == 1:
        back_refs[0][...] = back
        return
    first = pl.program_id(0) < pl.num_programs(0) // 2

    @pl.when(first)
    def _():
        back_refs[0][...] = back

    @pl.when(jnp.logical_not(first))
    def _():
        back_refs[1][...] = back


def row_block(array, c):
    _, members, _, piece, columns = array.shape
    return pl.BlockSpec((1, members, 1, piece, columns), lambda j, order: (order[j], 0, c, 0, 0))


def experts(order, c, x, pre, gates, spread, gate_w, up_w, held=(), halves=False):
    rows, width = x.shape
    tile = rows // pre.shape[0]
    hidden = gate_w.shape[1]
    lanes = spread.shape[0]
    steps = order.shape[0]
    half = steps // 2
    spots = [lambda j, order: (j, 0)]
    if halves:
        spots = [lambda j, order: (jnp.minimum(j, half - 1), 0), lambda j, order: (jnp.maximum(j - half, 0), 0)]
    at = lambda n: pl.BlockSpec((tile, n), lambda j, order: (order[j], 0))
    full = lambda shape: pl.BlockSpec(shape, lambda j, order: (0, 0), pipeline_mode=pl.Buffered(1))
    return pl.pallas_call(
        functools.partial(experts_kernel, len(held)),
        grid_spec=pltpu.PrefetchScalarGridSpec(
            num_scalar_prefetch=1,
            grid=(steps,),
            in_specs=[
                at(width), row_block(pre, c), at(lanes), full((lanes, hidden)), full((width, hidden)), full((width, hidden)),
                *[pl.BlockSpec(memory_space=pl.ANY)] * len(held),
            ],
            out_specs=[
                row_block(pre, c), at(hidden), at(hidden), pl.BlockSpec((1, lanes, tile), lambda j, order: (order[j], 0, 0)),
                *[pl.BlockSpec((tile, width), spot) for spot in spots],
            ],
        ),
        out_shape=[
            jax.ShapeDtypeStruct(pre.shape, bf16),
            jax.ShapeDtypeStruct((rows, hidden), bf16),
            jax.ShapeDtypeStruct((rows, hidden), bf16),
            jax.ShapeDtypeStruct((rows // tile, lanes, tile), f32),
            *[jax.ShapeDtypeStruct((steps * tile // len(spots), width), bf16) for _ in spots],
        ],
        input_output_aliases={7 + i: output for i, (output, _) in enumerate(held)},
        compiler_params=pltpu.CompilerParams(vmem_limit_bytes=58 * MIB),
        cost_estimate=pl.CostEstimate(flops=8 * steps * tile * width * hidden, bytes_accessed=steps * tile * (width * 4 + hidden * 10), transcendentals=steps * tile * hidden),
        name="experts",
    )(order, x, pre, gates, spread, gate_w, up_w, *[array for _, array in held])


def outputs_kernel(order, h_ref, w_ref, out_ref):
    hidden = h_ref[...].reshape(out_ref.shape[0], w_ref.shape[0])
    out_ref[...] = dot(hidden, w_ref[...]).astype(bf16)


def outputs(order, c, hidden_wt, down_w):
    _, members, _, piece, hidden = hidden_wt.shape
    steps = order.shape[0]
    tile = members * piece
    width = down_w.shape[1]
    return pl.pallas_call(
        outputs_kernel,
        grid_spec=pltpu.PrefetchScalarGridSpec(
            num_scalar_prefetch=1,
            grid=(steps,),
            in_specs=[
                row_block(hidden_wt, c),
                pl.BlockSpec((hidden, width), lambda j, order: (0, 0), pipeline_mode=pl.Buffered(1)),
            ],
            out_specs=pl.BlockSpec((tile, width), lambda j, order: (j, 0)),
        ),
        out_shape=jax.ShapeDtypeStruct((steps * tile, width), bf16),
        compiler_params=pltpu.CompilerParams(vmem_limit_bytes=32 * MIB),
        cost_estimate=pl.CostEstimate(flops=1, bytes_accessed=1, transcendentals=0),
        name="outputs",
    )(order, hidden_wt, down_w)


TOPK = 8


def row_norm(values, gain):
    return values * lax.rsqrt(jnp.mean(values * values, axis=-1, keepdims=True) + norm_eps) * gain


def after(value, *others):
    return lax.optimization_barrier((value, *others))[0]


def hop(block, bit, axis):
    size = lax.axis_size(axis)
    return lax.ppermute(block, axis, [(i, i ^ bit) for i in range(size)])


def bits_of(size):
    return [1 << k for k in range(size.bit_length() - 1)]


def step_order(bits):
    order = [0]
    for bit in reversed(bits):
        order = [r | bit for r in order] + order
    return order


class Exchange:
    def __init__(self, far, near, bits):
        self.moved = [hop(far, bits[0], "expert")]
        self.near, self.rest = near, bits[1:]
        self.left = [list(range(len(self.rest))) for _ in range(2)]
        self.sides = None

    def wait(self, behind):
        if self.sides is None:
            moved = after(self.moved, *behind) if behind else self.moved
            rows, width = self.near.shape[0] >> len(self.rest), self.near.shape[1]
            near, moved = self.near.reshape(-1, rows, width), moved[0].reshape(-1, rows, width)
            spots = itertools.product(range(2), repeat=len(self.rest))
            index = {spot: i for i, spot in enumerate(spots)}
            self.sides = []
            for part in (slice(0, rows // 2), slice(rows // 2, None)):
                self.sides.append({spot: [near[i, part], moved[i, part]] for spot, i in index.items()})
        else:
            for number, (side, got) in enumerate(zip(self.sides, self.got)):
                got = after(got, *behind) if behind else got
                self.sides[number] = {spot: [*parts, got[i]] for i, (spot, parts) in enumerate(side.items())}

    def send(self, *behind):
        self.wait(behind)
        sent, self.got = [], []
        add = lambda parts: sum(p.astype(f32) for p in parts).astype(bf16)
        for number, side in enumerate(self.sides):
            at = len(self.left[number]) - 1 if number else 0
            bit = self.rest[self.left[number].pop(at)]
            spots = sorted({spot[:at] + spot[at + 1 :] for spot in side})
            block = jnp.stack([add(side[spot[:at] + (0,) + spot[at:]]) for spot in spots])
            self.got.append(hop(block, bit, "expert"))
            sent.append(block)
            self.sides[number] = {spot: side[spot[:at] + (1,) + spot[at:]] for spot in spots}
        return sent

    def total(self, *behind):
        while any(self.left):
            self.send()
        self.wait(behind)
        parts = [sum(p.astype(f32) for p in side[()]).astype(bf16) for side in self.sides]
        return jnp.concatenate(parts, axis=0)


def neighbours():
    size = lax.axis_size("tensor")
    up = lambda v: lax.ppermute(v, "tensor", [(i, (i + 1) % size) for i in range(size)])
    down = lambda v: lax.ppermute(v, "tensor", [(i, (i - 1) % size) for i in range(size)])
    return up, down


def gather_line(block, behind=()):
    size, me = lax.axis_size("tensor"), lax.axis_index("tensor")
    if size != 4:
        return lax.all_gather(block, "tensor", axis=0, tiled=True)
    rows = block.shape[0]
    cut = rows // 2
    up, down = neighbours()
    low, high = up(block), down(block)
    if behind:
        low, high = after((low, high), *behind)
    far_low, far_high = up(low[:cut]), down(high[cut:])
    whole = jnp.zeros((rows * size, block.shape[1]), block.dtype)
    for part, member, shift in ((block, 0, 0), (low, 3, 0), (high, 1, 0), (far_low, 2, 0), (far_high, 2, cut)):
        at = lax.rem(me + member, size) * rows + shift
        whole = lax.dynamic_update_slice(whole, part, (at, 0))
    return whole


class Line:
    def __init__(self, part):
        self.size, self.me = lax.axis_size("tensor"), lax.axis_index("tensor")
        self.part, self.rows = part, part.shape[0] // self.size
        self.got = None

    def of(self, member, start, end):
        at = lax.rem(self.me + member, self.size) * self.rows
        return lax.dynamic_slice_in_dim(self.part, at + start, end - start, 0)

    def send(self, *behind):
        cut, rows = self.rows // 2, self.rows
        if self.size != 4:
            return []
        if behind:
            self.got = after(self.got, *behind)
        if self.got is None:
            low, high = self.of(2, cut, rows), self.of(2, 0, cut)
        else:
            from_low, from_high = (part.astype(f32) for part in self.got)
            low = jnp.concatenate([self.of(1, 0, cut), (self.of(1, cut, rows).astype(f32) + from_low).astype(bf16)])
            high = jnp.concatenate([(self.of(3, 0, cut).astype(f32) + from_high).astype(bf16), self.of(3, cut, rows)])
        up, down = neighbours()
        self.got = up(low), down(high)
        return [low, high]

    def total(self, *behind):
        if self.size != 4:
            return lax.psum_scatter(self.part, "tensor", scatter_dimension=0, tiled=True).astype(f32)
        low, high = after(self.got, *behind) if behind else self.got
        return self.of(0, 0, self.rows).astype(f32) + low.astype(f32) + high.astype(f32)


def local(
    hidden_in,
    attn_gain,
    query_gain,
    key_gain,
    w_qkv,
    w_out,
    moe_gain,
    w_router,
    w_gate,
    w_up,
    w_down,
    routes,
    pair_rank,
    out_grad,
):
    tok_dev, width = hidden_in.shape
    n_tensor = lax.axis_size("tensor")
    n_expert = lax.axis_size("expert")
    member = lax.axis_index("tensor")
    place = lax.axis_index("expert")
    group = tok_dev * n_tensor
    local_experts = w_gate.shape[0]
    quarter = w_gate.shape[2]
    n_experts = local_experts * n_expert
    hidden_loc = local_experts * quarter
    capacity = 9 * group * TOPK // (8 * n_experts)
    local_q = w_out.shape[0] // HD
    local_kv = (w_qkv.shape[1] // HD - local_q) // 2
    both = ("expert", "tensor")
    bits = bits_of(n_expert)
    chunks = 2 * max(n_expert // 8, 1)
    piece = tok_dev // chunks
    first = 16 * (tok_dev * 9 // 256) if chunks == 2 else piece
    lanes = 8 * (-(-local_experts // 8))

    gate_w = w_gate.transpose(1, 0, 2).reshape(width, hidden_loc)
    up_w = w_up.transpose(1, 0, 2).reshape(width, hidden_loc)
    down_w = w_down.reshape(hidden_loc, width)
    spread = (jnp.arange(hidden_loc)[None, :] // quarter == jnp.arange(lanes)[:, None]).astype(bf16)

    hidden_f = hidden_in.astype(f32)
    attn_normed, attn_pull = jax.vjp(row_norm, hidden_f, attn_gain.astype(f32))
    gathered = gather_line(attn_normed.astype(bf16))
    given = after(out_grad, gathered)

    cosine, sine = rope_tables(group)
    q_gain, k_gain = query_gain.astype(f32)[None, :], key_gain.astype(f32)[None, :]
    if chunks == 2:
        gathered = after(gathered, gate_w, up_w)
    raw, queries, keys, values = project(gathered, w_qkv, q_gain, k_gain, cosine, sine, local_q, local_kv)
    mixed_all = attend(queries, keys, values.T, local_q, local_kv)
    attn = mixed_all
    if chunks == 2:
        grad_line = [
            gather_line(given[:first], (queries,)),
            gather_line(after(given[first:], queries), (mixed_all,)),
        ]
        grad_all = [lax.all_gather(part, "expert", axis=0, tiled=True) for part in grad_line]
        pre = [dot(part, down_w, NT).reshape(n_expert, n_tensor, 1, -1, hidden_loc) for part in grad_all]
        attn = after(attn, *grad_line)
    attn = Line(dot(attn, w_out).astype(bf16))
    attn.send()
    attn.send()
    attn = attn.total()
    middle = hidden_f + attn
    moe_normed, moe_pull = jax.vjp(row_norm, middle, moe_gain.astype(f32))
    moe_in = moe_normed.astype(bf16)

    expert_ids = jnp.arange(n_experts, dtype=jnp.int32)
    hits = routes.T[None, :, :] == expert_ids[:, None, None]
    ranks = jnp.where(hits, pair_rank[0].reshape(group, TOPK).T[None, :, :] + 1, 0).sum(axis=1)
    ranks = jnp.where(ranks == 0, group * TOPK + 1, ranks)
    own_ranks = lax.dynamic_slice_in_dim(ranks, member * tok_dev, tok_dev, 1)
    before = (ranks[:, :, None] < own_ranks[:, None, :]).astype(f32).sum(axis=1)
    routed = own_ranks <= group * TOPK
    keep = routed & (before < capacity)

    logits = dot(w_router, moe_in, ((0,), (1,)))
    gates = jax.nn.softmax(jnp.where(routed, logits, -jnp.inf), axis=0)
    sent_gates = jnp.where(keep, gates, 0.0).astype(bf16).astype(f32)
    gates_in = jnp.broadcast_to(
        sent_gates.reshape(n_expert, 1, local_experts, tok_dev), (n_expert, n_tensor, local_experts, tok_dev)
    )
    gates_in = lax.all_to_all(gates_in.reshape(-1, local_experts, tok_dev), both, 0, 0, tiled=True)
    gates_in = gates_in.reshape(n_expert, n_tensor, local_experts, tok_dev).transpose(0, 1, 3, 2)
    gates_in = jnp.pad(gates_in, ((0, 0), (0, 0), (0, 0), (0, lanes - local_experts))).astype(bf16)

    def gates_of(start, count):
        return lax.dynamic_slice_in_dim(gates_in, start, count, 2).reshape(-1, lanes)

    order = place ^ jnp.array(step_order(bits), jnp.int32)

    def own_rows(part):
        return lax.psum_scatter(part, "tensor", scatter_dimension=0, tiled=True)

    def to_tokens(scores):
        scores = [s[:, :local_experts].reshape(n_expert, local_experts, n_tensor, -1) for s in scores]
        scores = jnp.concatenate(scores, axis=3).transpose(0, 2, 1, 3)
        scores = lax.all_to_all(scores.reshape(-1, local_experts, tok_dev), both, 0, 0, tiled=True)
        scores = scores.reshape(n_expert, n_tensor, local_experts, tok_dev).sum(axis=1)
        return jnp.where(keep, scores.reshape(n_experts, tok_dev), 0.0)

    if chunks == 2:
        moe_line = [gather_line(moe_in[:first], (pre[0],)), gather_line(moe_in[first:])]
        gates_0, gates_1 = gates_of(0, first), gates_of(first, tok_dev - first)
        moe_line[0] = after(moe_line[0], grad_all[1])
        moe_all = [lax.all_gather(part, "expert", axis=0, tiled=True) for part in moe_line]
        front, rear = order[: n_expert // 2], order[n_expert // 2 :]
        fixed = (spread, gate_w, up_w)
        x_0 = after(moe_all[0], pre[1])
        *kept_0, back_0 = experts(jnp.arange(n_expert, dtype=jnp.int32), 0, x_0, pre[0], gates_0, *fixed)
        back_0 = lax.psum_scatter(back_0, "expert", scatter_dimension=0, tiled=True)
        back_own = [own_rows(back_0)]
        far_0 = outputs(front, 0, kept_0[0], down_w)
        x_1 = after(moe_all[1], far_0)
        *kept_1, far, near = experts(order, 0, x_1, pre[1], gates_1, *fixed, halves=True)
        back_1 = Exchange(far, near, bits)
        x_0 = after(moe_all[0], kept_1[3])
        gate_grad = dot(x_0, kept_0[1], TN)
        scores = to_tokens([kept_0[3], kept_1[3]])
        sent = back_1.send(gate_grad, scores)
        hidden_0, hidden_1 = after((kept_0[0], kept_1[0]), *sent)
        near_0 = outputs(rear, 0, hidden_0, down_w)
        far_1, near_1 = (outputs(part, 0, hidden_1, down_w) for part in (front, rear))
        sent = back_1.send(near_0, far_1, near_1, back_0)
        out_0, out_1 = Exchange(far_0, near_0, bits), Exchange(far_1, near_1, bits)
        sent = out_0.send(*sent)
        up_grad = dot(after(x_0, *sent), kept_0[2], TN)
        back_1 = back_1.total(up_grad, back_own[0])
        back_own.append(own_rows(back_1))
        x_1, g_0 = after((moe_all[1], grad_all[0]), back_1)
        gate_grad = gate_grad + dot(x_1, kept_1[1], TN)
        down_grad = dot(kept_0[0].reshape(-1, hidden_loc), g_0, TN)
        sent = out_0.send(gate_grad, down_grad)
        back_own = after(back_own, *sent)
    else:
        def one_chunk(sums, c):
            x_c = lax.all_gather(lax.dynamic_slice_in_dim(moe_in, c * piece, piece, 0), both, axis=0, tiled=True)
            g_c = lax.all_gather(lax.dynamic_slice_in_dim(given, c * piece, piece, 0), both, axis=0, tiled=True)
            gates_c = gates_of(c * piece, piece)
            pre = dot(g_c, down_w, NT).reshape(n_expert, n_tensor, 1, piece, hidden_loc)
            given_c = (0, x_c, pre, gates_c, spread, gate_w, up_w)
            *kept, far = experts(order[: n_expert // 2], *given_c)
            *kept, near = experts(order[n_expert // 2 :], *given_c, list(enumerate(kept)))
            hw, gate_back, up_back, score = kept
            parts = (dot(hw.reshape(-1, hidden_loc), g_c, TN), dot(x_c, gate_back, TN), dot(x_c, up_back, TN))
            sums = tuple(a + b for a, b in zip(sums, parts))
            back = own_rows(Exchange(far, near, bits).total())
            out = [outputs(part, 0, hw, down_w) for part in (order[: n_expert // 2], order[n_expert // 2 :])]
            out = own_rows(Exchange(*out, bits).total())
            return sums, (back, score, out)

        zeros = (
            jnp.zeros((hidden_loc, width), f32),
            jnp.zeros((width, hidden_loc), f32),
            jnp.zeros((width, hidden_loc), f32),
        )
        grads, (back_own, scores, out_own) = lax.scan(one_chunk, zeros, jnp.arange(chunks))
        scores = to_tokens(scores)
        moe_out = jnp.concatenate(list(out_own), axis=0)
    moe_back = jnp.concatenate(list(back_own), axis=0).astype(f32)

    inner_gate = jnp.sum(gates * scores, axis=0, keepdims=True)
    logit_grad = (gates * (scores - inner_gate)).astype(bf16)
    router_grad = dot(logit_grad, moe_in)
    moe_in_grad = moe_back + dot(logit_grad, w_router, ((0,), (1,)))
    middle_part, moe_gain_grad = moe_pull(moe_in_grad)
    middle_grad = out_grad.astype(f32) + middle_part

    middle_all = lax.all_gather(middle_grad.astype(bf16), "tensor", axis=0, tiled=True)
    if chunks == 2:
        sent = out_1.send(middle_grad)
        x_1, g_1 = after((moe_all[1], grad_all[1]), *sent)
        up_grad = up_grad + dot(x_1, kept_1[2], TN)
        out_0 = out_0.total(up_grad)
        down_grad = down_grad + dot(kept_1[0].reshape(-1, hidden_loc), after(g_1, out_0), TN)
        sent = out_1.send(down_grad)
        middle_all = after(middle_all, *sent)
    mixed_grad = dot(middle_all, w_out, NT).astype(bf16)
    if chunks == 2:
        out_1 = out_1.total(mixed_grad)
        mixed_grad = after(mixed_grad, out_1)
    dq, dk, dv, query_gain_grad, key_gain_grad = attend_back(
        queries, mixed_grad, raw, keys, keys.T, values, q_gain, k_gain, cosine, sine, local_q, local_kv
    )
    qkv_grad = jnp.concatenate([dq, dk, dv], axis=1)
    if chunks == 2:
        out_own = [own_rows(part) for part in (out_0, out_1)]
        qkv_grad = after(qkv_grad, out_own[0])
        moe_out = jnp.concatenate(out_own, axis=0)
    normed_part = dot(qkv_grad, w_qkv, NT)
    normed_low = normed_part.astype(bf16)
    normed_line = Line(normed_low)
    sent = normed_line.send()
    out_weight_grad = dot(middle_all, after(mixed_all, *sent), TN).astype(bf16)
    grad_out = lax.psum_scatter(out_weight_grad, "expert", scatter_dimension=0, tiled=True)
    weight_grad = dot(after(gathered, *sent), qkv_grad, TN).astype(bf16)
    attn_gain_grad = jnp.sum(normed_part * gathered.astype(f32), axis=0) / attn_gain.astype(f32)
    gain_rows = [attn_gain_grad[None, :], moe_gain_grad[None, :]]
    gain_rows += [jnp.pad(part, ((0, 0), (0, width - HD))) for part in (query_gain_grad, key_gain_grad)]
    small = jnp.concatenate([router_grad, *gain_rows], axis=0)
    small = jnp.pad(small, ((0, -small.shape[0] % n_expert), (0, 0))).reshape(n_expert, -1, width)
    small = lax.all_to_all(small, "expert", 0, 0, tiled=True).sum(axis=0)
    small = jnp.broadcast_to(small[None], (n_tensor, *small.shape))
    small = lax.all_to_all(small, "tensor", 0, 0, tiled=True).sum(axis=0)
    blocks = weight_grad.reshape(n_expert, -1, weight_grad.shape[1])
    blocks = [lax.dynamic_index_in_dim(blocks, place ^ r, 0, keepdims=False) for r in step_order(bits)]
    far, near = (
        jnp.concatenate(part, axis=0) for part in (blocks[: n_expert // 2], blocks[n_expert // 2 :])
    )
    grad_qkv = Exchange(far, near, bits)
    sent = normed_line.send(small, far, near)
    small = after(small, *sent) if sent else small
    small = lax.all_to_all(jnp.broadcast_to(small[None], (n_expert, *small.shape)), "expert", 0, 0, tiled=True)
    small = small.reshape(-1, width)
    sent = sum([grad_qkv.send(*sent) for _ in bits[1:]], [])
    grad_qkv = grad_qkv.total().astype(f32)
    normed_grad = normed_line.total(*sent)
    layer_out = (middle + moe_out.astype(f32)).astype(bf16)
    if chunks == 2:
        grads = [down_grad, gate_grad, up_grad]
    grad_down = grads[0].reshape(local_experts, quarter, width)
    grad_gate, grad_up = (
        part.reshape(width, local_experts, quarter).transpose(1, 0, 2) for part in grads[1:]
    )
    hidden_part, _ = attn_pull(normed_grad)
    input_grad = middle_grad + hidden_part
    return (
        layer_out,
        input_grad,
        small[n_experts],
        small[n_experts + 2, :HD],
        small[n_experts + 3, :HD],
        grad_qkv,
        grad_out.astype(f32).T,
        small[n_experts + 1],
        small[:n_experts].T,
        grad_gate,
        grad_up,
        grad_down,
    )


def solution(mesh):
    in_specs = (
        P(("expert", "tensor"), None),
        P(),
        P(),
        P(),
        P(None, "tensor"),
        P("tensor", None),
        P(),
        P(),
        P("expert", None, "tensor"),
        P("expert", None, "tensor"),
        P("expert", "tensor", None),
        P("expert", None),
        P("expert", None),
        P(("expert", "tensor"), None),
    )
    out_specs = (
        P(("expert", "tensor"), None),
        P(("expert", "tensor"), None),
        P(),
        P(),
        P(),
        P("expert", "tensor"),
        P("tensor", "expert"),
        P(),
        P(),
        P("expert", None, "tensor"),
        P("expert", None, "tensor"),
        P("expert", "tensor", None),
    )
    return jax.shard_map(local, mesh=mesh, in_specs=in_specs, out_specs=out_specs, check_vma=False)
```

```python
import functools
import itertools
import jax
import jax.numpy as jnp
from jax import lax
from jax.experimental import pallas as pl
from jax.experimental.pallas import tpu as pltpu
from jax.sharding import PartitionSpec as P

HD = 128
ATT_BLOCK = 256
norm_eps = 1e-06
rope_base = 1000000.0
bf16 = jnp.bfloat16
f32 = jnp.float32
MIB = 1 << 20


def dot(a, b, contract=((1,), (0,))):
    return lax.dot_general(a, b, (contract, ((), ())), preferred_element_type=f32)


NT = ((1,), (1,))
TN = ((0,), (0,))


def rope_tables(length):
    half = HD // 2
    freqs = jnp.power(rope_base, -(jnp.arange(half).astype(f32) * (2.0 / HD)))
    angles = jnp.arange(length).astype(f32)[:, None] * freqs[None, :]
    cosine, sine = jnp.cos(angles), jnp.sin(angles)
    return jnp.concatenate([cosine, cosine], axis=1), jnp.concatenate([-sine, sine], axis=1)


def project_kernel(local_q, local_kv, x_ref, w_ref, qg_ref, kg_ref, cos_ref, sin_ref, raw_ref, q_ref, k_ref, v_ref):
    raw = dot(x_ref[...], w_ref[...])
    cosine, sine = cos_ref[...], sin_ref[...]
    raw_ref[...] = raw[:, : (local_q + local_kv) * HD]
    for h in range(local_q + local_kv):
        head = raw[:, h * HD : (h + 1) * HD]
        gain = qg_ref[...] if h < local_q else kg_ref[...]
        normed = head * lax.rsqrt(jnp.mean(head * head, axis=1, keepdims=True) + norm_eps) * gain
        turned = (normed * cosine + pltpu.roll(normed, HD // 2, 1) * sine).astype(bf16)
        if h < local_q:
            q_ref[:, h * HD : (h + 1) * HD] = turned
        else:
            k_ref[:, (h - local_q) * HD : (h - local_q + 1) * HD] = turned
    v_ref[...] = raw[:, (local_q + local_kv) * HD :].astype(bf16)


def project(x, w, q_gain, k_gain, cosine, sine, local_q, local_kv):
    rows, width = x.shape
    tile = 256
    cols = w.shape[1]
    full = lambda shape: pl.BlockSpec(shape, lambda i: (0,) * len(shape))
    row = lambda n: pl.BlockSpec((tile, n), lambda i: (i, 0))
    heads = local_q + local_kv
    return pl.pallas_call(
        functools.partial(project_kernel, local_q, local_kv),
        grid=(rows // tile,),
        in_specs=[row(width), full((width, cols)), full((1, HD)), full((1, HD)), row(HD), row(HD)],
        out_specs=[row(heads * HD), row(local_q * HD), row(local_kv * HD), row(local_kv * HD)],
        out_shape=[
            jax.ShapeDtypeStruct((rows, heads * HD), f32),
            jax.ShapeDtypeStruct((rows, local_q * HD), bf16),
            jax.ShapeDtypeStruct((rows, local_kv * HD), bf16),
            jax.ShapeDtypeStruct((rows, local_kv * HD), bf16),
        ],
        compiler_params=pltpu.CompilerParams(vmem_limit_bytes=40 * MIB),
        cost_estimate=pl.CostEstimate(flops=2 * rows * width * cols, bytes_accessed=rows * width * 2 + width * cols * 2 + rows * cols * 6, transcendentals=0),
        name="project",
    )(x, w, q_gain, k_gain, cosine, sine)


def attend_kernel(scale, q_ref, k_ref, vt_ref, o_ref):
    for b in range(q_ref.shape[0] // ATT_BLOCK):
        n = (b + 1) * ATT_BLOCK
        at = slice(b * ATT_BLOCK, n)
        weight = jnp.exp(dot(k_ref[:n, :], q_ref[at, :], NT) * scale)
        total = jnp.sum(weight, axis=0, keepdims=True)
        mixed = dot(vt_ref[:, :n], weight.astype(bf16)) * (1.0 / total)
        o_ref[at, :] = mixed.T.astype(bf16)


def attend(q, k, v_t, local_q, local_kv):
    rows = q.shape[0]
    repeat = local_q // local_kv
    return pl.pallas_call(
        functools.partial(attend_kernel, HD**-0.5),
        grid=(local_q,),
        in_specs=[
            pl.BlockSpec((rows, HD), lambda h: (0, h)),
            pl.BlockSpec((rows, HD), lambda h: (0, h // repeat)),
            pl.BlockSpec((HD, rows), lambda h: (h // repeat, 0)),
        ],
        out_specs=pl.BlockSpec((rows, HD), lambda h: (0, h)),
        out_shape=jax.ShapeDtypeStruct((rows, local_q * HD), bf16),
        compiler_params=pltpu.CompilerParams(vmem_limit_bytes=32 * MIB),
        cost_estimate=pl.CostEstimate(flops=local_q * rows * rows * HD * 3, bytes_accessed=rows * local_q * HD * 4, transcendentals=local_q * rows * rows),
        name="attend",
    )(q, k, v_t)


def unturn(grad, raw, gain, cosine, sine):
    grad = grad * cosine - pltpu.roll(grad, HD // 2, 1) * sine
    inv = lax.rsqrt(jnp.mean(raw * raw, axis=1, keepdims=True) + norm_eps)
    part = gain * grad
    back = inv * part - raw * (inv * inv * inv) * jnp.mean(raw * part, axis=1, keepdims=True)
    return back, jnp.sum(grad * raw * inv, axis=0, keepdims=True)


def attend_back_kernel(
    scale, repeat, q_ref, do_ref, raw_ref, k_ref, kt_ref, v_ref, rawk_ref, qg_ref, kg_ref, cos_ref, sin_ref,
    dq_ref, dk_ref, dv_ref, dqg_ref, dkg_ref, dqs, dks, dvs,
):
    h = pl.program_id(0)

    @pl.when(h == 0)
    def _():
        dqg_ref[...] = jnp.zeros_like(dqg_ref)
        dkg_ref[...] = jnp.zeros_like(dkg_ref)

    @pl.when(lax.rem(h, repeat) == 0)
    def _():
        dks[...] = jnp.zeros_like(dks)
        dvs[...] = jnp.zeros_like(dvs)

    for b in range(q_ref.shape[0] // ATT_BLOCK):
        n = (b + 1) * ATT_BLOCK
        at = slice(b * ATT_BLOCK, n)
        query, given = q_ref[at, :], do_ref[at, :]
        weight = jnp.exp(dot(k_ref[:n, :], query, NT) * scale)
        prob = weight * (1.0 / jnp.sum(weight, axis=0, keepdims=True))
        prob_grad = dot(v_ref[:n, :], given, NT)
        inner = jnp.sum(prob * prob_grad, axis=0, keepdims=True)
        score_grad = (prob * (prob_grad - inner)).astype(bf16)
        dks[:n, :] += dot(score_grad, query)
        dvs[:n, :] += dot(prob.astype(bf16), given)
        dqs[at, :] = dot(kt_ref[:, :n], score_grad).T * scale
    back, gain_part = unturn(dqs[...], raw_ref[...], qg_ref[...], cos_ref[...], sin_ref[...])
    dq_ref[...] = back.astype(bf16)
    dqg_ref[...] += gain_part

    @pl.when(lax.rem(h, repeat) == repeat - 1)
    def _():
        back_k, gain_k = unturn(dks[...] * scale, rawk_ref[...], kg_ref[...], cos_ref[...], sin_ref[...])
        dk_ref[...] = back_k.astype(bf16)
        dv_ref[...] = dvs[...].astype(bf16)
        dkg_ref[...] += gain_k


def attend_back(q, given, raw, k, k_t, v, q_gain, k_gain, cosine, sine, local_q, local_kv):
    rows = q.shape[0]
    repeat = local_q // local_kv
    head = pl.BlockSpec((rows, HD), lambda h: (0, h))
    shared = pl.BlockSpec((rows, HD), lambda h: (0, h // repeat))
    whole = pl.BlockSpec((rows, HD), lambda h: (0, 0))
    gain = pl.BlockSpec((1, HD), lambda h: (0, 0))
    return pl.pallas_call(
        functools.partial(attend_back_kernel, HD**-0.5, repeat),
        grid=(local_q,),
        in_specs=[
            head, head, head, shared, pl.BlockSpec((HD, rows), lambda h: (h // repeat, 0)), shared,
            pl.BlockSpec((rows, HD), lambda h: (0, local_q + h // repeat)), gain, gain, whole, whole,
        ],
        out_specs=[head, shared, shared, gain, gain],
        out_shape=[
            jax.ShapeDtypeStruct((rows, local_q * HD), bf16),
            jax.ShapeDtypeStruct((rows, local_kv * HD), bf16),
            jax.ShapeDtypeStruct((rows, local_kv * HD), bf16),
            jax.ShapeDtypeStruct((1, HD), f32),
            jax.ShapeDtypeStruct((1, HD), f32),
        ],
        scratch_shapes=[pltpu.VMEM((rows, HD), f32)] * 3,
        compiler_params=pltpu.CompilerParams(vmem_limit_bytes=40 * MIB),
        cost_estimate=pl.CostEstimate(flops=local_q * rows * rows * HD * 7, bytes_accessed=rows * local_q * HD * 10, transcendentals=local_q * rows * rows),
        name="attend_back",
    )(q, given, raw, k, k_t, v, raw, q_gain, k_gain, cosine, sine)


def experts_kernel(
    held, order, x_ref, pre_ref, gate_ref, spread_ref, wg_ref, wu_ref, *refs
):
    hw_ref, gb_ref, ub_ref, score_ref, *back_refs = refs[held:]
    x = x_ref[...]
    gate_pre = dot(x, wg_ref[...])
    sigma = 1.0 / (1.0 + jnp.exp(-gate_pre))
    active = gate_pre * sigma
    up_pre = dot(x, wu_ref[...])
    pre = pre_ref[...].reshape(gate_pre.shape)
    hidden = active * up_pre
    score_ref[...] = dot(spread_ref[...], (hidden * pre).astype(bf16), NT).reshape(score_ref.shape)
    weight = dot(gate_ref[...], spread_ref[...])
    hw_ref[...] = (hidden * weight).astype(bf16).reshape(hw_ref.shape)
    hidden_grad = pre * weight
    up_back = (hidden_grad * active).astype(bf16)
    gate_back = (hidden_grad * up_pre * sigma * (1.0 + gate_pre * (1.0 - sigma))).astype(bf16)
    gb_ref[...] = gate_back
    ub_ref[...] = up_back
    back = (dot(gate_back, wg_ref[...], NT) + dot(up_back, wu_ref[...], NT)).astype(bf16)
    if len(back_refs) == 1:
        back_refs[0][...] = back
        return
    first = pl.program_id(0) < pl.num_programs(0) // 2

    @pl.when(first)
    def _():
        back_refs[0][...] = back

    @pl.when(jnp.logical_not(first))
    def _():
        back_refs[1][...] = back


def row_block(array, c):
    _, members, _, piece, columns = array.shape
    return pl.BlockSpec((1, members, 1, piece, columns), lambda j, order: (order[j], 0, c, 0, 0))


def experts(order, c, x, pre, gates, spread, gate_w, up_w, held=(), halves=False):
    rows, width = x.shape
    tile = rows // pre.shape[0]
    hidden = gate_w.shape[1]
    lanes = spread.shape[0]
    steps = order.shape[0]
    half = steps // 2
    spots = [lambda j, order: (j, 0)]
    if halves:
        spots = [lambda j, order: (jnp.minimum(j, half - 1), 0), lambda j, order: (jnp.maximum(j - half, 0), 0)]
    at = lambda n: pl.BlockSpec((tile, n), lambda j, order: (order[j], 0))
    full = lambda shape: pl.BlockSpec(shape, lambda j, order: (0, 0), pipeline_mode=pl.Buffered(1))
    return pl.pallas_call(
        functools.partial(experts_kernel, len(held)),
        grid_spec=pltpu.PrefetchScalarGridSpec(
            num_scalar_prefetch=1,
            grid=(steps,),
            in_specs=[
                at(width), row_block(pre, c), at(lanes), full((lanes, hidden)), full((width, hidden)), full((width, hidden)),
                *[pl.BlockSpec(memory_space=pl.ANY)] * len(held),
            ],
            out_specs=[
                row_block(pre, c), at(hidden), at(hidden), pl.BlockSpec((1, lanes, tile), lambda j, order: (order[j], 0, 0)),
                *[pl.BlockSpec((tile, width), spot) for spot in spots],
            ],
        ),
        out_shape=[
            jax.ShapeDtypeStruct(pre.shape, bf16),
            jax.ShapeDtypeStruct((rows, hidden), bf16),
            jax.ShapeDtypeStruct((rows, hidden), bf16),
            jax.ShapeDtypeStruct((rows // tile, lanes, tile), f32),
            *[jax.ShapeDtypeStruct((steps * tile // len(spots), width), bf16) for _ in spots],
        ],
        input_output_aliases={7 + i: output for i, (output, _) in enumerate(held)},
        compiler_params=pltpu.CompilerParams(vmem_limit_bytes=58 * MIB),
        cost_estimate=pl.CostEstimate(flops=8 * steps * tile * width * hidden, bytes_accessed=steps * tile * (width * 4 + hidden * 10), transcendentals=steps * tile * hidden),
        name="experts",
    )(order, x, pre, gates, spread, gate_w, up_w, *[array for _, array in held])


def outputs_kernel(order, h_ref, w_ref, out_ref):
    hidden = h_ref[...].reshape(out_ref.shape[0], w_ref.shape[0])
    out_ref[...] = dot(hidden, w_ref[...]).astype(bf16)


def outputs(order, c, hidden_wt, down_w, flops=1):
    _, members, _, piece, hidden = hidden_wt.shape
    steps = order.shape[0]
    tile = members * piece
    width = down_w.shape[1]
    return pl.pallas_call(
        outputs_kernel,
        grid_spec=pltpu.PrefetchScalarGridSpec(
            num_scalar_prefetch=1,
            grid=(steps,),
            in_specs=[
                row_block(hidden_wt, c),
                pl.BlockSpec((hidden, width), lambda j, order: (0, 0), pipeline_mode=pl.Buffered(1)),
            ],
            out_specs=pl.BlockSpec((tile, width), lambda j, order: (j, 0)),
        ),
        out_shape=jax.ShapeDtypeStruct((steps * tile, width), bf16),
        compiler_params=pltpu.CompilerParams(vmem_limit_bytes=32 * MIB),
        cost_estimate=pl.CostEstimate(flops=flops, bytes_accessed=1, transcendentals=0),
        name="outputs",
    )(order, hidden_wt, down_w)


TOPK = 8


def row_norm(values, gain):
    return values * lax.rsqrt(jnp.mean(values * values, axis=-1, keepdims=True) + norm_eps) * gain


def after(value, *others):
    return lax.optimization_barrier((value, *others))[0]


def hop(block, bit, axis):
    size = lax.axis_size(axis)
    return lax.ppermute(block, axis, [(i, i ^ bit) for i in range(size)])


def bits_of(size):
    return [1 << k for k in range(size.bit_length() - 1)]


def step_order(bits):
    order = [0]
    for bit in reversed(bits):
        order = [r | bit for r in order] + order
    return order


class Exchange:
    def __init__(self, far, near, bits):
        self.moved = [hop(far, bits[0], "expert")]
        self.near, self.rest = near, bits[1:]
        self.left = [list(range(len(self.rest))) for _ in range(2)]
        self.sides = None

    def wait(self, behind):
        if self.sides is None:
            moved = after(self.moved, *behind) if behind else self.moved
            rows, width = self.near.shape[0] >> len(self.rest), self.near.shape[1]
            near, moved = self.near.reshape(-1, rows, width), moved[0].reshape(-1, rows, width)
            spots = itertools.product(range(2), repeat=len(self.rest))
            index = {spot: i for i, spot in enumerate(spots)}
            self.sides = []
            for part in (slice(0, rows // 2), slice(rows // 2, None)):
                self.sides.append({spot: [near[i, part], moved[i, part]] for spot, i in index.items()})
        else:
            for number, (side, got) in enumerate(zip(self.sides, self.got)):
                got = after(got, *behind) if behind else got
                self.sides[number] = {spot: [*parts, got[i]] for i, (spot, parts) in enumerate(side.items())}

    def send(self, *behind):
        self.wait(behind)
        sent, self.got = [], []
        add = lambda parts: sum(p.astype(f32) for p in parts).astype(bf16)
        for number, side in enumerate(self.sides):
            at = len(self.left[number]) - 1 if number else 0
            bit = self.rest[self.left[number].pop(at)]
            spots = sorted({spot[:at] + spot[at + 1 :] for spot in side})
            block = jnp.stack([add(side[spot[:at] + (0,) + spot[at:]]) for spot in spots])
            self.got.append(hop(block, bit, "expert"))
            sent.append(block)
            self.sides[number] = {spot: side[spot[:at] + (1,) + spot[at:]] for spot in spots}
        return sent

    def total(self, *behind):
        while any(self.left):
            self.send()
        self.wait(behind)
        parts = [sum(p.astype(f32) for p in side[()]).astype(bf16) for side in self.sides]
        return jnp.concatenate(parts, axis=0)


def neighbours():
    size = lax.axis_size("tensor")
    up = lambda v: lax.ppermute(v, "tensor", [(i, (i + 1) % size) for i in range(size)])
    down = lambda v: lax.ppermute(v, "tensor", [(i, (i - 1) % size) for i in range(size)])
    return up, down


def gather_line(block, behind=()):
    size, me = lax.axis_size("tensor"), lax.axis_index("tensor")
    if size != 4:
        return lax.all_gather(block, "tensor", axis=0, tiled=True)
    rows = block.shape[0]
    cut = rows // 2
    up, down = neighbours()
    low, high = up(block), down(block)
    if behind:
        low, high = after((low, high), *behind)
    far_low, far_high = up(low[:cut]), down(high[cut:])
    whole = after(jnp.zeros((rows * size, block.shape[1]), block.dtype), low)
    for part, member, shift in ((block, 0, 0), (low, 3, 0), (high, 1, 0), (far_low, 2, 0), (far_high, 2, cut)):
        at = lax.rem(me + member, size) * rows + shift
        whole = lax.dynamic_update_slice(whole, part, (at, 0))
    return whole


class Line:
    def __init__(self, part):
        self.size, self.me = lax.axis_size("tensor"), lax.axis_index("tensor")
        self.part, self.rows = part, part.shape[0] // self.size
        self.got = None

    def of(self, member, start, end):
        at = lax.rem(self.me + member, self.size) * self.rows
        return lax.dynamic_slice_in_dim(self.part, at + start, end - start, 0)

    def send(self, *behind):
        cut, rows = self.rows // 2, self.rows
        if self.size != 4:
            return []
        if behind:
            self.got = after(self.got, *behind)
        if self.got is None:
            low, high = self.of(2, cut, rows), self.of(2, 0, cut)
        else:
            from_low, from_high = (part.astype(f32) for part in self.got)
            low = jnp.concatenate([self.of(1, 0, cut), (self.of(1, cut, rows).astype(f32) + from_low).astype(bf16)])
            high = jnp.concatenate([(self.of(3, 0, cut).astype(f32) + from_high).astype(bf16), self.of(3, cut, rows)])
        up, down = neighbours()
        self.got = up(low), down(high)
        return [low, high]

    def total(self, *behind):
        if self.size != 4:
            return lax.psum_scatter(self.part, "tensor", scatter_dimension=0, tiled=True).astype(f32)
        low, high = after(self.got, *behind) if behind else self.got
        return self.of(0, 0, self.rows).astype(f32) + low.astype(f32) + high.astype(f32)


def local(
    hidden_in,
    attn_gain,
    query_gain,
    key_gain,
    w_qkv,
    w_out,
    moe_gain,
    w_router,
    w_gate,
    w_up,
    w_down,
    routes,
    pair_rank,
    out_grad,
):
    tok_dev, width = hidden_in.shape
    n_tensor = lax.axis_size("tensor")
    n_expert = lax.axis_size("expert")
    member = lax.axis_index("tensor")
    place = lax.axis_index("expert")
    group = tok_dev * n_tensor
    local_experts = w_gate.shape[0]
    quarter = w_gate.shape[2]
    n_experts = local_experts * n_expert
    hidden_loc = local_experts * quarter
    capacity = 9 * group * TOPK // (8 * n_experts)
    local_q = w_out.shape[0] // HD
    local_kv = (w_qkv.shape[1] // HD - local_q) // 2
    both = ("expert", "tensor")
    bits = bits_of(n_expert)
    chunks = 2 * max(n_expert // 8, 1)
    piece = tok_dev // chunks
    first = 16 * (tok_dev * 9 // 256) if chunks == 2 else piece
    lanes = 8 * (-(-local_experts // 8))

    gate_w = w_gate.transpose(1, 0, 2).reshape(width, hidden_loc)
    up_w = w_up.transpose(1, 0, 2).reshape(width, hidden_loc)
    down_w = w_down.reshape(hidden_loc, width)
    spread = (jnp.arange(hidden_loc)[None, :] // quarter == jnp.arange(lanes)[:, None]).astype(bf16)

    hidden_f = hidden_in.astype(f32)
    attn_normed, attn_pull = jax.vjp(row_norm, hidden_f, attn_gain.astype(f32))
    gathered = gather_line(attn_normed.astype(bf16))
    given = after(out_grad, gathered)

    cosine, sine = rope_tables(group)
    q_gain, k_gain = query_gain.astype(f32)[None, :], key_gain.astype(f32)[None, :]
    if chunks == 2:
        gathered = after(gathered, gate_w, up_w)
    raw, queries, keys, values = project(gathered, w_qkv, q_gain, k_gain, cosine, sine, local_q, local_kv)
    mixed_all = attend(queries, keys, values.T, local_q, local_kv)
    attn = mixed_all
    if chunks == 2:
        line_1 = gather_line(given[first:], (queries,))
        line_0 = gather_line(after(given[:first], queries), (mixed_all,))
        grad_line = [line_0, line_1]
        all_1 = lax.all_gather(line_1, "expert", axis=0, tiled=True)
        all_0 = lax.all_gather(line_0, "expert", axis=0, tiled=True)
        grad_all = [all_0, all_1]
        pre = [dot(part, down_w, NT).reshape(n_expert, n_tensor, 1, -1, hidden_loc) for part in grad_all]
        attn = after(attn, *grad_line)
    attn = Line(dot(attn, w_out).astype(bf16))
    attn.send()
    attn.send()
    attn = attn.total()
    middle = hidden_f + attn
    moe_normed, moe_pull = jax.vjp(row_norm, middle, moe_gain.astype(f32))
    moe_in = moe_normed.astype(bf16)

    expert_ids = jnp.arange(n_experts, dtype=jnp.int32)
    hits = routes.T[None, :, :] == expert_ids[:, None, None]
    ranks = jnp.where(hits, pair_rank[0].reshape(group, TOPK).T[None, :, :] + 1, 0).sum(axis=1)
    ranks = jnp.where(ranks == 0, group * TOPK + 1, ranks)
    own_ranks = lax.dynamic_slice_in_dim(ranks, member * tok_dev, tok_dev, 1)
    before = (ranks[:, :, None] < own_ranks[:, None, :]).astype(f32).sum(axis=1)
    routed = own_ranks <= group * TOPK
    keep = routed & (before < capacity)

    logits = dot(w_router, moe_in, ((0,), (1,)))
    gates = jax.nn.softmax(jnp.where(routed, logits, -jnp.inf), axis=0)
    sent_gates = jnp.where(keep, gates, 0.0).astype(bf16).astype(f32)
    gates_in = jnp.broadcast_to(
        sent_gates.reshape(n_expert, 1, local_experts, tok_dev), (n_expert, n_tensor, local_experts, tok_dev)
    )
    gates_in = lax.all_to_all(gates_in.reshape(-1, local_experts, tok_dev), both, 0, 0, tiled=True)
    gates_in = gates_in.reshape(n_expert, n_tensor, local_experts, tok_dev).transpose(0, 1, 3, 2)
    gates_in = jnp.pad(gates_in, ((0, 0), (0, 0), (0, 0), (0, lanes - local_experts))).astype(bf16)

    def gates_of(start, count):
        return lax.dynamic_slice_in_dim(gates_in, start, count, 2).reshape(-1, lanes)

    order = place ^ jnp.array(step_order(bits), jnp.int32)

    def own_rows(part):
        return lax.psum_scatter(part, "tensor", scatter_dimension=0, tiled=True)

    def to_tokens(scores):
        scores = [s[:, :local_experts].reshape(n_expert, local_experts, n_tensor, -1) for s in scores]
        scores = jnp.concatenate(scores, axis=3).transpose(0, 2, 1, 3)
        scores = lax.all_to_all(scores.reshape(-1, local_experts, tok_dev), both, 0, 0, tiled=True)
        scores = scores.reshape(n_expert, n_tensor, local_experts, tok_dev).sum(axis=1)
        return jnp.where(keep, scores.reshape(n_experts, tok_dev), 0.0)

    if chunks == 2:
        moe_line = [gather_line(moe_in[:first], (pre[1],)), gather_line(moe_in[first:])]
        gates_0, gates_1 = gates_of(0, first), gates_of(first, tok_dev - first)
        moe_line[0] = after(moe_line[0], grad_all[0])
        moe_all = [lax.all_gather(part, "expert", axis=0, tiled=True) for part in moe_line]
        front, rear = order[: n_expert // 2], order[n_expert // 2 :]
        fixed = (spread, gate_w, up_w)
        x_0 = moe_all[0]
        *kept_0, back_0 = experts(jnp.arange(n_expert, dtype=jnp.int32), 0, x_0, pre[0], gates_0, *fixed)
        back_0 = lax.psum_scatter(back_0, "expert", scatter_dimension=0, tiled=True)
        far_0 = outputs(front, 0, kept_0[0], down_w)
        x_1 = after(moe_all[1], far_0)
        *kept_1, far, near = experts(order, 0, x_1, pre[1], gates_1, *fixed, halves=True)
        back_1 = Exchange(far, near, bits)
        x_0 = after(moe_all[0], kept_1[3])
        gate_grad = dot(x_0, kept_0[1], TN)
        scores = to_tokens([kept_0[3], kept_1[3]])
        sent = back_1.send(gate_grad, scores)
        hidden_0, hidden_1 = after((kept_0[0], kept_1[0]), *sent)
        far_1, near_1 = (outputs(part, 0, hidden_1, down_w) for part in (front, rear))
        back_0 = after(back_0, far_1, near_1)
        back_own = [own_rows(back_0)]
        sent = back_1.send(far_1, near_1)
        near_flops = 2 * 2 * n_expert // 2 * n_tensor * first * width * hidden_loc
        near_0 = outputs(rear, 0, after(hidden_0, *sent), down_w, near_flops)
        out_0, out_1 = Exchange(far_0, near_0, bits), Exchange(far_1, near_1, bits)
        sent = out_0.send(*sent)
        back_1 = back_1.total(*sent, back_own[0])
        back_own.append(own_rows(back_1))
        x_1, g_0 = after((moe_all[1], grad_all[0]), back_1)
        gate_grad = gate_grad + dot(x_1, kept_1[1], TN)
        down_grad = dot(kept_0[0].reshape(-1, hidden_loc), g_0, TN)
        sent = out_0.send(gate_grad, down_grad)
        back_own = after(back_own, *sent)
    else:
        def one_chunk(sums, c):
            x_c = lax.all_gather(lax.dynamic_slice_in_dim(moe_in, c * piece, piece, 0), both, axis=0, tiled=True)
            g_c = lax.all_gather(lax.dynamic_slice_in_dim(given, c * piece, piece, 0), both, axis=0, tiled=True)
            gates_c = gates_of(c * piece, piece)
            pre = dot(g_c, down_w, NT).reshape(n_expert, n_tensor, 1, piece, hidden_loc)
            given_c = (0, x_c, pre, gates_c, spread, gate_w, up_w)
            *kept, far = experts(order[: n_expert // 2], *given_c)
            *kept, near = experts(order[n_expert // 2 :], *given_c, list(enumerate(kept)))
            hw, gate_back, up_back, score = kept
            parts = (dot(hw.reshape(-1, hidden_loc), g_c, TN), dot(x_c, gate_back, TN), dot(x_c, up_back, TN))
            sums = tuple(a + b for a, b in zip(sums, parts))
            back = own_rows(Exchange(far, near, bits).total())
            out = [outputs(part, 0, hw, down_w) for part in (order[: n_expert // 2], order[n_expert // 2 :])]
            out = own_rows(Exchange(*out, bits).total())
            return sums, (back, score, out)

        zeros = (
            jnp.zeros((hidden_loc, width), f32),
            jnp.zeros((width, hidden_loc), f32),
            jnp.zeros((width, hidden_loc), f32),
        )
        grads, (back_own, scores, out_own) = lax.scan(one_chunk, zeros, jnp.arange(chunks))
        scores = to_tokens(scores)
        moe_out = jnp.concatenate(list(out_own), axis=0)
    moe_back = jnp.concatenate(list(back_own), axis=0).astype(f32)

    inner_gate = jnp.sum(gates * scores, axis=0, keepdims=True)
    logit_grad = (gates * (scores - inner_gate)).astype(bf16)
    router_grad = dot(logit_grad, moe_in)
    moe_in_grad = moe_back + dot(logit_grad, w_router, ((0,), (1,)))
    middle_part, moe_gain_grad = moe_pull(moe_in_grad)
    middle_grad = out_grad.astype(f32) + middle_part

    middle_all = lax.all_gather(middle_grad.astype(bf16), "tensor", axis=0, tiled=True)
    if chunks == 2:
        sent = out_1.send(middle_grad)
        x_0, x_1, g_1 = after((moe_all[0], moe_all[1], grad_all[1]), *sent)
        up_grad = dot(x_0, kept_0[2], TN) + dot(x_1, kept_1[2], TN)
        out_0 = out_0.total(up_grad)
        down_grad = down_grad + dot(kept_1[0].reshape(-1, hidden_loc), after(g_1, out_0), TN)
        sent = out_1.send(down_grad)
        middle_all = after(middle_all, *sent)
    mixed_grad = dot(middle_all, w_out, NT).astype(bf16)
    if chunks == 2:
        out_1 = out_1.total(mixed_grad)
        mixed_grad = after(mixed_grad, out_1)
    dq, dk, dv, query_gain_grad, key_gain_grad = attend_back(
        queries, mixed_grad, raw, keys, keys.T, values, q_gain, k_gain, cosine, sine, local_q, local_kv
    )
    qkv_grad = jnp.concatenate([dq, dk, dv], axis=1)
    if chunks == 2:
        out_own = [own_rows(part) for part in (out_0, out_1)]
        qkv_grad = after(qkv_grad, out_own[0])
        moe_out = jnp.concatenate(out_own, axis=0)
    normed_part = dot(qkv_grad, w_qkv, NT)
    normed_low = normed_part.astype(bf16)
    normed_line = Line(normed_low)
    sent = normed_line.send()
    out_weight_grad = dot(middle_all, after(mixed_all, *sent), TN).astype(bf16)
    grad_out = lax.psum_scatter(out_weight_grad, "expert", scatter_dimension=0, tiled=True)
    weight_grad = dot(after(gathered, *sent), qkv_grad, TN).astype(bf16)
    attn_gain_grad = jnp.sum(normed_part * gathered.astype(f32), axis=0) / attn_gain.astype(f32)
    gain_rows = [attn_gain_grad[None, :], moe_gain_grad[None, :]]
    gain_rows += [jnp.pad(part, ((0, 0), (0, width - HD))) for part in (query_gain_grad, key_gain_grad)]
    small = jnp.concatenate([router_grad, *gain_rows], axis=0)
    small = jnp.pad(small, ((0, -small.shape[0] % n_expert), (0, 0))).reshape(n_expert, -1, width)
    small = lax.all_to_all(small, "expert", 0, 0, tiled=True).sum(axis=0)
    small = jnp.broadcast_to(small[None], (n_tensor, *small.shape))
    small = lax.all_to_all(small, "tensor", 0, 0, tiled=True).sum(axis=0)
    blocks = weight_grad.reshape(n_expert, -1, weight_grad.shape[1])
    blocks = [lax.dynamic_index_in_dim(blocks, place ^ r, 0, keepdims=False) for r in step_order(bits)]
    far, near = (
        jnp.concatenate(part, axis=0) for part in (blocks[: n_expert // 2], blocks[n_expert // 2 :])
    )
    grad_qkv = Exchange(far, near, bits)
    sent = normed_line.send(small, far, near)
    small = after(small, *sent) if sent else small
    small = lax.all_to_all(jnp.broadcast_to(small[None], (n_expert, *small.shape)), "expert", 0, 0, tiled=True)
    small = small.reshape(-1, width)
    sent = sum([grad_qkv.send(*sent) for _ in bits[1:]], [])
    grad_qkv = grad_qkv.total().astype(f32)
    normed_grad = normed_line.total(*sent)
    layer_out = (middle + moe_out.astype(f32)).astype(bf16)
    if chunks == 2:
        grads = [down_grad, gate_grad, up_grad]
    grad_down = grads[0].reshape(local_experts, quarter, width)
    grad_gate, grad_up = (
        part.reshape(width, local_experts, quarter).transpose(1, 0, 2) for part in grads[1:]
    )
    hidden_part, _ = attn_pull(normed_grad)
    input_grad = middle_grad + hidden_part
    return (
        layer_out,
        input_grad,
        small[n_experts],
        small[n_experts + 2, :HD],
        small[n_experts + 3, :HD],
        grad_qkv,
        grad_out.astype(f32).T,
        small[n_experts + 1],
        small[:n_experts].T,
        grad_gate,
        grad_up,
        grad_down,
    )


def solution(mesh):
    in_specs = (
        P(("expert", "tensor"), None),
        P(),
        P(),
        P(),
        P(None, "tensor"),
        P("tensor", None),
        P(),
        P(),
        P("expert", None, "tensor"),
        P("expert", None, "tensor"),
        P("expert", "tensor", None),
        P("expert", None),
        P("expert", None),
        P(("expert", "tensor"), None),
    )
    out_specs = (
        P(("expert", "tensor"), None),
        P(("expert", "tensor"), None),
        P(),
        P(),
        P(),
        P("expert", "tensor"),
        P("tensor", "expert"),
        P(),
        P(),
        P("expert", None, "tensor"),
        P("expert", None, "tensor"),
        P("expert", "tensor", None),
    )
    return jax.shard_map(local, mesh=mesh, in_specs=in_specs, out_specs=out_specs, check_vma=False)
```

```python
import functools
import itertools
import jax
import jax.numpy as jnp
from jax import lax
from jax.experimental import pallas as pl
from jax.experimental.pallas import tpu as pltpu
from jax.sharding import PartitionSpec as P

HD = 128
ATT_BLOCK = 256
norm_eps = 1e-06
rope_base = 1000000.0
bf16 = jnp.bfloat16
f32 = jnp.float32
MIB = 1 << 20


def dot(a, b, contract=((1,), (0,))):
    return lax.dot_general(a, b, (contract, ((), ())), preferred_element_type=f32)


NT = ((1,), (1,))
TN = ((0,), (0,))


def rope_tables(length):
    half = HD // 2
    freqs = jnp.power(rope_base, -(jnp.arange(half).astype(f32) * (2.0 / HD)))
    angles = jnp.arange(length).astype(f32)[:, None] * freqs[None, :]
    cosine, sine = jnp.cos(angles), jnp.sin(angles)
    return jnp.concatenate([cosine, cosine], axis=1), jnp.concatenate([-sine, sine], axis=1)


def project_kernel(local_q, local_kv, x_ref, w_ref, qg_ref, kg_ref, cos_ref, sin_ref, raw_ref, q_ref, k_ref, v_ref):
    raw = dot(x_ref[...], w_ref[...])
    cosine, sine = cos_ref[...], sin_ref[...]
    raw_ref[...] = raw[:, : (local_q + local_kv) * HD]
    for h in range(local_q + local_kv):
        head = raw[:, h * HD : (h + 1) * HD]
        gain = qg_ref[...] if h < local_q else kg_ref[...]
        normed = head * lax.rsqrt(jnp.mean(head * head, axis=1, keepdims=True) + norm_eps) * gain
        turned = (normed * cosine + pltpu.roll(normed, HD // 2, 1) * sine).astype(bf16)
        if h < local_q:
            q_ref[:, h * HD : (h + 1) * HD] = turned
        else:
            k_ref[:, (h - local_q) * HD : (h - local_q + 1) * HD] = turned
    v_ref[...] = raw[:, (local_q + local_kv) * HD :].astype(bf16)


def project(x, w, q_gain, k_gain, cosine, sine, local_q, local_kv):
    rows, width = x.shape
    tile = 256
    cols = w.shape[1]
    full = lambda shape: pl.BlockSpec(shape, lambda i: (0,) * len(shape))
    row = lambda n: pl.BlockSpec((tile, n), lambda i: (i, 0))
    heads = local_q + local_kv
    return pl.pallas_call(
        functools.partial(project_kernel, local_q, local_kv),
        grid=(rows // tile,),
        in_specs=[row(width), full((width, cols)), full((1, HD)), full((1, HD)), row(HD), row(HD)],
        out_specs=[row(heads * HD), row(local_q * HD), row(local_kv * HD), row(local_kv * HD)],
        out_shape=[
            jax.ShapeDtypeStruct((rows, heads * HD), f32),
            jax.ShapeDtypeStruct((rows, local_q * HD), bf16),
            jax.ShapeDtypeStruct((rows, local_kv * HD), bf16),
            jax.ShapeDtypeStruct((rows, local_kv * HD), bf16),
        ],
        compiler_params=pltpu.CompilerParams(vmem_limit_bytes=40 * MIB),
        cost_estimate=pl.CostEstimate(flops=2 * rows * width * cols, bytes_accessed=rows * width * 2 + width * cols * 2 + rows * cols * 6, transcendentals=0),
        name="project",
    )(x, w, q_gain, k_gain, cosine, sine)


def attend_kernel(scale, q_ref, k_ref, vt_ref, o_ref):
    for b in range(q_ref.shape[0] // ATT_BLOCK):
        n = (b + 1) * ATT_BLOCK
        at = slice(b * ATT_BLOCK, n)
        weight = jnp.exp(dot(k_ref[:n, :], q_ref[at, :], NT) * scale)
        total = jnp.sum(weight, axis=0, keepdims=True)
        mixed = dot(vt_ref[:, :n], weight.astype(bf16)) * (1.0 / total)
        o_ref[at, :] = mixed.T.astype(bf16)


def attend(q, k, v_t, local_q, local_kv):
    rows = q.shape[0]
    repeat = local_q // local_kv
    return pl.pallas_call(
        functools.partial(attend_kernel, HD**-0.5),
        grid=(local_q,),
        in_specs=[
            pl.BlockSpec((rows, HD), lambda h: (0, h)),
            pl.BlockSpec((rows, HD), lambda h: (0, h // repeat)),
            pl.BlockSpec((HD, rows), lambda h: (h // repeat, 0)),
        ],
        out_specs=pl.BlockSpec((rows, HD), lambda h: (0, h)),
        out_shape=jax.ShapeDtypeStruct((rows, local_q * HD), bf16),
        compiler_params=pltpu.CompilerParams(vmem_limit_bytes=32 * MIB),
        cost_estimate=pl.CostEstimate(flops=local_q * rows * rows * HD * 3, bytes_accessed=rows * local_q * HD * 4, transcendentals=local_q * rows * rows),
        name="attend",
    )(q, k, v_t)


def unturn(grad, raw, gain, cosine, sine):
    grad = grad * cosine - pltpu.roll(grad, HD // 2, 1) * sine
    inv = lax.rsqrt(jnp.mean(raw * raw, axis=1, keepdims=True) + norm_eps)
    part = gain * grad
    back = inv * part - raw * (inv * inv * inv) * jnp.mean(raw * part, axis=1, keepdims=True)
    return back, jnp.sum(grad * raw * inv, axis=0, keepdims=True)


def attend_back_kernel(
    scale, repeat, q_ref, do_ref, raw_ref, k_ref, kt_ref, v_ref, rawk_ref, qg_ref, kg_ref, cos_ref, sin_ref,
    dq_ref, dk_ref, dv_ref, dqg_ref, dkg_ref, dqs, dks, dvs,
):
    h = pl.program_id(0)

    @pl.when(h == 0)
    def _():
        dqg_ref[...] = jnp.zeros_like(dqg_ref)
        dkg_ref[...] = jnp.zeros_like(dkg_ref)

    @pl.when(lax.rem(h, repeat) == 0)
    def _():
        dks[...] = jnp.zeros_like(dks)
        dvs[...] = jnp.zeros_like(dvs)

    for b in range(q_ref.shape[0] // ATT_BLOCK):
        n = (b + 1) * ATT_BLOCK
        at = slice(b * ATT_BLOCK, n)
        query, given = q_ref[at, :], do_ref[at, :]
        weight = jnp.exp(dot(k_ref[:n, :], query, NT) * scale)
        prob = weight * (1.0 / jnp.sum(weight, axis=0, keepdims=True))
        prob_grad = dot(v_ref[:n, :], given, NT)
        inner = jnp.sum(prob * prob_grad, axis=0, keepdims=True)
        score_grad = (prob * (prob_grad - inner)).astype(bf16)
        dks[:n, :] += dot(score_grad, query)
        dvs[:n, :] += dot(prob.astype(bf16), given)
        dqs[at, :] = dot(kt_ref[:, :n], score_grad).T * scale
    back, gain_part = unturn(dqs[...], raw_ref[...], qg_ref[...], cos_ref[...], sin_ref[...])
    dq_ref[...] = back.astype(bf16)
    dqg_ref[...] += gain_part

    @pl.when(lax.rem(h, repeat) == repeat - 1)
    def _():
        back_k, gain_k = unturn(dks[...] * scale, rawk_ref[...], kg_ref[...], cos_ref[...], sin_ref[...])
        dk_ref[...] = back_k.astype(bf16)
        dv_ref[...] = dvs[...].astype(bf16)
        dkg_ref[...] += gain_k


def attend_back(q, given, raw, k, k_t, v, q_gain, k_gain, cosine, sine, local_q, local_kv):
    rows = q.shape[0]
    repeat = local_q // local_kv
    head = pl.BlockSpec((rows, HD), lambda h: (0, h))
    shared = pl.BlockSpec((rows, HD), lambda h: (0, h // repeat))
    whole = pl.BlockSpec((rows, HD), lambda h: (0, 0))
    gain = pl.BlockSpec((1, HD), lambda h: (0, 0))
    return pl.pallas_call(
        functools.partial(attend_back_kernel, HD**-0.5, repeat),
        grid=(local_q,),
        in_specs=[
            head, head, head, shared, pl.BlockSpec((HD, rows), lambda h: (h // repeat, 0)), shared,
            pl.BlockSpec((rows, HD), lambda h: (0, local_q + h // repeat)), gain, gain, whole, whole,
        ],
        out_specs=[head, shared, shared, gain, gain],
        out_shape=[
            jax.ShapeDtypeStruct((rows, local_q * HD), bf16),
            jax.ShapeDtypeStruct((rows, local_kv * HD), bf16),
            jax.ShapeDtypeStruct((rows, local_kv * HD), bf16),
            jax.ShapeDtypeStruct((1, HD), f32),
            jax.ShapeDtypeStruct((1, HD), f32),
        ],
        scratch_shapes=[pltpu.VMEM((rows, HD), f32)] * 3,
        compiler_params=pltpu.CompilerParams(vmem_limit_bytes=40 * MIB),
        cost_estimate=pl.CostEstimate(flops=local_q * rows * rows * HD * 7, bytes_accessed=rows * local_q * HD * 10, transcendentals=local_q * rows * rows),
        name="attend_back",
    )(q, given, raw, k, k_t, v, raw, q_gain, k_gain, cosine, sine)


def experts_kernel(
    held, order, x_ref, pre_ref, gate_ref, spread_ref, wg_ref, wu_ref, *refs
):
    hw_ref, gb_ref, ub_ref, score_ref, *back_refs = refs[held:]
    x = x_ref[...]
    gate_pre = dot(x, wg_ref[...])
    sigma = 1.0 / (1.0 + jnp.exp(-gate_pre))
    active = gate_pre * sigma
    up_pre = dot(x, wu_ref[...])
    pre = pre_ref[...].reshape(gate_pre.shape)
    hidden = active * up_pre
    score_ref[...] = dot(spread_ref[...], (hidden * pre).astype(bf16), NT).reshape(score_ref.shape)
    weight = dot(gate_ref[...], spread_ref[...])
    hw_ref[...] = (hidden * weight).astype(bf16).reshape(hw_ref.shape)
    hidden_grad = pre * weight
    up_back = (hidden_grad * active).astype(bf16)
    gate_back = (hidden_grad * up_pre * sigma * (1.0 + gate_pre * (1.0 - sigma))).astype(bf16)
    gb_ref[...] = gate_back
    ub_ref[...] = up_back
    back = (dot(gate_back, wg_ref[...], NT) + dot(up_back, wu_ref[...], NT)).astype(bf16)
    if len(back_refs) == 1:
        back_refs[0][...] = back
        return
    first = pl.program_id(0) < pl.num_programs(0) // 2

    @pl.when(first)
    def _():
        back_refs[0][...] = back

    @pl.when(jnp.logical_not(first))
    def _():
        back_refs[1][...] = back


def row_block(array, c):
    _, members, _, piece, columns = array.shape
    return pl.BlockSpec((1, members, 1, piece, columns), lambda j, order: (order[j], 0, c, 0, 0))


def experts(order, c, x, pre, gates, spread, gate_w, up_w, held=(), halves=False):
    rows, width = x.shape
    tile = rows // pre.shape[0]
    hidden = gate_w.shape[1]
    lanes = spread.shape[0]
    steps = order.shape[0]
    half = steps // 2
    spots = [lambda j, order: (j, 0)]
    if halves:
        spots = [lambda j, order: (jnp.minimum(j, half - 1), 0), lambda j, order: (jnp.maximum(j - half, 0), 0)]
    at = lambda n: pl.BlockSpec((tile, n), lambda j, order: (order[j], 0))
    full = lambda shape: pl.BlockSpec(shape, lambda j, order: (0, 0), pipeline_mode=pl.Buffered(1))
    return pl.pallas_call(
        functools.partial(experts_kernel, len(held)),
        grid_spec=pltpu.PrefetchScalarGridSpec(
            num_scalar_prefetch=1,
            grid=(steps,),
            in_specs=[
                at(width), row_block(pre, c), at(lanes), full((lanes, hidden)), full((width, hidden)), full((width, hidden)),
                *[pl.BlockSpec(memory_space=pl.ANY)] * len(held),
            ],
            out_specs=[
                row_block(pre, c), at(hidden), at(hidden), pl.BlockSpec((1, lanes, tile), lambda j, order: (order[j], 0, 0)),
                *[pl.BlockSpec((tile, width), spot) for spot in spots],
            ],
        ),
        out_shape=[
            jax.ShapeDtypeStruct(pre.shape, bf16),
            jax.ShapeDtypeStruct((rows, hidden), bf16),
            jax.ShapeDtypeStruct((rows, hidden), bf16),
            jax.ShapeDtypeStruct((rows // tile, lanes, tile), f32),
            *[jax.ShapeDtypeStruct((steps * tile // len(spots), width), bf16) for _ in spots],
        ],
        input_output_aliases={7 + i: output for i, (output, _) in enumerate(held)},
        compiler_params=pltpu.CompilerParams(vmem_limit_bytes=58 * MIB),
        cost_estimate=pl.CostEstimate(flops=8 * steps * tile * width * hidden, bytes_accessed=steps * tile * (width * 4 + hidden * 10), transcendentals=steps * tile * hidden),
        name="experts",
    )(order, x, pre, gates, spread, gate_w, up_w, *[array for _, array in held])


def outputs_kernel(order, h_ref, w_ref, out_ref):
    hidden = h_ref[...].reshape(out_ref.shape[0], w_ref.shape[0])
    out_ref[...] = dot(hidden, w_ref[...]).astype(bf16)


def outputs(order, c, hidden_wt, down_w, flops=1):
    _, members, _, piece, hidden = hidden_wt.shape
    steps = order.shape[0]
    tile = members * piece
    width = down_w.shape[1]
    return pl.pallas_call(
        outputs_kernel,
        grid_spec=pltpu.PrefetchScalarGridSpec(
            num_scalar_prefetch=1,
            grid=(steps,),
            in_specs=[
                row_block(hidden_wt, c),
                pl.BlockSpec((hidden, width), lambda j, order: (0, 0), pipeline_mode=pl.Buffered(1)),
            ],
            out_specs=pl.BlockSpec((tile, width), lambda j, order: (j, 0)),
        ),
        out_shape=jax.ShapeDtypeStruct((steps * tile, width), bf16),
        compiler_params=pltpu.CompilerParams(vmem_limit_bytes=32 * MIB),
        cost_estimate=pl.CostEstimate(flops=flops, bytes_accessed=1, transcendentals=0),
        name="outputs",
    )(order, hidden_wt, down_w)


def rows_product_kernel(x_ref, g_ref, out_ref):
    @pl.when(pl.program_id(0) == 0)
    def _():
        out_ref[...] = jnp.zeros_like(out_ref)

    out_ref[...] += dot(x_ref[...], g_ref[...], TN)


def rows_product(x, g):
    rows, width = x.shape
    columns = g.shape[1]
    tile = rows // 4
    return pl.pallas_call(
        rows_product_kernel,
        grid=(4,),
        in_specs=[pl.BlockSpec((tile, width), lambda j: (j, 0)), pl.BlockSpec((tile, columns), lambda j: (j, 0))],
        out_specs=pl.BlockSpec((width, columns), lambda j: (0, 0)),
        out_shape=jax.ShapeDtypeStruct((width, columns), f32),
        compiler_params=pltpu.CompilerParams(vmem_limit_bytes=52 * MIB),
        cost_estimate=pl.CostEstimate(flops=1, bytes_accessed=1, transcendentals=0),
        name="rows_product",
    )(x, g)


TOPK = 8


def row_norm(values, gain):
    return values * lax.rsqrt(jnp.mean(values * values, axis=-1, keepdims=True) + norm_eps) * gain


def after(value, *others):
    return lax.optimization_barrier((value, *others))[0]


def hop(block, bit, axis):
    size = lax.axis_size(axis)
    return lax.ppermute(block, axis, [(i, i ^ bit) for i in range(size)])


def bits_of(size):
    return [1 << k for k in range(size.bit_length() - 1)]


def step_order(bits):
    order = [0]
    for bit in reversed(bits):
        order = [r | bit for r in order] + order
    return order


class Exchange:
    def __init__(self, far, near, bits):
        self.moved = [hop(far, bits[0], "expert")]
        self.near, self.rest = near, bits[1:]
        self.left = [list(range(len(self.rest))) for _ in range(2)]
        self.sides = None

    def wait(self, behind):
        if self.sides is None:
            moved = after(self.moved, *behind) if behind else self.moved
            rows, width = self.near.shape[0] >> len(self.rest), self.near.shape[1]
            near, moved = self.near.reshape(-1, rows, width), moved[0].reshape(-1, rows, width)
            spots = itertools.product(range(2), repeat=len(self.rest))
            index = {spot: i for i, spot in enumerate(spots)}
            self.sides = []
            for part in (slice(0, rows // 2), slice(rows // 2, None)):
                self.sides.append({spot: [near[i, part], moved[i, part]] for spot, i in index.items()})
        else:
            for number, (side, got) in enumerate(zip(self.sides, self.got)):
                got = after(got, *behind) if behind else got
                self.sides[number] = {spot: [*parts, got[i]] for i, (spot, parts) in enumerate(side.items())}

    def send(self, *behind):
        self.wait(behind)
        sent, self.got = [], []
        add = lambda parts: sum(p.astype(f32) for p in parts).astype(bf16)
        for number, side in enumerate(self.sides):
            at = len(self.left[number]) - 1 if number else 0
            bit = self.rest[self.left[number].pop(at)]
            spots = sorted({spot[:at] + spot[at + 1 :] for spot in side})
            block = jnp.stack([add(side[spot[:at] + (0,) + spot[at:]]) for spot in spots])
            self.got.append(hop(block, bit, "expert"))
            sent.append(block)
            self.sides[number] = {spot: side[spot[:at] + (1,) + spot[at:]] for spot in spots}
        return sent

    def total(self, *behind):
        while any(self.left):
            self.send()
        self.wait(behind)
        parts = [sum(p.astype(f32) for p in side[()]).astype(bf16) for side in self.sides]
        return jnp.concatenate(parts, axis=0)


def neighbours():
    size = lax.axis_size("tensor")
    up = lambda v: lax.ppermute(v, "tensor", [(i, (i + 1) % size) for i in range(size)])
    down = lambda v: lax.ppermute(v, "tensor", [(i, (i - 1) % size) for i in range(size)])
    return up, down


def gather_line(block, behind=()):
    size, me = lax.axis_size("tensor"), lax.axis_index("tensor")
    if size != 4:
        return lax.all_gather(block, "tensor", axis=0, tiled=True)
    rows = block.shape[0]
    cut = rows // 2
    up, down = neighbours()
    low, high = up(block), down(block)
    if behind:
        low, high = after((low, high), *behind)
    far_low, far_high = up(low[:cut]), down(high[cut:])
    whole = after(jnp.zeros((rows * size, block.shape[1]), block.dtype), low)
    for part, member, shift in ((block, 0, 0), (low, 3, 0), (high, 1, 0), (far_low, 2, 0), (far_high, 2, cut)):
        at = lax.rem(me + member, size) * rows + shift
        whole = lax.dynamic_update_slice(whole, part, (at, 0))
    return whole


class Line:
    def __init__(self, part):
        self.size, self.me = lax.axis_size("tensor"), lax.axis_index("tensor")
        self.part, self.rows = part, part.shape[0] // self.size
        self.got = None

    def of(self, member, start, end):
        at = lax.rem(self.me + member, self.size) * self.rows
        return lax.dynamic_slice_in_dim(self.part, at + start, end - start, 0)

    def send(self, *behind):
        cut, rows = self.rows // 2, self.rows
        if self.size != 4:
            return []
        if behind:
            self.got = after(self.got, *behind)
        if self.got is None:
            low, high = self.of(2, cut, rows), self.of(2, 0, cut)
        else:
            from_low, from_high = (part.astype(f32) for part in self.got)
            low = jnp.concatenate([self.of(1, 0, cut), (self.of(1, cut, rows).astype(f32) + from_low).astype(bf16)])
            high = jnp.concatenate([(self.of(3, 0, cut).astype(f32) + from_high).astype(bf16), self.of(3, cut, rows)])
        up, down = neighbours()
        self.got = up(low), down(high)
        return [low, high]

    def total(self, *behind):
        if self.size != 4:
            return lax.psum_scatter(self.part, "tensor", scatter_dimension=0, tiled=True).astype(f32)
        low, high = after(self.got, *behind) if behind else self.got
        return self.of(0, 0, self.rows).astype(f32) + low.astype(f32) + high.astype(f32)


def local(
    hidden_in,
    attn_gain,
    query_gain,
    key_gain,
    w_qkv,
    w_out,
    moe_gain,
    w_router,
    w_gate,
    w_up,
    w_down,
    routes,
    pair_rank,
    out_grad,
):
    tok_dev, width = hidden_in.shape
    n_tensor = lax.axis_size("tensor")
    n_expert = lax.axis_size("expert")
    member = lax.axis_index("tensor")
    place = lax.axis_index("expert")
    group = tok_dev * n_tensor
    local_experts = w_gate.shape[0]
    quarter = w_gate.shape[2]
    n_experts = local_experts * n_expert
    hidden_loc = local_experts * quarter
    capacity = 9 * group * TOPK // (8 * n_experts)
    local_q = w_out.shape[0] // HD
    local_kv = (w_qkv.shape[1] // HD - local_q) // 2
    both = ("expert", "tensor")
    bits = bits_of(n_expert)
    chunks = 2 * max(n_expert // 8, 1)
    piece = tok_dev // chunks
    first = 16 * (tok_dev * 9 // 256) if chunks == 2 else piece
    lanes = 8 * (-(-local_experts // 8))

    gate_w = w_gate.transpose(1, 0, 2).reshape(width, hidden_loc)
    up_w = w_up.transpose(1, 0, 2).reshape(width, hidden_loc)
    down_w = w_down.reshape(hidden_loc, width)
    spread = (jnp.arange(hidden_loc)[None, :] // quarter == jnp.arange(lanes)[:, None]).astype(bf16)

    hidden_f = hidden_in.astype(f32)
    attn_normed, attn_pull = jax.vjp(row_norm, hidden_f, attn_gain.astype(f32))
    gathered = gather_line(attn_normed.astype(bf16))
    given = after(out_grad, gathered)

    cosine, sine = rope_tables(group)
    q_gain, k_gain = query_gain.astype(f32)[None, :], key_gain.astype(f32)[None, :]
    if chunks == 2:
        gathered = after(gathered, gate_w, up_w)
    raw, queries, keys, values = project(gathered, w_qkv, q_gain, k_gain, cosine, sine, local_q, local_kv)
    mixed_all = attend(queries, keys, values.T, local_q, local_kv)
    attn = mixed_all
    if chunks == 2:
        line_1 = gather_line(given[first:], (queries,))
        line_0 = gather_line(after(given[:first], queries), (mixed_all,))
        grad_line = [line_0, line_1]
        all_1 = lax.all_gather(line_1, "expert", axis=0, tiled=True)
        all_0 = lax.all_gather(line_0, "expert", axis=0, tiled=True)
        grad_all = [all_0, all_1]
        pre = [dot(part, down_w, NT).reshape(n_expert, n_tensor, 1, -1, hidden_loc) for part in grad_all]
        attn = after(attn, *grad_line)
    attn = Line(dot(attn, w_out).astype(bf16))
    attn.send()
    attn.send()
    attn = attn.total()
    middle = hidden_f + attn
    moe_normed, moe_pull = jax.vjp(row_norm, middle, moe_gain.astype(f32))
    moe_in = moe_normed.astype(bf16)

    expert_ids = jnp.arange(n_experts, dtype=jnp.int32)
    hits = routes.T[None, :, :] == expert_ids[:, None, None]
    ranks = jnp.where(hits, pair_rank[0].reshape(group, TOPK).T[None, :, :] + 1, 0).sum(axis=1)
    ranks = jnp.where(ranks == 0, group * TOPK + 1, ranks)
    own_ranks = lax.dynamic_slice_in_dim(ranks, member * tok_dev, tok_dev, 1)
    before = (ranks[:, :, None] < own_ranks[:, None, :]).astype(f32).sum(axis=1)
    routed = own_ranks <= group * TOPK
    keep = routed & (before < capacity)

    logits = dot(w_router, moe_in, ((0,), (1,)))
    gates = jax.nn.softmax(jnp.where(routed, logits, -jnp.inf), axis=0)
    sent_gates = jnp.where(keep, gates, 0.0).astype(bf16).astype(f32)
    gates_in = jnp.broadcast_to(
        sent_gates.reshape(n_expert, 1, local_experts, tok_dev), (n_expert, n_tensor, local_experts, tok_dev)
    )
    gates_in = lax.all_to_all(gates_in.reshape(-1, local_experts, tok_dev), both, 0, 0, tiled=True)
    gates_in = gates_in.reshape(n_expert, n_tensor, local_experts, tok_dev).transpose(0, 1, 3, 2)
    gates_in = jnp.pad(gates_in, ((0, 0), (0, 0), (0, 0), (0, lanes - local_experts))).astype(bf16)

    def gates_of(start, count):
        return lax.dynamic_slice_in_dim(gates_in, start, count, 2).reshape(-1, lanes)

    order = place ^ jnp.array(step_order(bits), jnp.int32)

    def own_rows(part):
        return lax.psum_scatter(part, "tensor", scatter_dimension=0, tiled=True)

    def to_tokens(scores):
        scores = [s[:, :local_experts].reshape(n_expert, local_experts, n_tensor, -1) for s in scores]
        scores = jnp.concatenate(scores, axis=3).transpose(0, 2, 1, 3)
        scores = lax.all_to_all(scores.reshape(-1, local_experts, tok_dev), both, 0, 0, tiled=True)
        scores = scores.reshape(n_expert, n_tensor, local_experts, tok_dev).sum(axis=1)
        return jnp.where(keep, scores.reshape(n_experts, tok_dev), 0.0)

    if chunks == 2:
        moe_line = [gather_line(moe_in[:first], (pre[1],)), gather_line(moe_in[first:])]
        gates_0, gates_1 = gates_of(0, first), gates_of(first, tok_dev - first)
        moe_line[0] = after(moe_line[0], grad_all[0])
        moe_all = [lax.all_gather(part, "expert", axis=0, tiled=True) for part in moe_line]
        front, rear = order[: n_expert // 2], order[n_expert // 2 :]
        fixed = (spread, gate_w, up_w)
        x_0 = moe_all[0]
        *kept_0, back_0 = experts(jnp.arange(n_expert, dtype=jnp.int32), 0, x_0, pre[0], gates_0, *fixed)
        back_0 = lax.psum_scatter(back_0, "expert", scatter_dimension=0, tiled=True)
        far_0 = outputs(front, 0, kept_0[0], down_w)
        x_1 = after(moe_all[1], far_0)
        *kept_1, far, near = experts(order, 0, x_1, pre[1], gates_1, *fixed, halves=True)
        back_1 = Exchange(far, near, bits)
        scores = to_tokens([kept_0[3], kept_1[3]])
        far_1, near_1 = (outputs(part, 0, kept_1[0], down_w) for part in (front, rear))
        sent = back_1.send(far_1, near_1, scores)
        x_0, hidden_0 = after((moe_all[0], kept_0[0]), *sent)
        gate_grad = rows_product(x_0, kept_0[1])
        back_0 = after(back_0, gate_grad)
        back_own = [own_rows(back_0)]
        sent = back_1.send(gate_grad)
        near_flops = 2 * 2 * n_expert // 2 * n_tensor * first * width * hidden_loc
        near_0 = outputs(rear, 0, after(hidden_0, *sent), down_w, near_flops)
        out_0, out_1 = Exchange(far_0, near_0, bits), Exchange(far_1, near_1, bits)
        sent = out_1.send(*sent)
        back_1 = back_1.total(*sent, near_0, back_own[0])
        back_own.append(own_rows(back_1))
        x_1, g_0 = after((moe_all[1], grad_all[0]), back_1)
        gate_grad = gate_grad + dot(x_1, kept_1[1], TN)
        down_grad = dot(kept_0[0].reshape(-1, hidden_loc), g_0, TN)
        sent = out_1.send(gate_grad, down_grad)
        back_own = after(back_own, *sent)
    else:
        def one_chunk(sums, c):
            x_c = lax.all_gather(lax.dynamic_slice_in_dim(moe_in, c * piece, piece, 0), both, axis=0, tiled=True)
            g_c = lax.all_gather(lax.dynamic_slice_in_dim(given, c * piece, piece, 0), both, axis=0, tiled=True)
            gates_c = gates_of(c * piece, piece)
            pre = dot(g_c, down_w, NT).reshape(n_expert, n_tensor, 1, piece, hidden_loc)
            given_c = (0, x_c, pre, gates_c, spread, gate_w, up_w)
            *kept, far = experts(order[: n_expert // 2], *given_c)
            *kept, near = experts(order[n_expert // 2 :], *given_c, list(enumerate(kept)))
            hw, gate_back, up_back, score = kept
            parts = (dot(hw.reshape(-1, hidden_loc), g_c, TN), dot(x_c, gate_back, TN), dot(x_c, up_back, TN))
            sums = tuple(a + b for a, b in zip(sums, parts))
            back = own_rows(Exchange(far, near, bits).total())
            out = [outputs(part, 0, hw, down_w) for part in (order[: n_expert // 2], order[n_expert // 2 :])]
            out = own_rows(Exchange(*out, bits).total())
            return sums, (back, score, out)

        zeros = (
            jnp.zeros((hidden_loc, width), f32),
            jnp.zeros((width, hidden_loc), f32),
            jnp.zeros((width, hidden_loc), f32),
        )
        grads, (back_own, scores, out_own) = lax.scan(one_chunk, zeros, jnp.arange(chunks))
        scores = to_tokens(scores)
        moe_out = jnp.concatenate(list(out_own), axis=0)
    moe_back = jnp.concatenate(list(back_own), axis=0).astype(f32)

    inner_gate = jnp.sum(gates * scores, axis=0, keepdims=True)
    logit_grad = (gates * (scores - inner_gate)).astype(bf16)
    router_grad = dot(logit_grad, moe_in)
    moe_in_grad = moe_back + dot(logit_grad, w_router, ((0,), (1,)))
    middle_part, moe_gain_grad = moe_pull(moe_in_grad)
    middle_grad = out_grad.astype(f32) + middle_part

    middle_all = lax.all_gather(middle_grad.astype(bf16), "tensor", axis=0, tiled=True)
    if chunks == 2:
        sent = out_0.send(middle_grad)
        x_0, x_1, g_1 = after((moe_all[0], moe_all[1], grad_all[1]), *sent)
        up_grad = dot(x_0, kept_0[2], TN) + dot(x_1, kept_1[2], TN)
        out_1 = out_1.total(up_grad)
        down_grad = down_grad + dot(kept_1[0].reshape(-1, hidden_loc), after(g_1, out_1), TN)
        sent = out_0.send(down_grad)
        middle_all = after(middle_all, *sent)
    mixed_grad = dot(middle_all, w_out, NT).astype(bf16)
    if chunks == 2:
        out_0 = out_0.total(mixed_grad)
        mixed_grad = after(mixed_grad, out_0)
    dq, dk, dv, query_gain_grad, key_gain_grad = attend_back(
        queries, mixed_grad, raw, keys, keys.T, values, q_gain, k_gain, cosine, sine, local_q, local_kv
    )
    qkv_grad = jnp.concatenate([dq, dk, dv], axis=1)
    if chunks == 2:
        out_own = [own_rows(part) for part in (out_1, out_0)][::-1]
        qkv_grad = after(qkv_grad, out_own[1])
        moe_out = jnp.concatenate(out_own, axis=0)
    normed_part = dot(qkv_grad, w_qkv, NT)
    normed_low = normed_part.astype(bf16)
    normed_line = Line(normed_low)
    sent = normed_line.send()
    out_weight_grad = dot(middle_all, after(mixed_all, *sent), TN).astype(bf16)
    grad_out = lax.psum_scatter(out_weight_grad, "expert", scatter_dimension=0, tiled=True)
    weight_grad = dot(after(gathered, *sent), qkv_grad, TN).astype(bf16)
    attn_gain_grad = jnp.sum(normed_part * gathered.astype(f32), axis=0) / attn_gain.astype(f32)
    gain_rows = [attn_gain_grad[None, :], moe_gain_grad[None, :]]
    gain_rows += [jnp.pad(part, ((0, 0), (0, width - HD))) for part in (query_gain_grad, key_gain_grad)]
    small = jnp.concatenate([router_grad, *gain_rows], axis=0)
    small = jnp.pad(small, ((0, -small.shape[0] % n_expert), (0, 0))).reshape(n_expert, -1, width)
    small = lax.all_to_all(small, "expert", 0, 0, tiled=True).sum(axis=0)
    blocks = weight_grad.reshape(n_expert, -1, weight_grad.shape[1])
    blocks = [lax.dynamic_index_in_dim(blocks, place ^ r, 0, keepdims=False) for r in step_order(bits)]
    far, near = (
        jnp.concatenate(part, axis=0) for part in (blocks[: n_expert // 2], blocks[n_expert // 2 :])
    )
    grad_qkv = Exchange(far, near, bits)
    if chunks == 2:
        grads = [down_grad, gate_grad, up_grad]
    grad_down = grads[0].reshape(local_experts, quarter, width)
    grad_gate, grad_up = (
        part.reshape(width, local_experts, quarter).transpose(1, 0, 2) for part in grads[1:]
    )
    sent = normed_line.send(far, near, grad_gate, grad_up)
    small = after(small, *sent) if sent else small
    for bit in bits_of(n_tensor):
        small = small + hop(small, bit, "tensor")
    small = lax.all_to_all(jnp.broadcast_to(small[None], (n_expert, *small.shape)), "expert", 0, 0, tiled=True)
    small = small.reshape(-1, width)
    sent = sum([grad_qkv.send(*sent) for _ in bits[1:]], [])
    grad_qkv = grad_qkv.total().astype(f32)
    normed_grad = normed_line.total(*sent)
    layer_out = (middle + moe_out.astype(f32)).astype(bf16)
    hidden_part, _ = attn_pull(normed_grad)
    input_grad = middle_grad + hidden_part
    return (
        layer_out,
        input_grad,
        small[n_experts],
        small[n_experts + 2, :HD],
        small[n_experts + 3, :HD],
        grad_qkv,
        grad_out.astype(f32).T,
        small[n_experts + 1],
        small[:n_experts].T,
        grad_gate,
        grad_up,
        grad_down,
    )


def solution(mesh):
    in_specs = (
        P(("expert", "tensor"), None),
        P(),
        P(),
        P(),
        P(None, "tensor"),
        P("tensor", None),
        P(),
        P(),
        P("expert", None, "tensor"),
        P("expert", None, "tensor"),
        P("expert", "tensor", None),
        P("expert", None),
        P("expert", None),
        P(("expert", "tensor"), None),
    )
    out_specs = (
        P(("expert", "tensor"), None),
        P(("expert", "tensor"), None),
        P(),
        P(),
        P(),
        P("expert", "tensor"),
        P("tensor", "expert"),
        P(),
        P(),
        P("expert", None, "tensor"),
        P("expert", None, "tensor"),
        P("expert", "tensor", None),
    )
    return jax.shard_map(local, mesh=mesh, in_specs=in_specs, out_specs=out_specs, check_vma=False)
```

```python
import functools
import itertools
import jax
import jax.numpy as jnp
from jax import lax
from jax.experimental import pallas as pl
from jax.experimental.pallas import tpu as pltpu
from jax.sharding import PartitionSpec as P

HD = 128
ATT_BLOCK = 256
norm_eps = 1e-06
rope_base = 1000000.0
bf16 = jnp.bfloat16
f32 = jnp.float32
MIB = 1 << 20


def dot(a, b, contract=((1,), (0,))):
    return lax.dot_general(a, b, (contract, ((), ())), preferred_element_type=f32)


NT = ((1,), (1,))
TN = ((0,), (0,))


def rope_tables(length):
    half = HD // 2
    freqs = jnp.power(rope_base, -(jnp.arange(half).astype(f32) * (2.0 / HD)))
    angles = jnp.arange(length).astype(f32)[:, None] * freqs[None, :]
    cosine, sine = jnp.cos(angles), jnp.sin(angles)
    return jnp.concatenate([cosine, cosine], axis=1), jnp.concatenate([-sine, sine], axis=1)


def project_kernel(local_q, local_kv, x_ref, w_ref, qg_ref, kg_ref, cos_ref, sin_ref, raw_ref, q_ref, k_ref, v_ref):
    raw = dot(x_ref[...], w_ref[...])
    cosine, sine = cos_ref[...], sin_ref[...]
    raw_ref[...] = raw[:, : (local_q + local_kv) * HD]
    for h in range(local_q + local_kv):
        head = raw[:, h * HD : (h + 1) * HD]
        gain = qg_ref[...] if h < local_q else kg_ref[...]
        normed = head * lax.rsqrt(jnp.mean(head * head, axis=1, keepdims=True) + norm_eps) * gain
        turned = (normed * cosine + pltpu.roll(normed, HD // 2, 1) * sine).astype(bf16)
        if h < local_q:
            q_ref[:, h * HD : (h + 1) * HD] = turned
        else:
            k_ref[:, (h - local_q) * HD : (h - local_q + 1) * HD] = turned
    v_ref[...] = raw[:, (local_q + local_kv) * HD :].astype(bf16)


def project(x, w, q_gain, k_gain, cosine, sine, local_q, local_kv):
    rows, width = x.shape
    tile = 256
    cols = w.shape[1]
    full = lambda shape: pl.BlockSpec(shape, lambda i: (0,) * len(shape))
    row = lambda n: pl.BlockSpec((tile, n), lambda i: (i, 0))
    heads = local_q + local_kv
    return pl.pallas_call(
        functools.partial(project_kernel, local_q, local_kv),
        grid=(rows // tile,),
        in_specs=[row(width), full((width, cols)), full((1, HD)), full((1, HD)), row(HD), row(HD)],
        out_specs=[row(heads * HD), row(local_q * HD), row(local_kv * HD), row(local_kv * HD)],
        out_shape=[
            jax.ShapeDtypeStruct((rows, heads * HD), f32),
            jax.ShapeDtypeStruct((rows, local_q * HD), bf16),
            jax.ShapeDtypeStruct((rows, local_kv * HD), bf16),
            jax.ShapeDtypeStruct((rows, local_kv * HD), bf16),
        ],
        compiler_params=pltpu.CompilerParams(vmem_limit_bytes=40 * MIB),
        cost_estimate=pl.CostEstimate(flops=2 * rows * width * cols, bytes_accessed=rows * width * 2 + width * cols * 2 + rows * cols * 6, transcendentals=0),
        name="project",
    )(x, w, q_gain, k_gain, cosine, sine)


def attend_kernel(scale, q_ref, k_ref, vt_ref, o_ref):
    for b in range(q_ref.shape[0] // ATT_BLOCK):
        n = (b + 1) * ATT_BLOCK
        at = slice(b * ATT_BLOCK, n)
        weight = jnp.exp(dot(k_ref[:n, :], q_ref[at, :], NT) * scale)
        total = jnp.sum(weight, axis=0, keepdims=True)
        mixed = dot(vt_ref[:, :n], weight.astype(bf16)) * (1.0 / total)
        o_ref[at, :] = mixed.T.astype(bf16)


def attend(q, k, v_t, local_q, local_kv):
    rows = q.shape[0]
    repeat = local_q // local_kv
    return pl.pallas_call(
        functools.partial(attend_kernel, HD**-0.5),
        grid=(local_q,),
        in_specs=[
            pl.BlockSpec((rows, HD), lambda h: (0, h)),
            pl.BlockSpec((rows, HD), lambda h: (0, h // repeat)),
            pl.BlockSpec((HD, rows), lambda h: (h // repeat, 0)),
        ],
        out_specs=pl.BlockSpec((rows, HD), lambda h: (0, h)),
        out_shape=jax.ShapeDtypeStruct((rows, local_q * HD), bf16),
        compiler_params=pltpu.CompilerParams(vmem_limit_bytes=32 * MIB),
        cost_estimate=pl.CostEstimate(flops=local_q * rows * rows * HD * 3, bytes_accessed=rows * local_q * HD * 4, transcendentals=local_q * rows * rows),
        name="attend",
    )(q, k, v_t)


def unturn(grad, raw, gain, cosine, sine):
    grad = grad * cosine - pltpu.roll(grad, HD // 2, 1) * sine
    inv = lax.rsqrt(jnp.mean(raw * raw, axis=1, keepdims=True) + norm_eps)
    part = gain * grad
    back = inv * part - raw * (inv * inv * inv) * jnp.mean(raw * part, axis=1, keepdims=True)
    return back, jnp.sum(grad * raw * inv, axis=0, keepdims=True)


def attend_back_kernel(
    scale, repeat, q_ref, do_ref, raw_ref, k_ref, kt_ref, v_ref, rawk_ref, qg_ref, kg_ref, cos_ref, sin_ref,
    dq_ref, dk_ref, dv_ref, dqg_ref, dkg_ref, dqs, dks, dvs,
):
    h = pl.program_id(0)

    @pl.when(h == 0)
    def _():
        dqg_ref[...] = jnp.zeros_like(dqg_ref)
        dkg_ref[...] = jnp.zeros_like(dkg_ref)

    @pl.when(lax.rem(h, repeat) == 0)
    def _():
        dks[...] = jnp.zeros_like(dks)
        dvs[...] = jnp.zeros_like(dvs)

    for b in range(q_ref.shape[0] // ATT_BLOCK):
        n = (b + 1) * ATT_BLOCK
        at = slice(b * ATT_BLOCK, n)
        query, given = q_ref[at, :], do_ref[at, :]
        weight = jnp.exp(dot(k_ref[:n, :], query, NT) * scale)
        prob = weight * (1.0 / jnp.sum(weight, axis=0, keepdims=True))
        prob_grad = dot(v_ref[:n, :], given, NT)
        inner = jnp.sum(prob * prob_grad, axis=0, keepdims=True)
        score_grad = (prob * (prob_grad - inner)).astype(bf16)
        dks[:n, :] += dot(score_grad, query)
        dvs[:n, :] += dot(prob.astype(bf16), given)
        dqs[at, :] = dot(kt_ref[:, :n], score_grad).T * scale
    back, gain_part = unturn(dqs[...], raw_ref[...], qg_ref[...], cos_ref[...], sin_ref[...])
    dq_ref[...] = back.astype(bf16)
    dqg_ref[...] += gain_part

    @pl.when(lax.rem(h, repeat) == repeat - 1)
    def _():
        back_k, gain_k = unturn(dks[...] * scale, rawk_ref[...], kg_ref[...], cos_ref[...], sin_ref[...])
        dk_ref[...] = back_k.astype(bf16)
        dv_ref[...] = dvs[...].astype(bf16)
        dkg_ref[...] += gain_k


def attend_back(q, given, raw, k, k_t, v, q_gain, k_gain, cosine, sine, local_q, local_kv):
    rows = q.shape[0]
    repeat = local_q // local_kv
    head = pl.BlockSpec((rows, HD), lambda h: (0, h))
    shared = pl.BlockSpec((rows, HD), lambda h: (0, h // repeat))
    whole = pl.BlockSpec((rows, HD), lambda h: (0, 0))
    gain = pl.BlockSpec((1, HD), lambda h: (0, 0))
    return pl.pallas_call(
        functools.partial(attend_back_kernel, HD**-0.5, repeat),
        grid=(local_q,),
        in_specs=[
            head, head, head, shared, pl.BlockSpec((HD, rows), lambda h: (h // repeat, 0)), shared,
            pl.BlockSpec((rows, HD), lambda h: (0, local_q + h // repeat)), gain, gain, whole, whole,
        ],
        out_specs=[head, shared, shared, gain, gain],
        out_shape=[
            jax.ShapeDtypeStruct((rows, local_q * HD), bf16),
            jax.ShapeDtypeStruct((rows, local_kv * HD), bf16),
            jax.ShapeDtypeStruct((rows, local_kv * HD), bf16),
            jax.ShapeDtypeStruct((1, HD), f32),
            jax.ShapeDtypeStruct((1, HD), f32),
        ],
        scratch_shapes=[pltpu.VMEM((rows, HD), f32)] * 3,
        compiler_params=pltpu.CompilerParams(vmem_limit_bytes=40 * MIB),
        cost_estimate=pl.CostEstimate(flops=local_q * rows * rows * HD * 7, bytes_accessed=rows * local_q * HD * 10, transcendentals=local_q * rows * rows),
        name="attend_back",
    )(q, given, raw, k, k_t, v, raw, q_gain, k_gain, cosine, sine)


def experts_kernel(
    held, order, x_ref, pre_ref, gate_ref, spread_ref, wg_ref, wu_ref, *refs
):
    hw_ref, gb_ref, ub_ref, score_ref, *back_refs = refs[held:]
    x = x_ref[...]
    gate_pre = dot(x, wg_ref[...])
    sigma = 1.0 / (1.0 + jnp.exp(-gate_pre))
    active = gate_pre * sigma
    up_pre = dot(x, wu_ref[...])
    pre = pre_ref[...].reshape(gate_pre.shape)
    hidden = active * up_pre
    score_ref[...] = dot(spread_ref[...], (hidden * pre).astype(bf16), NT).reshape(score_ref.shape)
    weight = dot(gate_ref[...], spread_ref[...])
    hw_ref[...] = (hidden * weight).astype(bf16).reshape(hw_ref.shape)
    hidden_grad = pre * weight
    up_back = (hidden_grad * active).astype(bf16)
    gate_back = (hidden_grad * up_pre * sigma * (1.0 + gate_pre * (1.0 - sigma))).astype(bf16)
    gb_ref[...] = gate_back
    ub_ref[...] = up_back
    back = (dot(gate_back, wg_ref[...], NT) + dot(up_back, wu_ref[...], NT)).astype(bf16)
    if len(back_refs) == 1:
        back_refs[0][...] = back
        return
    first = pl.program_id(0) < pl.num_programs(0) // 2

    @pl.when(first)
    def _():
        back_refs[0][...] = back

    @pl.when(jnp.logical_not(first))
    def _():
        back_refs[1][...] = back


def row_block(array, c):
    _, members, _, piece, columns = array.shape
    return pl.BlockSpec((1, members, 1, piece, columns), lambda j, order: (order[j], 0, c, 0, 0))


def experts(order, c, x, pre, gates, spread, gate_w, up_w, held=(), halves=False):
    rows, width = x.shape
    tile = rows // pre.shape[0]
    hidden = gate_w.shape[1]
    lanes = spread.shape[0]
    steps = order.shape[0]
    half = steps // 2
    spots = [lambda j, order: (j, 0)]
    if halves:
        spots = [lambda j, order: (jnp.minimum(j, half - 1), 0), lambda j, order: (jnp.maximum(j - half, 0), 0)]
    at = lambda n: pl.BlockSpec((tile, n), lambda j, order: (order[j], 0))
    full = lambda shape: pl.BlockSpec(shape, lambda j, order: (0, 0), pipeline_mode=pl.Buffered(1))
    return pl.pallas_call(
        functools.partial(experts_kernel, len(held)),
        grid_spec=pltpu.PrefetchScalarGridSpec(
            num_scalar_prefetch=1,
            grid=(steps,),
            in_specs=[
                at(width), row_block(pre, c), at(lanes), full((lanes, hidden)), full((width, hidden)), full((width, hidden)),
                *[pl.BlockSpec(memory_space=pl.ANY)] * len(held),
            ],
            out_specs=[
                row_block(pre, c), at(hidden), at(hidden), pl.BlockSpec((1, lanes, tile), lambda j, order: (order[j], 0, 0)),
                *[pl.BlockSpec((tile, width), spot) for spot in spots],
            ],
        ),
        out_shape=[
            jax.ShapeDtypeStruct(pre.shape, bf16),
            jax.ShapeDtypeStruct((rows, hidden), bf16),
            jax.ShapeDtypeStruct((rows, hidden), bf16),
            jax.ShapeDtypeStruct((rows // tile, lanes, tile), f32),
            *[jax.ShapeDtypeStruct((steps * tile // len(spots), width), bf16) for _ in spots],
        ],
        input_output_aliases={7 + i: output for i, (output, _) in enumerate(held)},
        compiler_params=pltpu.CompilerParams(vmem_limit_bytes=58 * MIB),
        cost_estimate=pl.CostEstimate(flops=8 * steps * tile * width * hidden, bytes_accessed=steps * tile * (width * 4 + hidden * 10), transcendentals=steps * tile * hidden),
        name="experts",
    )(order, x, pre, gates, spread, gate_w, up_w, *[array for _, array in held])


def outputs_kernel(order, h_ref, w_ref, out_ref):
    hidden = h_ref[...].reshape(out_ref.shape[0], w_ref.shape[0])
    out_ref[...] = dot(hidden, w_ref[...]).astype(bf16)


def outputs(order, c, hidden_wt, down_w, flops=1):
    _, members, _, piece, hidden = hidden_wt.shape
    steps = order.shape[0]
    tile = members * piece
    width = down_w.shape[1]
    return pl.pallas_call(
        outputs_kernel,
        grid_spec=pltpu.PrefetchScalarGridSpec(
            num_scalar_prefetch=1,
            grid=(steps,),
            in_specs=[
                row_block(hidden_wt, c),
                pl.BlockSpec((hidden, width), lambda j, order: (0, 0), pipeline_mode=pl.Buffered(1)),
            ],
            out_specs=pl.BlockSpec((tile, width), lambda j, order: (j, 0)),
        ),
        out_shape=jax.ShapeDtypeStruct((steps * tile, width), bf16),
        compiler_params=pltpu.CompilerParams(vmem_limit_bytes=32 * MIB),
        cost_estimate=pl.CostEstimate(flops=flops, bytes_accessed=1, transcendentals=0),
        name="outputs",
    )(order, hidden_wt, down_w)


def rows_product_kernel(x_ref, g_ref, out_ref):
    @pl.when(pl.program_id(0) == 0)
    def _():
        out_ref[...] = jnp.zeros_like(out_ref)

    out_ref[...] += dot(x_ref[...], g_ref[...], TN)


def rows_product(x, g):
    rows, width = x.shape
    columns = g.shape[1]
    tile = rows // 4
    return pl.pallas_call(
        rows_product_kernel,
        grid=(4,),
        in_specs=[pl.BlockSpec((tile, width), lambda j: (j, 0)), pl.BlockSpec((tile, columns), lambda j: (j, 0))],
        out_specs=pl.BlockSpec((width, columns), lambda j: (0, 0)),
        out_shape=jax.ShapeDtypeStruct((width, columns), f32),
        compiler_params=pltpu.CompilerParams(vmem_limit_bytes=52 * MIB),
        cost_estimate=pl.CostEstimate(flops=1, bytes_accessed=1, transcendentals=0),
        name="rows_product",
    )(x, g)


TOPK = 8


def row_norm(values, gain):
    return values * lax.rsqrt(jnp.mean(values * values, axis=-1, keepdims=True) + norm_eps) * gain


def after(value, *others):
    return lax.optimization_barrier((value, *others))[0]


def hop(block, bit, axis):
    size = lax.axis_size(axis)
    return lax.ppermute(block, axis, [(i, i ^ bit) for i in range(size)])


def bits_of(size):
    return [1 << k for k in range(size.bit_length() - 1)]


def step_order(bits):
    order = [0]
    for bit in reversed(bits):
        order = [r | bit for r in order] + order
    return order


class Exchange:
    def __init__(self, far, near, bits):
        self.moved = [hop(far, bits[0], "expert")]
        self.near, self.rest = near, bits[1:]
        self.left = [list(range(len(self.rest))) for _ in range(2)]
        self.sides = None

    def wait(self, behind):
        if self.sides is None:
            moved = after(self.moved, *behind) if behind else self.moved
            rows, width = self.near.shape[0] >> len(self.rest), self.near.shape[1]
            near, moved = self.near.reshape(-1, rows, width), moved[0].reshape(-1, rows, width)
            spots = itertools.product(range(2), repeat=len(self.rest))
            index = {spot: i for i, spot in enumerate(spots)}
            self.sides = []
            for part in (slice(0, rows // 2), slice(rows // 2, None)):
                self.sides.append({spot: [near[i, part], moved[i, part]] for spot, i in index.items()})
        else:
            for number, (side, got) in enumerate(zip(self.sides, self.got)):
                got = after(got, *behind) if behind else got
                self.sides[number] = {spot: [*parts, got[i]] for i, (spot, parts) in enumerate(side.items())}

    def send(self, *behind):
        self.wait(behind)
        sent, self.got = [], []
        add = lambda parts: sum(p.astype(f32) for p in parts).astype(bf16)
        for number, side in enumerate(self.sides):
            at = len(self.left[number]) - 1 if number else 0
            bit = self.rest[self.left[number].pop(at)]
            spots = sorted({spot[:at] + spot[at + 1 :] for spot in side})
            block = jnp.stack([add(side[spot[:at] + (0,) + spot[at:]]) for spot in spots])
            self.got.append(hop(block, bit, "expert"))
            sent.append(block)
            self.sides[number] = {spot: side[spot[:at] + (1,) + spot[at:]] for spot in spots}
        return sent

    def total(self, *behind):
        while any(self.left):
            self.send()
        self.wait(behind)
        parts = [sum(p.astype(f32) for p in side[()]).astype(bf16) for side in self.sides]
        return jnp.concatenate(parts, axis=0)


def neighbours():
    size = lax.axis_size("tensor")
    up = lambda v: lax.ppermute(v, "tensor", [(i, (i + 1) % size) for i in range(size)])
    down = lambda v: lax.ppermute(v, "tensor", [(i, (i - 1) % size) for i in range(size)])
    return up, down


def gather_line(block, behind=()):
    size, me = lax.axis_size("tensor"), lax.axis_index("tensor")
    if size != 4:
        return lax.all_gather(block, "tensor", axis=0, tiled=True)
    rows = block.shape[0]
    cut = rows // 2
    up, down = neighbours()
    low, high = up(block), down(block)
    if behind:
        low, high = after((low, high), *behind)
    far_low, far_high = up(low[:cut]), down(high[cut:])
    whole = after(jnp.zeros((rows * size, block.shape[1]), block.dtype), low)
    for part, member, shift in ((block, 0, 0), (low, 3, 0), (high, 1, 0), (far_low, 2, 0), (far_high, 2, cut)):
        at = lax.rem(me + member, size) * rows + shift
        whole = lax.dynamic_update_slice(whole, part, (at, 0))
    return whole


class Line:
    def __init__(self, part):
        self.size, self.me = lax.axis_size("tensor"), lax.axis_index("tensor")
        self.part, self.rows = part, part.shape[0] // self.size
        self.got = None

    def of(self, member, start, end):
        at = lax.rem(self.me + member, self.size) * self.rows
        return lax.dynamic_slice_in_dim(self.part, at + start, end - start, 0)

    def send(self, *behind):
        cut, rows = self.rows // 2, self.rows
        if self.size != 4:
            return []
        if behind:
            self.got = after(self.got, *behind)
        if self.got is None:
            low, high = self.of(2, cut, rows), self.of(2, 0, cut)
        else:
            from_low, from_high = (part.astype(f32) for part in self.got)
            low = jnp.concatenate([self.of(1, 0, cut), (self.of(1, cut, rows).astype(f32) + from_low).astype(bf16)])
            high = jnp.concatenate([(self.of(3, 0, cut).astype(f32) + from_high).astype(bf16), self.of(3, cut, rows)])
        up, down = neighbours()
        self.got = up(low), down(high)
        return [low, high]

    def total(self, *behind):
        if self.size != 4:
            return lax.psum_scatter(self.part, "tensor", scatter_dimension=0, tiled=True).astype(f32)
        low, high = after(self.got, *behind) if behind else self.got
        return self.of(0, 0, self.rows).astype(f32) + low.astype(f32) + high.astype(f32)


def local(
    hidden_in,
    attn_gain,
    query_gain,
    key_gain,
    w_qkv,
    w_out,
    moe_gain,
    w_router,
    w_gate,
    w_up,
    w_down,
    routes,
    pair_rank,
    out_grad,
):
    tok_dev, width = hidden_in.shape
    n_tensor = lax.axis_size("tensor")
    n_expert = lax.axis_size("expert")
    member = lax.axis_index("tensor")
    place = lax.axis_index("expert")
    group = tok_dev * n_tensor
    local_experts = w_gate.shape[0]
    quarter = w_gate.shape[2]
    n_experts = local_experts * n_expert
    hidden_loc = local_experts * quarter
    capacity = 9 * group * TOPK // (8 * n_experts)
    local_q = w_out.shape[0] // HD
    local_kv = (w_qkv.shape[1] // HD - local_q) // 2
    both = ("expert", "tensor")
    bits = bits_of(n_expert)
    chunks = 2 * max(n_expert // 8, 1)
    piece = tok_dev // chunks
    first = 16 * (tok_dev * 9 // 256) if chunks == 2 else piece
    lanes = 8 * (-(-local_experts // 8))

    gate_w = w_gate.transpose(1, 0, 2).reshape(width, hidden_loc)
    up_w = w_up.transpose(1, 0, 2).reshape(width, hidden_loc)
    down_w = w_down.reshape(hidden_loc, width)
    spread = (jnp.arange(hidden_loc)[None, :] // quarter == jnp.arange(lanes)[:, None]).astype(bf16)

    hidden_f = hidden_in.astype(f32)
    attn_normed, attn_pull = jax.vjp(row_norm, hidden_f, attn_gain.astype(f32))
    gathered = gather_line(attn_normed.astype(bf16))
    given = after(out_grad, gathered)

    cosine, sine = rope_tables(group)
    q_gain, k_gain = query_gain.astype(f32)[None, :], key_gain.astype(f32)[None, :]
    if chunks == 2:
        gathered = after(gathered, gate_w, up_w)
    raw, queries, keys, values = project(gathered, w_qkv, q_gain, k_gain, cosine, sine, local_q, local_kv)
    mixed_all = attend(queries, keys, values.T, local_q, local_kv)
    attn = mixed_all
    if chunks == 2:
        line_1 = gather_line(given[first:], (queries,))
        line_0 = gather_line(after(given[:first], queries), (mixed_all,))
        grad_line = [line_0, line_1]
        all_1 = lax.all_gather(line_1, "expert", axis=0, tiled=True)
        all_0 = lax.all_gather(line_0, "expert", axis=0, tiled=True)
        grad_all = [all_0, all_1]
        pre = [dot(part, down_w, NT).reshape(n_expert, n_tensor, 1, -1, hidden_loc) for part in grad_all]
        attn = after(attn, *grad_line)
    attn = Line(dot(attn, w_out).astype(bf16))
    attn.send()
    attn.send()
    attn = attn.total()
    middle = hidden_f + attn
    moe_normed, moe_pull = jax.vjp(row_norm, middle, moe_gain.astype(f32))
    moe_in = moe_normed.astype(bf16)

    expert_ids = jnp.arange(n_experts, dtype=jnp.int32)
    hits = routes.T[None, :, :] == expert_ids[:, None, None]
    ranks = jnp.where(hits, pair_rank[0].reshape(group, TOPK).T[None, :, :] + 1, 0).sum(axis=1)
    ranks = jnp.where(ranks == 0, group * TOPK + 1, ranks)
    own_ranks = lax.dynamic_slice_in_dim(ranks, member * tok_dev, tok_dev, 1)
    before = (ranks[:, :, None] < own_ranks[:, None, :]).astype(f32).sum(axis=1)
    routed = own_ranks <= group * TOPK
    keep = routed & (before < capacity)

    logits = dot(w_router, moe_in, ((0,), (1,)))
    gates = jax.nn.softmax(jnp.where(routed, logits, -jnp.inf), axis=0)
    sent_gates = jnp.where(keep, gates, 0.0).astype(bf16).astype(f32)
    gates_in = jnp.broadcast_to(
        sent_gates.reshape(n_expert, 1, local_experts, tok_dev), (n_expert, n_tensor, local_experts, tok_dev)
    )
    gates_in = lax.all_to_all(gates_in.reshape(-1, local_experts, tok_dev), both, 0, 0, tiled=True)
    gates_in = gates_in.reshape(n_expert, n_tensor, local_experts, tok_dev).transpose(0, 1, 3, 2)
    gates_in = jnp.pad(gates_in, ((0, 0), (0, 0), (0, 0), (0, lanes - local_experts))).astype(bf16)

    def gates_of(start, count):
        return lax.dynamic_slice_in_dim(gates_in, start, count, 2).reshape(-1, lanes)

    order = place ^ jnp.array(step_order(bits), jnp.int32)

    def own_rows(part):
        return lax.psum_scatter(part, "tensor", scatter_dimension=0, tiled=True)

    def to_tokens(scores):
        scores = [s[:, :local_experts].reshape(n_expert, local_experts, n_tensor, -1) for s in scores]
        scores = jnp.concatenate(scores, axis=3).transpose(0, 2, 1, 3)
        scores = lax.all_to_all(scores.reshape(-1, local_experts, tok_dev), both, 0, 0, tiled=True)
        scores = scores.reshape(n_expert, n_tensor, local_experts, tok_dev).sum(axis=1)
        return jnp.where(keep, scores.reshape(n_experts, tok_dev), 0.0)

    if chunks == 2:
        moe_line = [gather_line(moe_in[:first], (pre[1],)), gather_line(moe_in[first:])]
        gates_0, gates_1 = gates_of(0, first), gates_of(first, tok_dev - first)
        moe_line[0] = after(moe_line[0], grad_all[0])
        moe_all = [lax.all_gather(part, "expert", axis=0, tiled=True) for part in moe_line]
        front, rear = order[: n_expert // 2], order[n_expert // 2 :]
        fixed = (spread, gate_w, up_w)
        x_0 = moe_all[0]
        *kept_0, back_0 = experts(jnp.arange(n_expert, dtype=jnp.int32), 0, x_0, pre[0], gates_0, *fixed)
        back_0 = lax.psum_scatter(back_0, "expert", scatter_dimension=0, tiled=True)
        far_0 = outputs(front, 0, kept_0[0], down_w)
        x_1 = after(moe_all[1], far_0)
        *kept_1, far, near = experts(order, 0, x_1, pre[1], gates_1, *fixed, halves=True)
        back_1 = Exchange(far, near, bits)
        scores = to_tokens([kept_0[3], kept_1[3]])
        far_1, near_1 = (outputs(part, 0, kept_1[0], down_w) for part in (front, rear))
        sent = back_1.send(far_1, near_1, scores)
        x_0, hidden_0 = after((moe_all[0], kept_0[0]), *sent)
        gate_grad = rows_product(x_0, kept_0[1])
        back_0 = after(back_0, gate_grad)
        back_own = [own_rows(back_0)]
        sent = back_1.send(gate_grad)
        near_flops = 2 * 2 * n_expert // 2 * n_tensor * first * width * hidden_loc
        near_0 = outputs(rear, 0, after(hidden_0, *sent), down_w, near_flops)
        out_0, out_1 = Exchange(far_0, near_0, bits), Exchange(far_1, near_1, bits)
        sent = out_1.send(*sent)
        back_1 = back_1.total(*sent, near_0, back_own[0])
        back_own.append(own_rows(back_1))
        x_1, g_0 = after((moe_all[1], grad_all[0]), back_1)
        gate_grad = gate_grad + dot(x_1, kept_1[1], TN)
        down_grad = dot(kept_0[0].reshape(-1, hidden_loc), g_0, TN)
        sent = out_1.send(gate_grad, down_grad)
        back_own = after(back_own, *sent)
    else:
        def one_chunk(sums, c):
            x_c = lax.all_gather(lax.dynamic_slice_in_dim(moe_in, c * piece, piece, 0), both, axis=0, tiled=True)
            g_c = lax.all_gather(lax.dynamic_slice_in_dim(given, c * piece, piece, 0), both, axis=0, tiled=True)
            gates_c = gates_of(c * piece, piece)
            pre = dot(g_c, down_w, NT).reshape(n_expert, n_tensor, 1, piece, hidden_loc)
            given_c = (0, x_c, pre, gates_c, spread, gate_w, up_w)
            *kept, far = experts(order[: n_expert // 2], *given_c)
            *kept, near = experts(order[n_expert // 2 :], *given_c, list(enumerate(kept)))
            hw, gate_back, up_back, score = kept
            parts = (dot(hw.reshape(-1, hidden_loc), g_c, TN), dot(x_c, gate_back, TN), dot(x_c, up_back, TN))
            sums = tuple(a + b for a, b in zip(sums, parts))
            back = own_rows(Exchange(far, near, bits).total())
            out = [outputs(part, 0, hw, down_w) for part in (order[: n_expert // 2], order[n_expert // 2 :])]
            out = own_rows(Exchange(*out, bits).total())
            return sums, (back, score, out)

        zeros = (
            jnp.zeros((hidden_loc, width), f32),
            jnp.zeros((width, hidden_loc), f32),
            jnp.zeros((width, hidden_loc), f32),
        )
        grads, (back_own, scores, out_own) = lax.scan(one_chunk, zeros, jnp.arange(chunks))
        scores = to_tokens(scores)
        moe_out = jnp.concatenate(list(out_own), axis=0)
    moe_back = jnp.concatenate(list(back_own), axis=0).astype(f32)

    inner_gate = jnp.sum(gates * scores, axis=0, keepdims=True)
    logit_grad = (gates * (scores - inner_gate)).astype(bf16)
    router_grad = dot(logit_grad, moe_in)
    moe_in_grad = moe_back + dot(logit_grad, w_router, ((0,), (1,)))
    middle_part, moe_gain_grad = moe_pull(moe_in_grad)
    middle_grad = out_grad.astype(f32) + middle_part

    middle_all = lax.all_gather(middle_grad.astype(bf16), "tensor", axis=0, tiled=True)
    if chunks == 2:
        sent = out_0.send(middle_grad)
        x_0, x_1, g_1 = after((moe_all[0], moe_all[1], grad_all[1]), *sent)
        up_grad = dot(x_0, kept_0[2], TN) + dot(x_1, kept_1[2], TN)
        out_1 = out_1.total(up_grad)
        down_grad = down_grad + dot(kept_1[0].reshape(-1, hidden_loc), after(g_1, out_1), TN)
        sent = out_0.send(down_grad)
        middle_all = after(middle_all, *sent)
    mixed_grad = dot(middle_all, w_out, NT).astype(bf16)
    if chunks == 2:
        out_0 = out_0.total(mixed_grad)
        mixed_grad = after(mixed_grad, out_0)
    dq, dk, dv, query_gain_grad, key_gain_grad = attend_back(
        queries, mixed_grad, raw, keys, keys.T, values, q_gain, k_gain, cosine, sine, local_q, local_kv
    )
    qkv_grad = jnp.concatenate([dq, dk, dv], axis=1)
    if chunks == 2:
        out_own = [own_rows(part) for part in (out_1, out_0)][::-1]
        qkv_grad = after(qkv_grad, out_own[1])
        moe_out = jnp.concatenate(out_own, axis=0)
    normed_part = dot(qkv_grad, w_qkv, NT)
    normed_low = normed_part.astype(bf16)
    normed_line = Line(normed_low)
    sent = normed_line.send()
    out_weight_grad = dot(middle_all, after(mixed_all, *sent), TN).astype(bf16)
    grad_out = lax.psum_scatter(out_weight_grad, "expert", scatter_dimension=0, tiled=True)
    weight_grad = dot(after(gathered, *sent), qkv_grad, TN).astype(bf16)
    attn_gain_grad = jnp.sum(normed_part * gathered.astype(f32), axis=0) / attn_gain.astype(f32)
    gain_rows = [attn_gain_grad[None, :], moe_gain_grad[None, :]]
    gain_rows += [jnp.pad(part, ((0, 0), (0, width - HD))) for part in (query_gain_grad, key_gain_grad)]
    small = jnp.concatenate([router_grad, *gain_rows], axis=0)
    small = jnp.pad(small, ((0, -small.shape[0] % n_expert), (0, 0))).reshape(n_expert, -1, width)
    small = lax.all_to_all(small, "expert", 0, 0, tiled=True).sum(axis=0)
    blocks = weight_grad.reshape(n_expert, -1, weight_grad.shape[1])
    blocks = [lax.dynamic_index_in_dim(blocks, place ^ r, 0, keepdims=False) for r in step_order(bits)]
    far, near = (
        jnp.concatenate(part, axis=0) for part in (blocks[: n_expert // 2], blocks[n_expert // 2 :])
    )
    grad_qkv = Exchange(far, near, bits)
    if chunks == 2:
        grads = [down_grad, gate_grad, up_grad]
    grad_down = grads[0].reshape(local_experts, quarter, width)
    grad_gate, grad_up = (
        part.reshape(width, local_experts, quarter).transpose(1, 0, 2) for part in grads[1:]
    )
    sent = normed_line.send(far, near, grad_gate, grad_up)
    sent = sum([grad_qkv.send(*sent) for _ in bits[1:]], [])
    small = after(small, *sent) if sent else small
    for bit in bits_of(n_tensor):
        small = small + hop(small, bit, "tensor")
    small = lax.all_to_all(jnp.broadcast_to(small[None], (n_expert, *small.shape)), "expert", 0, 0, tiled=True)
    small = small.reshape(-1, width)
    grad_qkv = grad_qkv.total().astype(f32)
    normed_grad = normed_line.total(*sent)
    layer_out = (middle + moe_out.astype(f32)).astype(bf16)
    hidden_part, _ = attn_pull(normed_grad)
    input_grad = middle_grad + hidden_part
    return (
        layer_out,
        input_grad,
        small[n_experts],
        small[n_experts + 2, :HD],
        small[n_experts + 3, :HD],
        grad_qkv,
        grad_out.astype(f32).T,
        small[n_experts + 1],
        small[:n_experts].T,
        grad_gate,
        grad_up,
        grad_down,
    )


def solution(mesh):
    in_specs = (
        P(("expert", "tensor"), None),
        P(),
        P(),
        P(),
        P(None, "tensor"),
        P("tensor", None),
        P(),
        P(),
        P("expert", None, "tensor"),
        P("expert", None, "tensor"),
        P("expert", "tensor", None),
        P("expert", None),
        P("expert", None),
        P(("expert", "tensor"), None),
    )
    out_specs = (
        P(("expert", "tensor"), None),
        P(("expert", "tensor"), None),
        P(),
        P(),
        P(),
        P("expert", "tensor"),
        P("tensor", "expert"),
        P(),
        P(),
        P("expert", None, "tensor"),
        P("expert", None, "tensor"),
        P("expert", "tensor", None),
    )
    return jax.shard_map(local, mesh=mesh, in_specs=in_specs, out_specs=out_specs, check_vma=False)
```
